256 devices in a mesh: beam: 32 (over z, y), slab: 8 (over x, core).
Axes of the slice: x: 4, y: 4, z: 8, core: 2. Of those that a mesh axis runs over, the one named last changes fastest.
Arguments:
- pot_first: bfloat16 [4096, 4096], P('beam'), may hold values from -3.140625 to 3.140625
- pot_second: bfloat16 [4096, 4096], P('beam'), may hold values from -3.140625 to 3.140625
- beam_index: int32 [8, 2], replicated, may hold values from -3 to 3
- aberration: float32 [8], replicated, may hold values from -3.140625 to 3.140625
- tile_table: int32 [256, 4], replicated, may hold values from 0 to 4095, as said below
- tile_count: int32 [256], replicated, may hold values from 1 to 4, as said below
Outputs:
- detector_sums: float32 [256, 4, 3, 16], P(('beam', 'slab'))
The draws below stay inside these ranges and needn't reach their ends.
Inputs may be any that keep to these rules, and one draw needn't show every extreme that they name: `tile_table`: group the blocks by the beam index of their device, block // 8; among the 32 slots of one group, active or not, exactly 1 name a tile of row band b, for every band b = ty // 2. The first tile_count[block] slots of a block are active; some block has all 4 active.
All inputs are finite; a program needn't handle non-finite values.
Results may differ from the reference program's by a relative error of at most 0.012.
The reference program's roundings to bfloat16 on the way count: a program that leaves them out, or rounds other values in their place, can miss the bound.
Values may be sent and summed in bfloat16 or wider, within the bound.
A program may use at most 128 MiB of HBM per device.

```python
import math
import jax
import jax.numpy as jnp
from jax import lax

A = 64
N = 4096
F = 64
QMAX = 3
G = 3
NDET = 16
TMAX = 4
BLK_DEV = 1
BEAMS = 8
BLOCKS = 256
N_BEAM = 32
N_SLAB = 8


def draw_tile_table(key, part):
    key = jax.random.fold_in(key, 11)
    across = N // A
    band_tiles = N // N_BEAM // A
    length = N_SLAB * BLK_DEV * TMAX
    capacity = length // N_BEAM
    key_list = jax.random.split(key, 3)
    orders = jax.vmap(lambda subkey: jax.random.permutation(subkey, length))(jax.random.split(key_list[0], N_BEAM))
    band_ids = orders // capacity
    row_in = jax.random.randint(key_list[1], (N_BEAM, length), 0, band_tiles)
    col_ids = jax.random.randint(key_list[2], (N_BEAM, length), 0, across)
    tile_ids = (band_ids * band_tiles + row_in) * across + col_ids
    return tile_ids.reshape(N_BEAM * N_SLAB * BLK_DEV, TMAX).astype(jnp.int32)


def draw_tile_count(key, part):
    key = jax.random.fold_in(key, 23)
    first_key, second_key = jax.random.split(key)
    counts = jax.random.randint(first_key, (BLOCKS,), 1, TMAX + 1)
    full_block = jax.random.randint(second_key, (), 0, BLOCKS)
    return counts.at[full_block].set(TMAX).astype(jnp.int32)


def touch_ends(drawn, key, least, top_value):
    spot = [jax.random.randint(jax.random.fold_in(key, axis), (), 0, length) for axis, length in enumerate(drawn.shape)]
    main_axis = drawn.shape.index(max(drawn.shape))
    next_to = spot[:main_axis] + [(spot[main_axis] + 1) % drawn.shape[main_axis]] + spot[main_axis + 1:]
    return drawn.at[tuple(spot)].set(least).at[tuple(next_to)].set(top_value)


def setup_inputs(seed: int = 0) -> dict:
    seeds = jax.random.split(jax.random.key(seed), 7)
    return {
        "pot_first": jnp.clip(jax.random.uniform(seeds[0], (N, N), jnp.float32, -3.140625, 3.140625), -3.140625, 3.140625).astype(jnp.bfloat16),
        "pot_second": jnp.clip(jax.random.uniform(seeds[1], (N, N), jnp.float32, -3.140625, 3.140625), -3.140625, 3.140625).astype(jnp.bfloat16),
        "beam_index": touch_ends(jax.random.randint(seeds[2], (BEAMS, 2), -QMAX, QMAX + 1), jax.random.fold_in(seeds[2], 1), -QMAX, QMAX).astype(jnp.int32),
        "aberration": jnp.clip(jax.random.uniform(seeds[3], (BEAMS,), jnp.float32, -3.140625, 3.140625), -3.140625, 3.140625),
        "tile_table": draw_tile_table(jax.random.fold_in(seeds[6], 71), 0),
        "tile_count": draw_tile_count(jax.random.fold_in(seeds[6], 71), 0),
    }


def rounded(values):
    return lax.optimization_barrier(values.astype(jnp.bfloat16)).astype(jnp.float32)


def radix_pair(factor):
    digits = jnp.arange(A, dtype=jnp.int32)
    product = (digits[:, None] * digits[None, :]) % A
    angles = (2.0 * math.pi / A) * product.astype(jnp.float32)
    cosine = rounded(jnp.cos(angles)) * factor
    sine_tab = rounded(jnp.sin(angles)) * factor
    return cosine, sine_tab


def mix_lines(real_part, imag_part, cosine, sine_tab, orient, pattern):
    highest = lax.Precision.HIGHEST
    out_real = jnp.einsum(pattern, real_part, cosine, precision=highest) + orient * jnp.einsum(pattern, imag_part, sine_tab, precision=highest)
    out_imag = jnp.einsum(pattern, imag_part, cosine, precision=highest) - orient * jnp.einsum(pattern, real_part, sine_tab, precision=highest)
    return out_real, out_imag


def twist_lines(real_part, imag_part, orient):
    digits = jnp.arange(A, dtype=jnp.int32)
    product = (digits[:, None] * digits[None, :]) % N
    angles = (2.0 * math.pi / N) * product.astype(jnp.float32)
    cosine = jnp.cos(angles)
    turned = orient * jnp.sin(angles)
    return real_part * cosine + imag_part * turned, imag_part * cosine - real_part * turned


def forward_line(real_part, imag_part):
    full_shape = real_part.shape
    leading = full_shape[:-1]
    cosine, sine_tab = radix_pair(1.0 / A)
    real_part = rounded(real_part).reshape(leading + (A, A))
    imag_part = rounded(imag_part).reshape(leading + (A, A))
    real_part, imag_part = mix_lines(real_part, imag_part, cosine, sine_tab, 1.0, "...nm,nk->...km")
    real_part, imag_part = twist_lines(real_part, imag_part, 1.0)
    real_part, imag_part = rounded(real_part), rounded(imag_part)
    real_part, imag_part = mix_lines(real_part, imag_part, cosine, sine_tab, 1.0, "...km,mj->...kj")
    return jnp.swapaxes(real_part, -1, -2).reshape(full_shape), jnp.swapaxes(imag_part, -1, -2).reshape(full_shape)


def inverse_line(real_part, imag_part):
    full_shape = real_part.shape
    leading = full_shape[:-1]
    cosine, sine_tab = radix_pair(1.0)
    real_part = rounded(real_part).reshape(leading + (A, A))
    imag_part = rounded(imag_part).reshape(leading + (A, A))
    real_part, imag_part = mix_lines(real_part, imag_part, cosine, sine_tab, -1.0, "...jk,jb->...kb")
    real_part, imag_part = twist_lines(real_part, imag_part, -1.0)
    real_part, imag_part = rounded(real_part), rounded(imag_part)
    real_part, imag_part = mix_lines(real_part, imag_part, cosine, sine_tab, -1.0, "...kb,ka->...ab")
    return real_part.reshape(full_shape), imag_part.reshape(full_shape)


def exit_wave(pot_first, pot_second, beam_row):
    places = jnp.arange(N, dtype=jnp.int32)
    wave_y = jnp.remainder(F * beam_row[0], N)
    wave_x = jnp.remainder(F * beam_row[1], N)
    windings = (wave_y * places[:, None] + wave_x * places[None, :]) % N
    angles = (2.0 * math.pi / N) * windings.astype(jnp.float32)
    plane_cos, plane_sin = jnp.cos(angles), jnp.sin(angles)
    potential = pot_first.astype(jnp.float32)
    trans_cos, trans_sin = jnp.cos(potential), jnp.sin(potential)
    real_part = plane_cos * trans_cos - plane_sin * trans_sin
    imag_part = plane_cos * trans_sin + plane_sin * trans_cos
    real_part, imag_part = forward_line(real_part, imag_part)
    real_part, imag_part = forward_line(real_part.T, imag_part.T)
    signed = jnp.where(places < N // 2, places, places - N)
    radius = signed[:, None] ** 2 + signed[None, :] ** 2
    phases = (-math.pi / N) * (radius % (2 * N)).astype(jnp.float32)
    inside = radius <= (N // 3) ** 2
    prop_cos = jnp.where(inside, jnp.cos(phases), 0.0)
    prop_sin = jnp.where(inside, jnp.sin(phases), 0.0)
    real_part, imag_part = real_part * prop_cos - imag_part * prop_sin, real_part * prop_sin + imag_part * prop_cos
    real_part, imag_part = inverse_line(real_part, imag_part)
    real_part, imag_part = inverse_line(real_part.T, imag_part.T)
    potential = pot_second.astype(jnp.float32)
    trans_cos, trans_sin = jnp.cos(potential), jnp.sin(potential)
    return real_part * trans_cos - imag_part * trans_sin, real_part * trans_sin + imag_part * trans_cos


def coefficients(tile_ids, beam_rows, shifts):
    across = N // A
    offsets = jnp.arange(G, dtype=jnp.int32)
    spot_y = (tile_ids // across)[:, None] * A + A // 2 + offsets[None, :]
    spot_x = (tile_ids % across)[:, None] * A + A // 2 + 2 * offsets[None, :]
    wave_y = jnp.remainder(F * beam_rows[:, 0], N)[:, None, None]
    wave_x = jnp.remainder(F * beam_rows[:, 1], N)[:, None, None]
    windings = (wave_y * spot_y[None] % N + wave_x * spot_x[None] % N) % N
    phases = shifts[:, None, None] + (2.0 * math.pi / N) * windings.astype(jnp.float32)
    return jnp.cos(phases), -jnp.sin(phases)


def detector_weights(beam_total):
    digits = jnp.arange(A, dtype=jnp.int32)
    signed = jnp.where(digits < A // 2, digits, digits - A)
    radius = (signed[:, None] ** 2 + signed[None, :] ** 2).reshape(A * A)
    step_width = A // (2 * NDET)
    bin_index = jnp.arange(NDET, dtype=jnp.int32)
    member = (radius[:, None] >= (step_width * bin_index[None, :]) ** 2) & (radius[:, None] < (step_width * (bin_index[None, :] + 1)) ** 2)
    counts = jnp.sum(member.astype(jnp.float32), axis=0)
    return jnp.where(member, (A * A) / (beam_total * counts), 0.0)


def reference(pot_first, pot_second, beam_index, aberration, tile_table, tile_count):
    across = N // A
    tile_ids = tile_table.reshape(-1)
    tile_rows = tile_ids // across
    tile_cols = tile_ids % across
    slot_total = tile_ids.shape[0]

    def beam_step(running, inputs):
        beam_row, shift = inputs
        exit_real, exit_imag = exit_wave(pot_first, pot_second, beam_row)
        crop_real = exit_real.reshape(across, A, across, A)[tile_rows, :, tile_cols, :]
        crop_imag = exit_imag.reshape(across, A, across, A)[tile_rows, :, tile_cols, :]
        coef_cos, coef_sin = coefficients(tile_ids, beam_row[None, :], shift[None])
        coef_cos = coef_cos[0][:, :, None, None]
        coef_sin = coef_sin[0][:, :, None, None]
        probe_real = running[0] + (coef_cos * crop_real[:, None] - coef_sin * crop_imag[:, None])
        probe_imag = running[1] + (coef_cos * crop_imag[:, None] + coef_sin * crop_real[:, None])
        return (probe_real, probe_imag), None

    zeros = jnp.zeros((slot_total, G, A, A), jnp.float32)
    (probe_real, probe_imag), _ = lax.scan(beam_step, (zeros, zeros), (beam_index, aberration))
    cosine, sine_tab = radix_pair(1.0 / A)
    real_part, imag_part = mix_lines(rounded(probe_real), rounded(probe_imag), cosine, sine_tab, 1.0, "...yx,xk->...yk")
    real_part, imag_part = mix_lines(rounded(real_part), rounded(imag_part), cosine, sine_tab, 1.0, "...yk,yj->...jk")
    intensity = (real_part ** 2 + imag_part ** 2).reshape(slot_total * G, A * A)
    weights = detector_weights(BEAMS)
    binned = jnp.dot(intensity, weights, precision=lax.Precision.HIGHEST).reshape(tile_table.shape[0], TMAX, G, NDET)
    active = jnp.arange(TMAX, dtype=jnp.int32)[None, :] < tile_count[:, None]
    return jnp.where(active[:, :, None, None], binned, 0.0)
```

```python
import math

import jax
import jax.numpy as jnp
import numpy as np
from jax import lax
from jax.experimental import pallas as pl
from jax.experimental.pallas import tpu as pltpu
from jax.sharding import PartitionSpec as P

A = 64
N = 4096
F = 64
G = 3
NDET = 16
QMAX = 3
NB = 32
NS = 8
KY = 48
LOW = 24
F32 = jnp.float32
BF16 = jnp.bfloat16


def trig64(product):
    angles = 2.0 * np.pi / A * (np.asarray(product) % A)
    cosine = np.cos(angles).astype(np.float32).astype(jnp.bfloat16).astype(np.float32)
    sine = np.sin(angles).astype(np.float32).astype(jnp.bfloat16).astype(np.float32)
    return cosine, sine


def rotate_block(cosine, sine, orient):
    top = np.concatenate([cosine, orient * sine], axis=1)
    low = np.concatenate([-orient * sine, cosine], axis=1)
    return np.concatenate([top, low], axis=0)


def host_tables():
    d = np.arange(A)
    order = np.concatenate([np.arange(0, A, 2), np.arange(1, A, 2)])
    c, s = trig64(order[:, None] * d[None, :])
    xf1 = rotate_block(c, s, 1.0) / A
    c, s = trig64(d[:, None] * d[None, :])
    eye2 = np.eye(2)
    xf2 = rotate_block(np.kron(eye2, c), np.kron(eye2, s), -1.0) / A
    n1 = 2 * np.arange(NB)[:, None] + np.arange(2)[None, :]
    c, s = trig64(d[:, None, None] * n1[None])
    re = np.stack([c, s], axis=2).reshape(A, 2 * A)
    im = np.stack([-s, c], axis=2).reshape(A, 2 * A)
    yf1 = np.concatenate([re, im], axis=0) / A
    k2 = np.arange(56) - LOW - QMAX
    n2 = NS * np.arange(NS)[:, None] + np.arange(8)[None, :]
    c, s = trig64(k2[:, None, None] * n2[None])
    re = np.stack([c, s], axis=2).reshape(56, 2 * A)
    im = np.stack([-s, c], axis=2).reshape(56, 2 * A)
    yf2 = np.stack([re, im]) / A
    c, s = trig64(d[:, None] * (np.arange(KY) - LOW)[None, :])
    yi1 = rotate_block(c, s, -1.0)
    c, s = trig64(order[:, None] * d[None, :])
    yi2 = rotate_block(c, s, -1.0)
    k2 = np.arange(72) - QMAX
    c, s = trig64(k2[:, None] * d[None, :])
    zero = np.zeros_like(c)
    xi1 = np.stack(
        [
            np.stack(
                [np.concatenate([c, zero, s, zero], 1), np.concatenate([zero, c, zero, s], 1)]
            ),
            np.stack(
                [np.concatenate([-s, zero, c, zero], 1), np.concatenate([zero, -s, zero, c], 1)]
            ),
        ]
    )
    c, s = trig64(d[:, None] * d[None, :])
    df1 = rotate_block(c, s, -1.0) / A
    df2 = np.concatenate([c, s], axis=0) / A
    to16 = lambda t: t.astype(np.float32).astype(jnp.bfloat16)
    return {
        "xf1": to16(xf1),
        "xf2": to16(xf2),
        "yf1": to16(yf1),
        "yf2": yf2.astype(np.float32),
        "yi1": to16(yi1),
        "yi2": to16(yi2),
        "xi1": np.stack([xi1[..., :128], xi1[..., 128:]], axis=2).astype(np.float32),
        "df1": to16(df1),
        "df2": to16(df2),
    }


def ring_counts():
    d = np.arange(A)
    signed = np.where(d < A // 2, d, d - A)
    radius = signed[:, None] ** 2 + signed[None, :] ** 2
    width = A // (2 * NDET)
    return [
        int(((radius >= (width * b) ** 2) & (radius < (width * (b + 1)) ** 2)).sum())
        for b in range(NDET)
    ]


def poly_sincos(r):
    t = r * r
    sine = r + r * t * (-1.6666667e-1 + t * (8.3333333e-3 + t * (-1.9841270e-4 + t * 2.7557319e-6)))
    cosine = 1.0 + t * (-0.5 + t * (4.1666667e-2 + t * (-1.3888889e-3 + t * 2.4801587e-5)))
    return sine, cosine


def place(sine, cosine, quadrant):
    swap = (quadrant & 1) == 1
    a = jnp.where(swap, cosine, sine)
    b = jnp.where(swap, sine, cosine)
    a = jnp.where((quadrant & 2) == 2, -a, a)
    b = jnp.where(((quadrant + 1) & 2) == 2, -b, b)
    return a, b


def sincos(x):
    k = jnp.floor(x * (2.0 / math.pi) + 0.5)
    r = (x - k * 1.5707963) - k * 2.6794897e-8
    sine, cosine = poly_sincos(r)
    return place(sine, cosine, k.astype(jnp.int32))


def sincos_int(m, period):
    shift = int(math.log2(period)) - 2
    quadrant = (m + (period >> 3)) >> shift
    r = (m - (quadrant << shift)).astype(F32) * (2.0 * math.pi / period)
    sine, cosine = poly_sincos(r)
    return place(sine, cosine, quadrant)


def dot(a, b):
    return jnp.dot(a, b, preferred_element_type=F32)


def iota(shape, axis):
    return lax.broadcasted_iota(jnp.int32, shape, axis)


def x_forward(px, xf1, xf2, out, buf):
    pot = px[...].astype(F32)
    ti, tr = sincos(pot)
    wave = jnp.concatenate([tr.astype(BF16), ti.astype(BF16)], axis=0)
    y = dot(xf1[...], wave)
    row = iota((A, 128), 0)
    k1 = 2 * (row & 31) + (row >> 5)
    ts, tc = sincos_int(k1 * (iota((A, 128), 1) & 63), N)
    left = iota((32, 128), 1) < A
    for t in range(8):
        yr = y[:A, 128 * t : 128 * t + 128]
        yi = y[A:, 128 * t : 128 * t + 128]
        z = jnp.concatenate(
            [(yr * tc + yi * ts).astype(BF16), (yi * tc - yr * ts).astype(BF16)], axis=1
        )
        spec = dot(z, xf2[...])
        for part in range(2):
            block = spec[:, 128 * part : 128 * part + 128]
            even, odd = block[:32], block[32:]
            first = jnp.where(left, even, pltpu.roll(odd, A, 1))
            second = jnp.where(left, pltpu.roll(even, A, 1), odd)
            buf[pl.ds(part * 16 + 2 * t, 32, stride=32), :] = first
            buf[pl.ds(part * 16 + 2 * t + 1, 32, stride=32), :] = second
    out[...] = buf[...].astype(BF16)


def y_first(rows, yf1, out, buf, buf2):
    slab = lax.axis_index("slab")
    buf[...] = rows[...].astype(F32)
    for i in range(8):
        x = buf[pl.ds(i, 128, stride=8), :].astype(BF16)
        y = dot(yf1[...], x)
        ts, tc = sincos_int(iota((A, 128), 0) * (8 * slab + i), N)
        yr, yi = y[:A], y[A:]
        buf2[pl.ds(i, A, stride=16), :] = yr * tc + yi * ts
        buf2[pl.ds(8 + i, A, stride=16), :] = yi * tc - yr * ts
    out[...] = buf2[...].astype(BF16)


def y_second(beams, cols, yf2, yi1, yi2, out, buf, buf2):
    slab = lax.axis_index("slab")
    band = lax.axis_index("beam")
    jy = beams[slab, 0]
    jx = beams[slab, 1]
    forward = jnp.concatenate(
        [yf2[0, pl.ds(QMAX - jy, KY), :], yf2[1, pl.ds(QMAX - jy, KY), :]], axis=0
    ).astype(BF16)
    lane = iota((KY, 128), 1)
    fx = ((2 * band + (lane >> 6) + A * ((lane & 63) + jx) + N // 2) & (N - 1)) - N // 2
    qx = fx * fx
    ky0 = A * (iota((KY, 128), 0) - LOW)
    b_row = iota((A, 128), 0)

    def first(k1, carry):
        x = jnp.concatenate([cols[p, pl.ds(k1 * 16, 16), :] for p in range(NS)], axis=0)
        g = dot(forward, x)
        fy = ky0 + k1
        q = qx + fy * fy
        hs, hc = sincos_int(q, 2 * N)
        inside = q <= (N // 3) ** 2
        hc = jnp.where(inside, hc, 0.0)
        hs = jnp.where(inside, hs, 0.0)
        gr, gi = g[:KY], g[KY:]
        v = jnp.concatenate(
            [(gr * hc + gi * hs).astype(BF16), (gi * hc - gr * hs).astype(BF16)], axis=0
        )
        u = dot(yi1[...], v)
        ts, tc = sincos_int(b_row * k1, N)
        ur, ui = u[:A], u[A:]
        buf[pl.ds(k1, A, stride=128), :] = ur * tc - ui * ts
        buf[pl.ds(A + k1, A, stride=128), :] = ur * ts + ui * tc
        return carry

    lax.fori_loop(0, A, first, 0)

    def second(b, carry):
        z = buf[pl.ds(pl.multiple_of(b * 128, 128), 128), :].astype(BF16)
        w = dot(yi2[...], z)
        for k in range(4):
            buf2[pl.ds(k * A + b, 32, stride=256), :] = w[32 * k : 32 * k + 32]
        return carry

    lax.fori_loop(0, A, second, 0)
    out[...] = buf2[...].astype(BF16)


def x_inverse(beams, tiles, rows, xi1, out, buf, buf2):
    slab = lax.axis_index("slab")
    jx = beams[slab, 1]
    shifted = [
        jnp.concatenate([xi1[p, q, k, pl.ds(QMAX + jx, A), :] for k in range(2)], axis=1)
        for p in range(2)
        for q in range(2)
    ]
    table = jnp.concatenate(shifted, axis=0).astype(BF16)
    lane = iota((8, 128), 1)

    def first(f, carry):
        base = pl.multiple_of(f * 256, 256)
        z = jnp.concatenate([rows[pl.ds(base, 128), :], rows[pl.ds(base + 128, 128), :]], axis=1)
        u = dot(z, table)
        ts, tc = sincos_int((2 * f + (lane >> 6)) * (lane & 63), N)
        ts, tc = ts[:1], tc[:1]
        ur, ui = u[:, :128], u[:, 128:]
        zr = ur * tc - ui * ts
        zi = ur * ts + ui * tc
        for h in range(2):
            buf[pl.ds(h * A + f, A, stride=128), :] = zr[A * h : A * h + A]
            buf[pl.ds(h * A + 32 + f, A, stride=128), :] = zi[A * h : A * h + A]
        return carry

    lax.fori_loop(0, NB, first, 0)

    row = iota((128, 128), 0)
    col = iota((128, 128), 1)
    ids = tiles[...]
    ids = jnp.concatenate([ids, ids, ids, ids], axis=0)
    k1 = 2 * (col & 31) + (row >> 6)
    ws, wc = sincos_int((k1 * (ids & 63)) & 63, A)
    row_part = (row >> 5) & 1
    col_part = (col >> 5) & 1
    value = jnp.where(row_part == col_part, wc, jnp.where(row_part == 1, ws, -ws))
    value = jnp.where(((ids >> 6) & 1) == (col >> 6), value, 0.0).astype(BF16)
    left = iota((A, 128), 1) < A

    def second(y, carry):
        z = buf[pl.ds(pl.multiple_of(y * 128, 128), 128), :].astype(BF16)
        o = dot(value, z)
        both = jnp.where(left, o[:A], o[A:])
        both = both + pltpu.roll(both, A, 1)
        buf2[pl.ds(y, 32, stride=A), :] = jnp.where(left[:32], both[:32], both[32:])
        return carry

    lax.fori_loop(0, A, second, 0)
    out[...] = buf2[...].astype(BF16)


def detect(ids, coef, parts, pot, df1, df2, out, buf):
    left = iota((A, 128), 1) < A
    sign = jnp.where(left, -1.0, 1.0)
    ky = iota((A, 128), 0)
    kx = iota((A, 128), 1) & 63
    ky = jnp.where(ky < 32, ky, ky - A)
    kx = jnp.where(kx < 32, kx, kx - A)
    radius = ky * ky + kx * kx
    counts = ring_counts()
    width = A // (2 * NDET)
    for l in range(4):
        ident = ids[l]
        half = pl.multiple_of(((ident >> 6) & 1) * A, A)
        pair = pl.multiple_of(((ident & 63) >> 1) * 128, 128)
        tile = pot[pl.ds(half, A), pl.ds(pair, 128)].astype(F32)
        odd = (ident & 1) == 1
        turned = pltpu.roll(tile, A, 1)
        tile = jnp.where(left != odd, tile, turned)
        ps, pc = sincos(tile)
        ps = ps * sign
        fields = [parts[j, A * l : A * l + A, :].astype(F32) for j in range(8)]
        swapped = [pltpu.roll(f, A, 1) * sign for f in fields]
        for g in range(G):
            probe = jnp.zeros((A, 128), F32)
            for j in range(8):
                at = (j * 4 + l) * G + g
                probe = probe + fields[j] * coef[0, at] + swapped[j] * coef[1, at]
            probe = probe * pc + pltpu.roll(probe, A, 1) * ps
            d = dot(probe.astype(BF16), df1[...]).astype(BF16)
            w = dot(df2[...], d)
            value = w[:A] - sign * pltpu.roll(w[A:], A, 1)
            power = value * value
            for b in range(NDET):
                member = (radius >= (width * b) ** 2) & (radius < (width * (b + 1)) ** 2)
                part = jnp.where(member, power, 0.0) * (A * A / (8.0 * counts[b]))
                buf[(l * G + g) * NDET + b, :] = jnp.sum(part, axis=0)
    ones = jnp.ones((8, 128), F32)
    total = lax.dot_general(
        ones,
        buf[...],
        (((1,), (1,)), ((), ())),
        precision=lax.Precision.HIGHEST,
        preferred_element_type=F32,
    )
    out[...] = total


def call(kernel, out_shape, out_type, scratch, smem, args):
    specs = [
        pl.BlockSpec(memory_space=pltpu.SMEM if k < smem else pltpu.VMEM) for k in range(len(args))
    ]
    return pl.pallas_call(
        kernel,
        out_shape=jax.ShapeDtypeStruct(out_shape, out_type),
        in_specs=specs,
        out_specs=pl.BlockSpec(memory_space=pltpu.VMEM),
        scratch_shapes=[pltpu.VMEM(s, F32) for s in scratch],
        compiler_params=pltpu.CompilerParams(vmem_limit_bytes=50 * 1024 * 1024),
    )(*args)


def coefficients(tile_ids, beam_rows, shifts):
    across = N // A
    offsets = jnp.arange(G, dtype=jnp.int32)
    spot_y = (tile_ids // across)[:, None] * A + A // 2 + offsets[None, :]
    spot_x = (tile_ids % across)[:, None] * A + A // 2 + 2 * offsets[None, :]
    wave_y = jnp.remainder(F * beam_rows[:, 0], N)[:, None, None]
    wave_x = jnp.remainder(F * beam_rows[:, 1], N)[:, None, None]
    windings = (wave_y * spot_y[None] % N + wave_x * spot_x[None] % N) % N
    phases = shifts[:, None, None] + 2.0 * math.pi / N * windings.astype(F32)
    return (jnp.cos(phases), -jnp.sin(phases))


def shards(pot_first, pot_second, beam_index, aberration, tile_table, tile_count):
    band = lax.axis_index("beam")
    slab = lax.axis_index("slab")
    tab = host_tables()
    px = lax.dynamic_slice_in_dim(pot_first.reshape(2, A, N), 8 * slab, 8, 1)
    px = px.reshape(16, A, A).transpose(1, 0, 2).reshape(A, 1024)
    msg = call(
        x_forward, (1024, 128), BF16, [(1024, 128)], 0, (px, tab["xf1"], tab["xf2"])
    )
    rows = lax.all_to_all(msg.reshape(NB, 32, 128), "beam", 0, 0, tiled=True)
    piece = call(
        y_first,
        (1024, 128),
        BF16,
        [(1024, 128), (1024, 128)],
        0,
        (rows.reshape(1024, 128), tab["yf1"]),
    )
    cols = lax.all_gather(piece, "slab")
    msg = call(
        y_second,
        (8192, 128),
        BF16,
        [(8192, 128), (8192, 128)],
        1,
        (beam_index, cols, tab["yf2"], tab["yi1"], tab["yi2"]),
    )
    rows = lax.all_to_all(msg.reshape(NB, 256, 128), "beam", 0, 0, tiled=True)

    lists = tile_table.reshape(NB, NB)
    matched = (lists // 128) == band
    chosen = jnp.sum(jnp.where(matched, lists, 0), axis=1)
    within = jnp.arange(NB, dtype=jnp.int32) % 4
    active = within[None, :] < jnp.repeat(tile_count.reshape(NB, NS), 4, axis=1)
    active = jnp.sum(jnp.where(matched & active, 1.0, 0.0), axis=1)
    tiles = jnp.broadcast_to(chosen[:, None], (NB, 128))
    exits = call(
        x_inverse,
        (2048, 128),
        BF16,
        [(8192, 128), (2048, 128)],
        1,
        (beam_index, tiles, rows.reshape(8192, 128), tab["xi1"]),
    )
    parts = lax.all_to_all(exits.reshape(NS, 256, 128), "slab", 0, 0, tiled=True)
    own = lax.dynamic_slice_in_dim(chosen, 4 * slab, 4, 0)
    cc, cs = coefficients(own, beam_index, aberration)
    coef = jnp.stack([cc.reshape(-1), cs.reshape(-1)])
    sums = call(
        detect,
        (8, 192),
        F32,
        [(192, 128)],
        2,
        (own, coef, parts, pot_second, tab["df1"], tab["df2"]),
    )
    sums = sums[0].reshape(4, G * NDET)
    sums = jnp.where(lax.dynamic_slice_in_dim(active, 4 * slab, 4, 0)[:, None] > 0, sums, 0.0)
    spread = jnp.where(
        (jnp.arange(NS) == slab)[:, None, None], sums[None], 0.0
    ).reshape(NB, G * NDET)
    spread = lax.all_to_all(spread, "beam", 0, 0, tiled=True)
    spread = lax.psum(spread, "slab")
    mine = lax.dynamic_index_in_dim(lists, band, 0, keepdims=False) // 128
    mine = lax.dynamic_slice_in_dim(mine, 4 * slab, 4, 0)
    return spread[mine].reshape(1, 4, G, NDET)


def solution(mesh):
    return jax.shard_map(
        shards,
        mesh=mesh,
        in_specs=(P("beam", None), P("beam", None), P(), P(), P(), P()),
        out_specs=P(("beam", "slab"), None, None, None),
        check_vma=False,
    )
```

```python
import math

import jax
import jax.numpy as jnp
import numpy as np
from jax import lax
from jax.experimental import pallas as pl
from jax.experimental.pallas import tpu as pltpu
from jax.sharding import PartitionSpec as P

A = 64
N = 4096
F = 64
G = 3
NDET = 16
QMAX = 3
NB = 32
NS = 8
KY = 48
LOW = 24
AGC = 4
AXC = 4
F32 = jnp.float32
BF16 = jnp.bfloat16


def trig64(product):
    angles = 2.0 * np.pi / A * (np.asarray(product) % A)
    cosine = np.cos(angles).astype(np.float32).astype(jnp.bfloat16).astype(np.float32)
    sine = np.sin(angles).astype(np.float32).astype(jnp.bfloat16).astype(np.float32)
    return cosine, sine


def rotate_block(cosine, sine, orient):
    top = np.concatenate([cosine, orient * sine], axis=1)
    low = np.concatenate([-orient * sine, cosine], axis=1)
    return np.concatenate([top, low], axis=0)


def host_tables():
    d = np.arange(A)
    order = np.concatenate([np.arange(0, A, 2), np.arange(1, A, 2)])
    c, s = trig64(order[:, None] * d[None, :])
    xf1 = rotate_block(c, s, 1.0) / A
    c, s = trig64(d[:, None] * d[None, :])
    eye2 = np.eye(2)
    xf2 = rotate_block(np.kron(eye2, c), np.kron(eye2, s), -1.0) / A
    n1 = 2 * np.arange(NB)[:, None] + np.arange(2)[None, :]
    c, s = trig64(d[:, None, None] * n1[None])
    re = np.stack([c, s], axis=2).reshape(A, 2 * A)
    im = np.stack([-s, c], axis=2).reshape(A, 2 * A)
    yf1 = np.concatenate([re, im], axis=0) / A
    c, s = trig64(d[:, None] * (np.arange(KY) - LOW)[None, :])
    yi1 = rotate_block(c, s, -1.0)
    c, s = trig64(order[:, None] * d[None, :])
    yi2 = rotate_block(c, s, -1.0)
    c, s = trig64(d[:, None] * d[None, :])
    df1 = rotate_block(c, s, -1.0) / A
    df2 = np.concatenate([c, s], axis=0) / A
    to16 = lambda t: t.astype(np.float32).astype(jnp.bfloat16)
    return {
        "xf1": to16(xf1),
        "xf2": to16(xf2),
        "yf1": to16(yf1),
        "yi1": to16(yi1),
        "yi2": to16(yi2),
        "df1": to16(df1),
        "df2": to16(df2),
    }


def ring_counts():
    d = np.arange(A)
    signed = np.where(d < A // 2, d, d - A)
    radius = signed[:, None] ** 2 + signed[None, :] ** 2
    width = A // (2 * NDET)
    return [
        int(((radius >= (width * b) ** 2) & (radius < (width * (b + 1)) ** 2)).sum())
        for b in range(NDET)
    ]


def poly_sincos(r):
    t = r * r
    sine = r + r * t * (-1.6666667e-1 + t * (8.3333333e-3 + t * (-1.9841270e-4 + t * 2.7557319e-6)))
    cosine = 1.0 + t * (-0.5 + t * (4.1666667e-2 + t * (-1.3888889e-3 + t * 2.4801587e-5)))
    return sine, cosine


def place(sine, cosine, quadrant):
    swap = (quadrant & 1) == 1
    a = jnp.where(swap, cosine, sine)
    b = jnp.where(swap, sine, cosine)
    a = jnp.where((quadrant & 2) == 2, -a, a)
    b = jnp.where(((quadrant + 1) & 2) == 2, -b, b)
    return a, b


def sincos(x):
    k = jnp.floor(x * (2.0 / math.pi) + 0.5)
    r = (x - k * 1.5707963) - k * 2.6794897e-8
    sine, cosine = poly_sincos(r)
    return place(sine, cosine, k.astype(jnp.int32))


def sincos_int(m, period):
    shift = int(math.log2(period)) - 2
    quadrant = (m + (period >> 3)) >> shift
    r = (m - (quadrant << shift)).astype(F32) * (2.0 * math.pi / period)
    sine, cosine = poly_sincos(r)
    return place(sine, cosine, quadrant)


def dot(a, b):
    return jnp.dot(a, b, preferred_element_type=F32)


def iota(shape, axis):
    return lax.broadcasted_iota(jnp.int32, shape, axis)


def remote(src, dst, send, recv, target):
    return pltpu.make_async_remote_copy(
        src_ref=src,
        dst_ref=dst,
        send_sem=send,
        recv_sem=recv,
        device_id=target,
        device_id_type=pl.DeviceIdType.MESH,
    )


def x_forward(px, xf1, xf2, out, buf):
    pot = px[...].astype(F32)
    ti, tr = sincos(pot)
    wave = jnp.concatenate([tr.astype(BF16), ti.astype(BF16)], axis=0)
    y = dot(xf1[...], wave)
    row = iota((A, 128), 0)
    k1 = 2 * (row & 31) + (row >> 5)
    ts, tc = sincos_int(k1 * (iota((A, 128), 1) & 63), N)
    left = iota((32, 128), 1) < A
    for t in range(8):
        yr = y[:A, 128 * t : 128 * t + 128]
        yi = y[A:, 128 * t : 128 * t + 128]
        z = jnp.concatenate(
            [(yr * tc + yi * ts).astype(BF16), (yi * tc - yr * ts).astype(BF16)], axis=1
        )
        spec = dot(z, xf2[...])
        for part in range(2):
            block = spec[:, 128 * part : 128 * part + 128]
            even, odd = block[:32], block[32:]
            first = jnp.where(left, even, pltpu.roll(odd, A, 1))
            second = jnp.where(left, pltpu.roll(even, A, 1), odd)
            buf[pl.ds(part * 16 + 2 * t, 32, stride=32), :] = first
            buf[pl.ds(part * 16 + 2 * t + 1, 32, stride=32), :] = second
    for f in range(NB):
        out[f] = buf[32 * f : 32 * f + 32, :].astype(BF16)


def tables(jx, band, fresnel, twist):
    lane = iota((KY, 128), 1)
    fx = ((2 * band + (lane >> 6) + A * ((lane & 63) + jx) + N // 2) & (N - 1)) - N // 2
    qx = fx * fx
    ky0 = A * (iota((KY, 128), 0) - LOW)
    b_row = iota((A, 128), 0)

    def step(k1, carry):
        fy = ky0 + k1
        q = qx + fy * fy
        hs, hc = sincos_int(q, 2 * N)
        inside = q <= (N // 3) ** 2
        fresnel[k1, :KY, :] = jnp.where(inside, hc, 0.0)
        fresnel[k1, KY:, :] = jnp.where(inside, hs, 0.0)
        ts, tc = sincos_int(b_row * k1, N)
        twist[k1, :A, :] = tc
        twist[k1, A:, :] = ts
        return carry

    lax.fori_loop(0, A, step, 0, unroll=2)


def forward_table(jy):
    row = iota((KY, 128), 0)
    col = iota((KY, 128), 1)
    n2 = NS * (col >> 4) + (col & 7)
    s, c = sincos_int((n2 * (row - LOW - jy)) & (A - 1), A)
    s = s.astype(BF16).astype(F32) * (1.0 / A)
    c = c.astype(BF16).astype(F32) * (1.0 / A)
    first = (col & 8) == 0
    both = [jnp.where(first, c, s), jnp.where(first, -s, c)]
    return jnp.concatenate(both, axis=0).astype(BF16)


def inverse_table(jx):
    lane = iota((A, 128), 1)
    s, c = sincos_int(((iota((A, 128), 0) + jx) * (lane & 63)) & (A - 1), A)
    left = lane < A
    blocks = []
    for pair in ((c, s), (-s, c)):
        for q in range(2):
            keep = left if q == 0 else ~left
            blocks.append(jnp.concatenate([jnp.where(keep, v, 0.0) for v in pair], axis=1))
    return jnp.concatenate(blocks, axis=0).astype(BF16)


def y_first(slab, rows, yf1, out, buf, buf2):
    for f in range(NB):
        buf[32 * f : 32 * f + 32, :] = rows[f].astype(F32)
    for i in range(8):
        x = buf[pl.ds(i, 128, stride=8), :].astype(BF16)
        y = dot(yf1[...], x)
        ts, tc = sincos_int(iota((A, 128), 0) * (8 * slab + i), N)
        yr, yi = y[:A], y[A:]
        buf2[pl.ds(i, A, stride=16), :] = yr * tc + yi * ts
        buf2[pl.ds(8 + i, A, stride=16), :] = yi * tc - yr * ts
    out[...] = buf2[pl.ds(0, 1024), :].astype(BF16)


def y_second(start, forward, cols, yi1, fresnel, twist, buf):
    def step(k1, carry):
        x = jnp.concatenate(
            [cols[p, pl.ds(pl.multiple_of(k1 * 16, 16), 16), :] for p in range(NS)], axis=0
        )
        g = dot(forward, x)
        hc, hs = fresnel[k1, :KY, :], fresnel[k1, KY:, :]
        gr, gi = g[:KY], g[KY:]
        v = jnp.concatenate(
            [(gr * hc + gi * hs).astype(BF16), (gi * hc - gr * hs).astype(BF16)], axis=0
        )
        u = dot(yi1[...], v)
        tc, ts = twist[k1, :A, :], twist[k1, A:, :]
        ur, ui = u[:A], u[A:]
        buf[pl.ds(k1, A, stride=128), :] = ur * tc - ui * ts
        buf[pl.ds(A + k1, A, stride=128), :] = ur * ts + ui * tc
        return carry

    lax.fori_loop(start, start + A // AGC, step, 0, unroll=4)


def y_third(c, yi2, out, buf, buf2):
    size = A // AXC

    def step(b, carry):
        z = buf[pl.ds(pl.multiple_of((c * size + b) * 128, 128), 128), :].astype(BF16)
        w = dot(yi2[...], z)
        for k in range(4):
            buf2[pl.ds(k * size + b, NB, stride=4 * size), :] = w[32 * k : 32 * k + 32]
        return carry

    lax.fori_loop(0, size, step, 0, unroll=4)

    def pack(f, carry):
        out[c, f] = buf2[pl.ds(pl.multiple_of(f * 4 * size, 4 * size), 4 * size), :].astype(BF16)
        return carry

    lax.fori_loop(0, NB, pack, 0, unroll=4)


def x_second(c, table, rows, buf):
    size = A // AXC
    lane = iota((8, 128), 1)

    def step(f, carry):
        z = jnp.concatenate([rows[c, f, : 2 * size, :], rows[c, f, 2 * size :, :]], axis=1)
        u = dot(z, table)
        ts, tc = sincos_int((2 * f + (lane >> 6)) * (lane & 63), N)
        ts, tc = ts[:1], tc[:1]
        ur, ui = u[:, :128], u[:, 128:]
        zr = ur * tc - ui * ts
        zi = ur * ts + ui * tc
        for h in range(2):
            base = c * size * 128 + h * A + f
            buf[pl.ds(base, size, stride=128), :] = zr[size * h : size * h + size]
            buf[pl.ds(base + 32, size, stride=128), :] = zi[size * h : size * h + size]
        return carry

    lax.fori_loop(0, NB, step, 0, unroll=4)


def x_third(ids, out, buf, buf2):
    row = iota((128, 128), 0)
    col = iota((128, 128), 1)
    ids = jnp.broadcast_to(jnp.concatenate([ids, ids, ids, ids], axis=0), (128, 128))
    k1 = 2 * (col & 31) + (row >> 6)
    ws, wc = sincos_int((k1 * (ids & 63)) & 63, A)
    row_part = (row >> 5) & 1
    col_part = (col >> 5) & 1
    value = jnp.where(row_part == col_part, wc, jnp.where(row_part == 1, ws, -ws))
    value = jnp.where(((ids >> 6) & 1) == (col >> 6), value, 0.0).astype(BF16)
    left = iota((A, 128), 1) < A

    def step(y, carry):
        z = buf[pl.ds(pl.multiple_of(y * 128, 128), 128), :].astype(BF16)
        o = dot(value, z)
        both = jnp.where(left, o[:A], o[A:])
        both = both + pltpu.roll(both, A, 1)
        buf2[pl.ds(y, 32, stride=A), :] = jnp.where(left[:32], both[:32], both[32:])
        return carry

    lax.fori_loop(0, A, step, 0, unroll=4)
    for p in range(NS):
        out[p] = buf2[256 * p : 256 * p + 256, :].astype(BF16)


def own_tiles(band, slab, tiles):
    found = []
    for l in range(4):
        ident = jnp.int32(0)
        for q in range(NS):
            for k in range(4):
                value = tiles[(4 * slab + l) * NS + q, k]
                ident = ident + jnp.where((value >> 7) == band, value, 0)
        found.append(ident)
    return found


def probe_factors(ids, beams, shifts):
    sub = iota((8, 128), 0)
    lane = iota((8, 128), 1)
    by = jnp.zeros((8, 128), jnp.int32)
    bx = jnp.zeros((8, 128), jnp.int32)
    ab = jnp.zeros((8, 128), F32)
    for j in range(8):
        by = jnp.where(sub == j, beams[j, 0], by)
        bx = jnp.where(sub == j, beams[j, 1], bx)
        ab = jnp.where(sub == j, shifts[j], ab)
    ry = jnp.zeros((8, 128), jnp.int32)
    rx = jnp.zeros((8, 128), jnp.int32)
    for l in range(4):
        for g in range(G):
            here = lane == l * G + g
            ry = jnp.where(here, (ids[l] >> 6) * A + A // 2 + g, ry)
            rx = jnp.where(here, (ids[l] & 63) * A + A // 2 + 2 * g, rx)
    m = (F * (by * ry + bx * rx)) & (N - 1)
    s, c = sincos(ab + 2.0 * math.pi / N * m.astype(F32))
    return c, -s


def split_tiles(pot, out):
    for h in range(2):
        for pair in range(32):
            out[32 * h + pair] = pot[A * h : A * h + A, 128 * pair : 128 * pair + 128]


def detect(ids, alpha, parts, pot, df1, df2, out, buf):
    left = iota((A, 128), 1) < A
    sign = jnp.where(left, -1.0, 1.0)
    ky = iota((A, 128), 0)
    kx = iota((A, 128), 1) & 63
    ky = jnp.where(ky < 32, ky, ky - A)
    kx = jnp.where(kx < 32, kx, kx - A)
    radius = ky * ky + kx * kx
    counts = ring_counts()
    width = A // (2 * NDET)
    ones = jnp.ones((8, 128), F32)
    for l in range(4):
        ident = ids[l]
        tile = pot[((ident & 127) >> 1)].astype(F32)
        odd = (ident & 1) == 1
        turned = pltpu.roll(tile, A, 1)
        tile = jnp.where(left != odd, tile, turned)
        ps, pc = sincos(tile)
        ps = ps * sign
        fields = [parts[j, A * l : A * l + A, :].astype(F32) for j in range(8)]
        swapped = [pltpu.roll(f, A, 1) * sign for f in fields]
        for g in range(G):
            probe = jnp.zeros((A, 128), F32)
            at = l * G + g
            for j in range(8):
                probe = (
                    probe
                    + fields[j] * alpha[0][j : j + 1, at : at + 1]
                    + swapped[j] * alpha[1][j : j + 1, at : at + 1]
                )
            probe = probe * pc + pltpu.roll(probe, A, 1) * ps
            d = dot(probe.astype(BF16), df1[...]).astype(BF16)
            w = dot(df2[...], d)
            value = w[:A] - sign * pltpu.roll(w[A:], A, 1)
            power = value * value
            for b in range(NDET):
                member = (radius >= (width * b) ** 2) & (radius < (width * (b + 1)) ** 2)
                part = jnp.where(member, power, 0.0) * (A * A / (8.0 * counts[b]))
                buf[g * NDET + b : g * NDET + b + 1, :] = jnp.sum(part, axis=0, keepdims=True)
        total = lax.dot_general(
            ones,
            buf[0:128, :],
            (((1,), (1,)), ((), ())),
            precision=lax.Precision.HIGHEST,
            preferred_element_type=F32,
        )
        out[l] = total[:1]


def kernel(
    beams,
    shifts,
    tiles_s,
    counts,
    tiles_v,
    px,
    pot2,
    xf1,
    xf2,
    yf1,
    yi1,
    yi2,
    df1,
    df2,
    out,
    buf,
    buf2,
    pairs,
    fresnel,
    twist,
    msg1,
    rows1,
    cols,
    msg2,
    rows2,
    msg3,
    parts,
    res,
    sums,
    send1,
    recv1,
    sendg,
    recvg,
    send2,
    recv2,
    send3,
    recv3,
    send4,
    recv4,
):
    band = lax.axis_index("beam")
    slab = lax.axis_index("slab")
    jy = beams[slab, 0]
    jx = beams[slab, 1]
    barrier = pltpu.get_barrier_semaphore()

    def greet_beam(k, carry):
        target = {"beam": (band + k) & (NB - 1), "slab": slab}
        pl.semaphore_signal(
            barrier, inc=1, device_id=target, device_id_type=pl.DeviceIdType.MESH
        )
        return carry

    lax.fori_loop(1, NB, greet_beam, 0)

    def greet_slab(k, carry):
        target = {"beam": band, "slab": (slab + k) & (NS - 1)}
        pl.semaphore_signal(
            barrier, inc=1, device_id=target, device_id_type=pl.DeviceIdType.MESH
        )
        return carry

    lax.fori_loop(1, NS, greet_slab, 0)
    home = band >> 2

    def greet_home(k, carry):
        source = {"beam": (band + k) & (NB - 1), "slab": home}
        pl.semaphore_signal(
            barrier, inc=1, device_id=source, device_id_type=pl.DeviceIdType.MESH
        )
        return carry

    @pl.when(home != slab)
    def _():
        lax.fori_loop(1, NB, greet_home, 0)

    x_forward(px, xf1, xf2, msg1, buf)
    extra = 4 * (NS - 1) - jnp.where(home == slab, NS - 1, 0)
    pl.semaphore_wait(barrier, NB - 1 + NS - 1 + extra)

    def exchange1(k):
        target = (band + k) & (NB - 1)
        return remote(
            msg1.at[target], rows1.at[band], send1.at[target], recv1.at[band],
            {"beam": target, "slab": slab},
        )

    def arrival1(k):
        source = (band + k) & (NB - 1)
        return remote(
            msg1.at[source], rows1.at[source], send1.at[source], recv1.at[source],
            {"beam": source, "slab": slab},
        )

    lax.fori_loop(1, NB, lambda k, c: (exchange1(k).start(), c)[1], 0)
    rows1[band] = msg1[band]
    tables(jx, band, fresnel, twist)
    split_tiles(pot2, pairs)
    lax.fori_loop(1, NB, lambda k, c: (arrival1(k).wait_recv(), c)[1], 0)
    y_first(slab, rows1, yf1, cols.at[slab], buf, buf2)

    core = slab & 1
    right = (slab + 2) & (NS - 1)
    left = (slab + 6) & (NS - 1)
    far = (slab + 4) & (NS - 1)
    partner = slab ^ 1
    step = 1024 // AGC

    def gather(source, c, half, kind, target):
        begin = c * step + (step // 2 if half == 1 else 0)
        length = step if half is None else step // 2
        view = cols.at[source, pl.ds(begin, length), :]
        return remote(
            view, view, sendg.at[kind, c], recvg.at[source, c, 1 if half == 1 else 0],
            {"beam": band, "slab": target},
        )

    for c in range(AGC):
        gather(slab, c, None, 0, right).start()
        gather(slab, c, None, 1, left).start()
        gather(slab, c, None, 2, partner).start()
    for c in range(AGC):
        gather(left, c, None, 0, left).wait_recv()
        gather(left, c, 0, 3, right).start()
        gather(left, c, None, 4, partner).start()
        gather(right, c, None, 1, right).wait_recv()
        gather(right, c, 1, 5, left).start()
        gather(right, c, None, 6, partner).start()

    forward = forward_table(jy)
    for c in range(AGC):
        gather(far, c, 0, 3, left).wait_recv()
        gather(far, c, 1, 5, right).wait_recv()
        gather(far, c, None, 7, partner).start()
        for source in (partner, left ^ 1, right ^ 1, far ^ 1):
            gather(source, c, None, 2, partner).wait_recv()
        y_second(c * (A // AGC), forward, cols, yi1, fresnel, twist, buf)

    def exchange2(c, k):
        target = (band + k) & (NB - 1)
        return remote(
            msg2.at[c, target], rows2.at[c, band], send2.at[c, target], recv2.at[c, band],
            {"beam": target, "slab": slab},
        )

    def arrival2(c, k):
        source = (band + k) & (NB - 1)
        return remote(
            msg2.at[c, source], rows2.at[c, source], send2.at[c, source], recv2.at[c, source],
            {"beam": source, "slab": slab},
        )

    for c in range(AXC):
        y_third(c, yi2, msg2, buf, buf2)
        lax.fori_loop(1, NB, lambda k, z: (exchange2(c, k).start(), z)[1], 0)
        rows2[c, band] = msg2[c, band]

    table = inverse_table(jx)
    for c in range(AXC):
        lax.fori_loop(1, NB, lambda k, z: (arrival2(c, k).wait_recv(), z)[1], 0)
        x_second(c, table, rows2, buf)

    wanted = tiles_v[...]
    wanted = jnp.where((wanted >> 7) == band, wanted, 0).reshape(NB, NS, 4)
    wanted = jnp.sum(jnp.sum(wanted, axis=1), axis=1, keepdims=True)
    x_third(wanted, msg3, buf, buf2)

    def exchange3(k):
        target = (slab + k) & (NS - 1)
        return remote(
            msg3.at[target], parts.at[slab], send3.at[target], recv3.at[slab],
            {"beam": band, "slab": target},
        )

    def arrival3(k):
        source = (slab + k) & (NS - 1)
        return remote(
            msg3.at[source], parts.at[source], send3.at[source], recv3.at[source],
            {"beam": band, "slab": source},
        )

    lax.fori_loop(1, NS, lambda k, z: (exchange3(k).start(), z)[1], 0)
    parts[slab] = msg3[slab]
    ids = own_tiles(band, slab, tiles_s)
    alpha = probe_factors(ids, beams, shifts)
    lax.fori_loop(1, NS, lambda k, z: (arrival3(k).wait_recv(), z)[1], 0)
    detect(ids, alpha, parts, pairs, df1, df2, res, buf)

    def exchange4(l, p):
        group = 4 * slab + l
        return remote(
            res.at[l], sums.at[band], send4.at[l, p], recv4.at[band],
            {"beam": group, "slab": p},
        )

    def arrival4(source):
        return remote(
            res.at[0], sums.at[source], send4.at[0, 0], recv4.at[source],
            {"beam": source, "slab": home},
        )

    def each4(act):
        for l in range(4):

            def body(p, carry):
                @pl.when((4 * slab + l != band) | (p != slab))
                def _():
                    act(exchange4(l, p))

                return carry

            lax.fori_loop(0, NS, body, 0)

    each4(lambda copy: copy.start())

    @pl.when(home == slab)
    def _():
        sums[band] = res[band & 3]

    def finish(source, carry):
        @pl.when((source != band) | (home != slab))
        def _():
            arrival4(source).wait_recv()

        return carry

    lax.fori_loop(0, NB, finish, 0)
    block = band * NS + slab
    for k in range(4):
        row = sums[tiles_s[block, k] >> 7]
        row = jnp.where(k < counts[block], row, 0.0)
        for g in range(G):
            out[0, k, g : g + 1, :] = row[:, NDET * g : NDET * g + NDET]

    lax.fori_loop(1, NB, lambda k, z: (exchange1(k).wait_send(), z)[1], 0)
    for c in range(AGC):
        gather(slab, c, None, 0, right).wait_send()
        gather(slab, c, None, 1, left).wait_send()
        gather(slab, c, None, 2, partner).wait_send()
        gather(left, c, 0, 3, right).wait_send()
        gather(left, c, None, 4, partner).wait_send()
        gather(right, c, 1, 5, left).wait_send()
        gather(right, c, None, 6, partner).wait_send()
        gather(far, c, None, 7, partner).wait_send()
    for c in range(AXC):
        lax.fori_loop(1, NB, lambda k, z: (exchange2(c, k).wait_send(), z)[1], 0)
    lax.fori_loop(1, NS, lambda k, z: (exchange3(k).wait_send(), z)[1], 0)
    each4(lambda copy: copy.wait_send())


def shards(pot_first, pot_second, beam_index, aberration, tile_table, tile_count):
    slab = lax.axis_index("slab")
    tab = host_tables()
    px = lax.dynamic_slice_in_dim(pot_first.reshape(2, A, N), 8 * slab, 8, 1)
    px = px.reshape(16, A, A).transpose(1, 0, 2).reshape(A, 1024)
    names = ("xf1", "xf2", "yf1", "yi1", "yi2", "df1", "df2")
    args = (beam_index, aberration, tile_table, tile_count, tile_table, px, pot_second)
    args = args + tuple(tab[name] for name in names)
    specs = [pl.BlockSpec(memory_space=pltpu.SMEM if k < 4 else pltpu.VMEM) for k in range(len(args))]
    size = 4 * A // AXC
    dma = pltpu.SemaphoreType.DMA
    return pl.pallas_call(
        kernel,
        out_shape=jax.ShapeDtypeStruct((1, 4, G, NDET), F32),
        in_specs=specs,
        out_specs=pl.BlockSpec(memory_space=pltpu.VMEM),
        scratch_shapes=[
            pltpu.VMEM((A * 128, 128), F32),
            pltpu.VMEM((2048, 128), F32),
            pltpu.VMEM((64, A, 128), BF16),
            pltpu.VMEM((A, 2 * KY, 128), F32),
            pltpu.VMEM((A, 128, 128), F32),
            pltpu.VMEM((NB, 32, 128), BF16),
            pltpu.VMEM((NB, 32, 128), BF16),
            pltpu.VMEM((NS, 1024, 128), BF16),
            pltpu.VMEM((AXC, NB, size, 128), BF16),
            pltpu.VMEM((AXC, NB, size, 128), BF16),
            pltpu.VMEM((NS, 256, 128), BF16),
            pltpu.VMEM((NS, 256, 128), BF16),
            pltpu.VMEM((4, 1, 128), F32),
            pltpu.VMEM((NB, 1, 128), F32),
            dma((NB,)),
            dma((NB,)),
            dma((8, AGC)),
            dma((NS, AGC, 2)),
            dma((AXC, NB)),
            dma((AXC, NB)),
            dma((NS,)),
            dma((NS,)),
            dma((4, NS)),
            dma((NB,)),
        ],
        compiler_params=pltpu.CompilerParams(
            vmem_limit_bytes=50 * 1024 * 1024, collective_id=0, has_side_effects=True
        ),
    )(*args)


def solution(mesh):
    return jax.shard_map(
        shards,
        mesh=mesh,
        in_specs=(P("beam", None), P("beam", None), P(), P(), P(), P()),
        out_specs=P(("beam", "slab"), None, None, None),
        check_vma=False,
    )
```

```python
import math

import jax
import jax.numpy as jnp
import numpy as np
from jax import lax
from jax.experimental import pallas as pl
from jax.experimental.pallas import tpu as pltpu
from jax.sharding import PartitionSpec as P

A = 64
N = 4096
F = 64
G = 3
NDET = 16
QMAX = 3
NB = 32
NS = 8
KY = 48
LOW = 24
SPARE = 20
F32 = jnp.float32
BF16 = jnp.bfloat16


def ring_counts():
    d = np.arange(A)
    signed = np.where(d < A // 2, d, d - A)
    radius = signed[:, None] ** 2 + signed[None, :] ** 2
    width = A // (2 * NDET)
    return [
        int(((radius >= (width * b) ** 2) & (radius < (width * (b + 1)) ** 2)).sum())
        for b in range(NDET)
    ]


def poly_sincos(r):
    t = r * r
    sine = r + r * t * (-1.6666667e-1 + t * (8.3333333e-3 + t * (-1.9841270e-4 + t * 2.7557319e-6)))
    cosine = 1.0 + t * (-0.5 + t * (4.1666667e-2 + t * (-1.3888889e-3 + t * 2.4801587e-5)))
    return sine, cosine


def place(sine, cosine, quadrant):
    swap = (quadrant & 1) == 1
    a = jnp.where(swap, cosine, sine)
    b = jnp.where(swap, sine, cosine)
    a = jnp.where((quadrant & 2) == 2, -a, a)
    b = jnp.where(((quadrant + 1) & 2) == 2, -b, b)
    return a, b


def sincos(x):
    k = jnp.floor(x * (2.0 / math.pi) + 0.5)
    r = (x - k * 1.5707963) - k * 2.6794897e-8
    sine, cosine = poly_sincos(r)
    return place(sine, cosine, k.astype(jnp.int32))


def sincos_int(m, period):
    shift = int(math.log2(period)) - 2
    quadrant = (m + (period >> 3)) >> shift
    r = (m - (quadrant << shift)).astype(F32) * (2.0 * math.pi / period)
    sine, cosine = poly_sincos(r)
    return place(sine, cosine, quadrant)


def dot(a, b):
    return jnp.dot(a, b, preferred_element_type=F32)


def iota(shape, axis):
    return lax.broadcasted_iota(jnp.int32, shape, axis)


def remote(src, dst, send, recv, target):
    return pltpu.make_async_remote_copy(
        src_ref=src,
        dst_ref=dst,
        send_sem=send,
        recv_sem=recv,
        device_id=target,
        device_id_type=pl.DeviceIdType.MESH,
    )


def swap(v):
    return pltpu.roll(v, A, 1)


def left_half():
    return iota((1, 128), 1) < A


def sign():
    return jnp.where(left_half(), 1.0, -1.0)


def table64(product):
    s, c = sincos_int(product & (A - 1), A)
    return c.astype(BF16).astype(F32), s.astype(BF16).astype(F32)


def stacked(product, scale):
    c, s = table64(product)
    return jnp.concatenate([c * scale, s * scale], axis=0).astype(BF16)


def x_tables():
    row = iota((128, 128), 0)
    col = iota((128, 128), 1)
    k1 = 2 * (row & 31) + ((row >> 5) & 1)
    blocks = []
    for rho in range(2):
        c, s = table64(k1 * (2 * (col & 31) + rho))
        same = (row >> 6) == ((col >> 5) & 1)
        blocks.append(jnp.where(same, c, jnp.where(row < A, s, -s)) * (1.0 / A))
    first = jnp.concatenate(blocks, axis=0)[:, :A].astype(BF16)
    lane = iota((A, 128), 1)
    c, s = table64(iota((A, 128), 0) * (lane & 63))
    left = lane < A
    zero = jnp.zeros((A, 128), F32)
    rows = []
    for block in (jnp.where(left, c, -s), jnp.where(left, s, c)):
        block = block * (1.0 / A)
        rows.append(jnp.concatenate([block, zero], axis=1))
        rows.append(jnp.concatenate([zero, block], axis=1))
    second = jnp.concatenate(rows, axis=0).astype(BF16)
    return first, second


def x_forward(slab, potential, out, buf):
    odd = (slab & 1) == 1
    for h in range(2):
        block = potential[h].astype(F32)
        block = jnp.where(odd, block[8:], block[:8])
        sine, cosine = sincos(block)
        for part, wave in enumerate((cosine, sine)):
            for p in range(32):
                start = h * 8 * A + part * 32 + p
                buf[pl.ds(start, 8, stride=A), :] = wave[:, 128 * p : 128 * p + 128]
    first, second = x_tables()
    row = iota((A, 128), 0)
    k1 = 2 * (row & 31) + (row >> 5)
    ts, tc = sincos_int(k1 * (iota((A, 128), 1) & 63), N)
    left = left_half()
    waves = [buf[A * r : A * r + A, :].astype(BF16) for r in range(16)]
    for t in range(8):
        y = dot(first, jnp.concatenate([waves[2 * t], waves[2 * t + 1]], axis=1))
        lines = []
        for k in range(2):
            both = y[:, 128 * k : 128 * k + 128]
            both = jnp.where(left, both[:128], both[128:])
            lines.append(both + swap(both))
        line = jnp.where(left, lines[0], lines[1])
        yr, yi = line[:A], line[A:]
        z = jnp.concatenate(
            [(yr * tc + yi * ts).astype(BF16), (yi * tc - yr * ts).astype(BF16)], axis=1
        )
        spec = dot(z, second)
        for k in range(2):
            r = 2 * t + k
            for q in range(2):
                start = (r >> 3) * 16 + q * 8 + (r & 7)
                buf[pl.ds(1024 + start, 32, stride=32), :] = spec[
                    32 * q : 32 * q + 32, 128 * k : 128 * k + 128
                ]
    for f in range(NB):
        out[f] = buf[1024 + 32 * f : 1056 + 32 * f, :].astype(BF16)


def tables(jx, band, fresnel, twist):
    lane = iota((KY, 128), 1)
    ky0 = A * (iota((KY, 128), 0) - LOW)
    b_row = iota((A, 128), 0)
    turn = sign()

    def step(k1, carry):
        fy = ky0 + k1
        for q in range(2):
            fx = ((2 * band + q + A * ((lane & 63) + jx) + N // 2) & (N - 1)) - N // 2
            total = fx * fx + fy * fy
            hs, hc = sincos_int(total, 2 * N)
            inside = total <= (N // 3) ** 2
            fresnel[q, k1, :KY, :] = jnp.where(inside, hc, 0.0)
            fresnel[q, k1, KY:, :] = jnp.where(inside, hs, 0.0) * turn
        ts, tc = sincos_int(b_row * k1, N)
        twist[k1, :A, :] = tc
        twist[k1, A:, :] = ts * turn
        return carry

    lax.fori_loop(0, A, step, 0, unroll=2)


def y_first(q, slab, out, buf, buf2):
    turn = sign()
    table = stacked(iota((A, A), 0) * iota((A, A), 1), 1.0 / A)
    for i in range(0, 8, 2):
        x = [buf[pl.ds(q * 8 + i + k, A, stride=16), :].astype(BF16) for k in range(2)]
        y = dot(table, jnp.concatenate(x, axis=1))
        for k in range(2):
            line = y[:, 128 * k : 128 * k + 128]
            line = line[:A] + swap(line[A:]) * turn
            ts, tc = sincos_int(iota((A, 128), 0) * (8 * slab + i + k), N)
            buf2[pl.ds(i + k, A, stride=8), :] = line * tc + swap(line) * (ts * turn)
    out[...] = buf2[0:512, :].astype(BF16)


def forward_table(jy):
    row = iota((KY, 128), 0)
    col = iota((KY, 128), 1)
    n2 = NS * (col >> 4) + (col & 7)
    c, s = table64(n2 * (row - LOW - jy))
    blocks = []
    for parity in range(2):
        keep = ((col >> 3) & 1) == parity
        blocks.append(jnp.where(keep, c, 0.0))
        blocks.append(jnp.where(keep, s, 0.0))
    return (jnp.concatenate(blocks, axis=0) * (1.0 / A)).astype(BF16)


def y_second(q, forward, cols, fresnel, twist, buf):
    turn = sign()
    c, s = table64(iota((A, KY), 0) * (iota((A, KY), 1) - LOW))
    back = jnp.concatenate([c, s], axis=0).astype(BF16)

    def step(pair, carry):
        at = pl.multiple_of(pair * 16, 16)
        x = jnp.concatenate([cols[q, p, pl.ds(at, 16), :] for p in range(NS)], axis=0)
        g = dot(forward, x)
        v = []
        for k in range(2):
            line = g[96 * k : 96 * k + KY] + swap(g[96 * k + KY : 96 * k + 96]) * turn
            hc, hs = fresnel[q, 2 * pair + k, :KY, :], fresnel[q, 2 * pair + k, KY:, :]
            v.append((line * hc + swap(line) * hs).astype(BF16))
        u = dot(back, jnp.concatenate(v, axis=1))
        for k in range(2):
            line = u[:, 128 * k : 128 * k + 128]
            line = line[:A] - swap(line[A:]) * turn
            tc, ts = twist[2 * pair + k, :A, :], twist[2 * pair + k, A:, :]
            buf[pl.ds(2 * pair + k, A, stride=A), :] = line * tc - swap(line) * ts
        return carry

    lax.fori_loop(0, A // 2, step, 0, unroll=4)


def spare_lanes(jx):
    return ((iota((1, 128), 1) - (22 - jx)) & 63) < SPARE


def y_third(q, half, jx, out, buf, buf2):
    turn = sign()
    row = iota((A, A), 0)
    table = stacked((2 * (row & 31) + (row >> 5)) * iota((A, A), 1), 1.0)
    gap = spare_lanes(jx)

    def step(g, carry):
        lines = []
        for k in range(2):
            at = pl.multiple_of((32 * half + 4 * g + 2 * k) * A, 128)
            z = buf[pl.ds(at, 128), :].astype(BF16)
            w = dot(table, jnp.concatenate([z[:A], z[A:]], axis=1))
            for m in range(2):
                line = w[:, 128 * m : 128 * m + 128]
                lines.append(line[:A] - swap(line[A:]) * turn)
        for m in range(3):
            line = jnp.where(gap, pltpu.roll(lines[3], 128 - SPARE * (m + 1), 1), lines[m])
            for h in range(2):
                buf2[pl.ds(16 * m + 8 * h + g, NB, stride=48), :] = line[32 * h : 32 * h + 32]
        return carry

    lax.fori_loop(0, 8, step, 0, unroll=2)

    def pack(f, carry):
        out[q, half, f] = buf2[pl.ds(pl.multiple_of(f * 48, 16), 48), :].astype(BF16)
        return carry

    lax.fori_loop(0, NB, pack, 0, unroll=4)


def inverse_table(jx):
    lane = iota((A, 128), 1)
    c, s = table64((iota((A, 128), 0) + jx) * (lane & 63))
    left = lane < A
    whole = jnp.concatenate([jnp.where(left, c, s), jnp.where(left, -s, c)], axis=0)
    gap = ((iota((128, 128), 0) - (22 - jx)) & 63) < SPARE
    whole = jnp.where(gap, 0.0, whole)
    zero = jnp.zeros((128, 128), F32)
    rows = []
    for m in range(3):
        fourth = jnp.where(gap, pltpu.roll(whole, 128 - SPARE * (m + 1), 0), 0.0)
        rows.append(
            jnp.concatenate([whole if k == m else zero for k in range(3)] + [fourth], axis=1)
        )
    return jnp.concatenate(rows, axis=0).astype(BF16)


def x_second(q, half, table, rows, buf):
    lane = iota((8, 128), 1)
    turn = sign()

    def step(group, carry):
        lhs = []
        for k in range(4):
            block = rows[q, half, 4 * group + k]
            lhs.append(jnp.concatenate([block[16 * m : 16 * m + 16] for m in range(3)], axis=1))
        u = dot(jnp.concatenate(lhs, axis=0), table)
        for k in range(4):
            k1 = 2 * (4 * group + k) + q
            ts, tc = sincos_int(k1 * (lane & 63), N)
            ts, tc = ts[:1] * turn, tc[:1]
            for m in range(4):
                line = u[16 * k : 16 * k + 16, 128 * m : 128 * m + 128]
                line = line * tc - swap(line) * ts
                for h in range(2):
                    start = (32 * half + m) * 128 + h * A + k1
                    buf[pl.ds(start, 8, stride=512), :] = line[8 * h : 8 * h + 8]
        return carry

    lax.fori_loop(0, 8, step, 0, unroll=2)


def tile_table(ids):
    col = iota((NB, 128), 1)
    ids = jnp.broadcast_to(ids, (NB, 128))
    c, s = table64((col & 63) * (ids & 63))
    keep = ((ids >> 6) & 1) == (col >> 6)
    return jnp.concatenate([jnp.where(keep, c, 0.0), jnp.where(keep, s, 0.0)], axis=0).astype(BF16)


def x_third(half, table, out, buf, buf2):
    turn = sign()

    def step(pair, carry):
        at = pl.multiple_of((32 * half + 2 * pair) * 128, 256)
        z = buf[pl.ds(at, 256), :].astype(BF16)
        o = dot(table, jnp.concatenate([z[:128], z[128:]], axis=1))
        for k in range(2):
            line = o[:, 128 * k : 128 * k + 128]
            buf2[pl.ds(2 * pair + k, NB, stride=32), :] = line[:32] - swap(line[32:]) * turn
        return carry

    lax.fori_loop(0, 16, step, 0, unroll=4)
    for p in range(NS):
        out[half, p] = buf2[128 * p : 128 * p + 128, :].astype(BF16)


def own_tiles(band, slab, tiles):
    found = []
    for l in range(4):
        ident = jnp.int32(0)
        for q in range(NS):
            for k in range(4):
                value = tiles[(4 * slab + l) * NS + q, k]
                ident = ident + jnp.where((value >> 7) == band, value, 0)
        found.append(ident)
    return found


def probe_factors(ids, beams, shifts):
    sub = iota((8, 128), 0)
    lane = iota((8, 128), 1)
    by = jnp.zeros((8, 128), jnp.int32)
    bx = jnp.zeros((8, 128), jnp.int32)
    ab = jnp.zeros((8, 128), F32)
    for j in range(8):
        by = jnp.where(sub == j, beams[j, 0], by)
        bx = jnp.where(sub == j, beams[j, 1], bx)
        ab = jnp.where(sub == j, shifts[j], ab)
    ry = jnp.zeros((8, 128), jnp.int32)
    rx = jnp.zeros((8, 128), jnp.int32)
    for l in range(4):
        for g in range(G):
            here = lane == l * G + g
            ry = jnp.where(here, (ids[l] >> 6) * A + A // 2 + g, ry)
            rx = jnp.where(here, (ids[l] & 63) * A + A // 2 + 2 * g, rx)
    m = (F * (by * ry + bx * rx)) & (N - 1)
    s, c = sincos(ab + 2.0 * math.pi / N * m.astype(F32))
    return c, -s


def split_tiles(pot, out):
    for h in range(2):
        for pair in range(32):
            out[32 * h + pair] = pot[A * h : A * h + A, 128 * pair : 128 * pair + 128]


def detect(ids, alpha, parts, pot, out, buf):
    left = iota((A, 128), 1) < A
    turn = sign()
    lane = iota((A, 128), 1)
    c, s = table64(iota((A, 128), 0) * (lane & 63))
    along_x = jnp.concatenate([jnp.where(left, c, -s), jnp.where(left, s, c)], axis=0)
    along_x = (along_x * (1.0 / A)).astype(BF16)
    along_y = stacked(iota((A, A), 0) * iota((A, A), 1), 1.0 / A)
    ky = iota((A, 128), 0)
    kx = iota((A, 128), 1) & 63
    ky = jnp.where(ky < 32, ky, ky - A)
    kx = jnp.where(kx < 32, kx, kx - A)
    radius = ky * ky + kx * kx
    counts = ring_counts()
    width = A // (2 * NDET)
    ones = jnp.ones((8, 128), F32)
    for l in range(4):
        ident = ids[l]
        tile = pot[((ident & 127) >> 1)].astype(F32)
        odd = (ident & 1) == 1
        tile = jnp.where(left != odd, tile, swap(tile))
        ps, pc = sincos(tile)
        ps = ps * turn
        fields = [
            jnp.concatenate(
                [parts[h, j, 32 * l : 32 * l + 32, :].astype(F32) for h in range(2)], axis=0
            )
            for j in range(8)
        ]
        swapped = [swap(f) * turn for f in fields]
        for g in range(G):
            probe = jnp.zeros((A, 128), F32)
            at = l * G + g
            for j in range(8):
                probe = (
                    probe
                    + fields[j] * alpha[0][j : j + 1, at : at + 1]
                    - swapped[j] * alpha[1][j : j + 1, at : at + 1]
                )
            probe = probe * pc - swap(probe) * ps
            d = dot(probe.astype(BF16), along_x).astype(BF16)
            w = dot(along_y, d)
            value = w[:A] + swap(w[A:]) * turn
            power = value * value
            for b in range(NDET):
                member = (radius >= (width * b) ** 2) & (radius < (width * (b + 1)) ** 2)
                part = jnp.where(member, power, 0.0) * (A * A / (8.0 * counts[b]))
                buf[g * NDET + b : g * NDET + b + 1, :] = jnp.sum(part, axis=0, keepdims=True)
        total = lax.dot_general(
            ones,
            buf[0:128, :],
            (((1,), (1,)), ((), ())),
            precision=lax.Precision.HIGHEST,
            preferred_element_type=F32,
        )
        out[l] = total[:1]


def kernel(
    beams,
    shifts,
    tiles_s,
    counts,
    tiles_v,
    pot1_hbm,
    pot2_hbm,
    out,
    pot1,
    pot2,
    buf,
    buf2,
    buf3,
    pairs,
    fresnel,
    twist,
    msg1,
    rows1,
    cols,
    msg2,
    rows2,
    msg3,
    parts,
    res,
    sums,
    load,
    send1,
    recv1,
    sendg,
    recvg,
    send2,
    recv2,
    send3,
    recv3,
    send4,
    recv4,
):
    band = lax.axis_index("beam")
    slab = lax.axis_index("slab")
    jy = beams[slab, 0]
    jx = beams[slab, 1]
    loads = [
        pltpu.make_async_copy(
            pot1_hbm.at[pl.ds(pl.multiple_of(A * h + 16 * (slab >> 1), 16), 16), :],
            pot1.at[h],
            load.at[h],
        )
        for h in range(2)
    ]
    loads.append(pltpu.make_async_copy(pot2_hbm, pot2, load.at[2]))
    for copy in loads:
        copy.start()
    barrier = pltpu.get_barrier_semaphore()

    def greet(target):
        pl.semaphore_signal(
            barrier, inc=1, device_id=target, device_id_type=pl.DeviceIdType.MESH
        )

    def greet_beam(k, carry):
        greet({"beam": (band + k) & (NB - 1), "slab": slab})
        return carry

    lax.fori_loop(1, NB, greet_beam, 0)

    def greet_slab(k, carry):
        greet({"beam": band, "slab": (slab + k) & (NS - 1)})
        return carry

    lax.fori_loop(1, NS, greet_slab, 0)
    home = band >> 2

    def greet_home(k, carry):
        greet({"beam": (band + k) & (NB - 1), "slab": home})
        return carry

    @pl.when(home != slab)
    def _():
        lax.fori_loop(1, NB, greet_home, 0)

    loads[0].wait()
    loads[1].wait()
    x_forward(slab, pot1, msg1, buf)
    extra = 4 * (NS - 1) - jnp.where(home == slab, NS - 1, 0)
    pl.semaphore_wait(barrier, NB - 1 + NS - 1 + extra)

    def exchange1(k):
        target = (band + k) & (NB - 1)
        return remote(
            msg1.at[target], rows1.at[band], send1.at[target], recv1.at[band],
            {"beam": target, "slab": slab},
        )

    def arrival1(k):
        source = (band + k) & (NB - 1)
        return remote(
            msg1.at[source], rows1.at[source], send1.at[source], recv1.at[source],
            {"beam": source, "slab": slab},
        )

    lax.fori_loop(1, NB, lambda k, c: (exchange1(k).start(), c)[1], 0)
    rows1[band] = msg1[band]
    tables(jx, band, fresnel, twist)
    loads[2].wait()
    split_tiles(pot2, pairs)
    wanted = tiles_v[...]
    wanted = jnp.where((wanted >> 7) == band, wanted, 0).reshape(NB, NS, 4)
    wanted = jnp.sum(jnp.sum(wanted, axis=1), axis=1, keepdims=True)
    tile_tab = tile_table(wanted)
    ids = own_tiles(band, slab, tiles_s)
    forward = forward_table(jy)
    inverse = inverse_table(jx)
    lax.fori_loop(1, NB, lambda k, c: (arrival1(k).wait_recv(), c)[1], 0)

    right = (slab + 2) & (NS - 1)
    left = (slab + 6) & (NS - 1)
    far = (slab + 4) & (NS - 1)
    partner = slab ^ 1

    def gather(source, q, half, kind, target):
        begin = 256 if half == 1 else 0
        length = 512 if half is None else 256
        view = cols.at[q, source, pl.ds(begin, length), :]
        return remote(
            view, view, sendg.at[kind, q], recvg.at[source, q, 1 if half == 1 else 0],
            {"beam": band, "slab": target},
        )

    for f in range(NB):
        buf[32 * f : 32 * f + 32, :] = rows1[f].astype(F32)
    for q in range(2):
        y_first(q, slab, cols.at[q, slab], buf, buf2)
        gather(slab, q, None, 0, right).start()
        gather(slab, q, None, 1, left).start()
        gather(slab, q, None, 2, partner).start()

    def near(q):
        gather(left, q, None, 0, left).wait_recv()
        gather(left, q, 0, 3, right).start()
        gather(left, q, None, 4, partner).start()
        gather(right, q, None, 1, right).wait_recv()
        gather(right, q, 1, 5, left).start()
        gather(right, q, None, 6, partner).start()

    def distant(q):
        gather(far, q, 0, 3, left).wait_recv()
        gather(far, q, 1, 5, right).wait_recv()
        gather(far, q, None, 7, partner).start()

    def across(q):
        for source in (partner, left ^ 1, right ^ 1, far ^ 1):
            gather(source, q, None, 2, partner).wait_recv()

    def exchange2(q, half, k):
        target = (band + k) & (NB - 1)
        return remote(
            msg2.at[q, half, target], rows2.at[q, half, band],
            send2.at[2 * q + half, target], recv2.at[2 * q + half, band],
            {"beam": target, "slab": slab},
        )

    def arrival2(q, half, k):
        source = (band + k) & (NB - 1)
        return remote(
            msg2.at[q, half, source], rows2.at[q, half, source],
            send2.at[2 * q + half, source], recv2.at[2 * q + half, source],
            {"beam": source, "slab": slab},
        )

    def send_rows(q, half):
        y_third(q, half, jx, msg2, buf, buf2)
        lax.fori_loop(1, NB, lambda k, z: (exchange2(q, half, k).start(), z)[1], 0)
        rows2[q, half, band] = msg2[q, half, band]

    near(0)
    distant(0)
    across(0)
    y_second(0, forward, cols, fresnel, twist, buf)
    near(1)
    send_rows(0, 0)
    distant(1)
    send_rows(0, 1)
    across(1)
    y_second(1, forward, cols, fresnel, twist, buf)
    send_rows(1, 0)
    send_rows(1, 1)

    def exchange3(half, k):
        target = (slab + k) & (NS - 1)
        return remote(
            msg3.at[half, target], parts.at[half, slab],
            send3.at[half, target], recv3.at[half, slab],
            {"beam": band, "slab": target},
        )

    def arrival3(half, k):
        source = (slab + k) & (NS - 1)
        return remote(
            msg3.at[half, source], parts.at[half, source],
            send3.at[half, source], recv3.at[half, source],
            {"beam": band, "slab": source},
        )

    alpha = probe_factors(ids, beams, shifts)
    for q in range(2):
        for half in range(2):
            lax.fori_loop(1, NB, lambda k, z: (arrival2(q, half, k).wait_recv(), z)[1], 0)
            x_second(q, half, inverse, rows2, buf3)
            if q == 1:
                x_third(half, tile_tab, msg3, buf3, buf2)
                lax.fori_loop(1, NS, lambda k, z: (exchange3(half, k).start(), z)[1], 0)
                parts[half, slab] = msg3[half, slab]
    for half in range(2):
        lax.fori_loop(1, NS, lambda k, z: (arrival3(half, k).wait_recv(), z)[1], 0)
    detect(ids, alpha, parts, pairs, res, buf)

    def exchange4(l, p):
        group = 4 * slab + l
        return remote(
            res.at[l], sums.at[band], send4.at[l, p], recv4.at[band],
            {"beam": group, "slab": p},
        )

    def arrival4(source):
        return remote(
            res.at[0], sums.at[source], send4.at[0, 0], recv4.at[source],
            {"beam": source, "slab": home},
        )

    def each4(act):
        for l in range(4):

            def body(p, carry):
                @pl.when((4 * slab + l != band) | (p != slab))
                def _():
                    act(exchange4(l, p))

                return carry

            lax.fori_loop(0, NS, body, 0)

    each4(lambda copy: copy.start())

    @pl.when(home == slab)
    def _():
        sums[band] = res[band & 3]

    def finish(source, carry):
        @pl.when((source != band) | (home != slab))
        def _():
            arrival4(source).wait_recv()

        return carry

    lax.fori_loop(0, NB, finish, 0)
    block = band * NS + slab
    for k in range(4):
        row = sums[tiles_s[block, k] >> 7]
        row = jnp.where(k < counts[block], row, 0.0)
        for g in range(G):
            out[0, k, g : g + 1, :] = row[:, NDET * g : NDET * g + NDET]

    lax.fori_loop(1, NB, lambda k, z: (exchange1(k).wait_send(), z)[1], 0)
    for q in range(2):
        gather(slab, q, None, 0, right).wait_send()
        gather(slab, q, None, 1, left).wait_send()
        gather(slab, q, None, 2, partner).wait_send()
        gather(left, q, 0, 3, right).wait_send()
        gather(left, q, None, 4, partner).wait_send()
        gather(right, q, 1, 5, left).wait_send()
        gather(right, q, None, 6, partner).wait_send()
        gather(far, q, None, 7, partner).wait_send()
        for half in range(2):
            lax.fori_loop(1, NB, lambda k, z: (exchange2(q, half, k).wait_send(), z)[1], 0)
    for half in range(2):
        lax.fori_loop(1, NS, lambda k, z: (exchange3(half, k).wait_send(), z)[1], 0)
    each4(lambda copy: copy.wait_send())


def shards(pot_first, pot_second, beam_index, aberration, tile_table, tile_count):
    args = (beam_index, aberration, tile_table, tile_count, tile_table, pot_first, pot_second)
    spaces = [pltpu.SMEM] * 4 + [pltpu.VMEM] + [pl.ANY] * 2
    dma = pltpu.SemaphoreType.DMA
    return pl.pallas_call(
        kernel,
        out_shape=jax.ShapeDtypeStruct((1, 4, G, NDET), F32),
        in_specs=[pl.BlockSpec(memory_space=space) for space in spaces],
        out_specs=pl.BlockSpec(memory_space=pltpu.VMEM),
        scratch_shapes=[
            pltpu.VMEM((2, 16, N), BF16),
            pltpu.VMEM((128, N), BF16),
            pltpu.VMEM((A * A, 128), F32),
            pltpu.VMEM((1536, 128), F32),
            pltpu.VMEM((A * 128, 128), F32),
            pltpu.VMEM((64, A, 128), BF16),
            pltpu.VMEM((2, A, 2 * KY, 128), F32),
            pltpu.VMEM((A, 128, 128), F32),
            pltpu.VMEM((NB, 32, 128), BF16),
            pltpu.VMEM((NB, 32, 128), BF16),
            pltpu.VMEM((2, NS, 512, 128), BF16),
            pltpu.VMEM((2, 2, NB, 48, 128), BF16),
            pltpu.VMEM((2, 2, NB, 48, 128), BF16),
            pltpu.VMEM((2, NS, 128, 128), BF16),
            pltpu.VMEM((2, NS, 128, 128), BF16),
            pltpu.VMEM((4, 1, 128), F32),
            pltpu.VMEM((NB, 1, 128), F32),
            dma((3,)),
            dma((NB,)),
            dma((NB,)),
            dma((8, 2)),
            dma((NS, 2, 2)),
            dma((4, NB)),
            dma((4, NB)),
            dma((2, NS)),
            dma((2, NS)),
            dma((4, NS)),
            dma((NB,)),
        ],
        compiler_params=pltpu.CompilerParams(
            vmem_limit_bytes=50 * 1024 * 1024, collective_id=0, has_side_effects=True
        ),
    )(*args)


def solution(mesh):
    return jax.shard_map(
        shards,
        mesh=mesh,
        in_specs=(P("beam", None), P("beam", None), P(), P(), P(), P()),
        out_specs=P(("beam", "slab"), None, None, None),
        check_vma=False,
    )
```

```python
import math

import jax
import jax.numpy as jnp
import numpy as np
from jax import lax
from jax.experimental import pallas as pl
from jax.experimental.pallas import tpu as pltpu
from jax.sharding import PartitionSpec as P

A = 64
N = 4096
F = 64
G = 3
NDET = 16
QMAX = 3
NB = 32
NS = 8
KY = 48
LOW = 24
SPARE = 20
F32 = jnp.float32
BF16 = jnp.bfloat16


def ring_counts():
    d = np.arange(A)
    signed = np.where(d < A // 2, d, d - A)
    radius = signed[:, None] ** 2 + signed[None, :] ** 2
    width = A // (2 * NDET)
    return [
        int(((radius >= (width * b) ** 2) & (radius < (width * (b + 1)) ** 2)).sum())
        for b in range(NDET)
    ]


def poly_sincos(r):
    t = r * r
    sine = r + r * t * (-1.6666667e-1 + t * (8.3333333e-3 + t * (-1.9841270e-4 + t * 2.7557319e-6)))
    cosine = 1.0 + t * (-0.5 + t * (4.1666667e-2 + t * (-1.3888889e-3 + t * 2.4801587e-5)))
    return sine, cosine


def place(sine, cosine, quadrant):
    swap = (quadrant & 1) == 1
    a = jnp.where(swap, cosine, sine)
    b = jnp.where(swap, sine, cosine)
    a = jnp.where((quadrant & 2) == 2, -a, a)
    b = jnp.where(((quadrant + 1) & 2) == 2, -b, b)
    return a, b


def sincos(x):
    k = jnp.floor(x * (2.0 / math.pi) + 0.5)
    r = (x - k * 1.5707963) - k * 2.6794897e-8
    sine, cosine = poly_sincos(r)
    return place(sine, cosine, k.astype(jnp.int32))


def sincos_int(m, period):
    shift = int(math.log2(period)) - 2
    quadrant = (m + (period >> 3)) >> shift
    r = (m - (quadrant << shift)).astype(F32) * (2.0 * math.pi / period)
    sine, cosine = poly_sincos(r)
    return place(sine, cosine, quadrant)


def dot(a, b):
    return jnp.dot(a, b, preferred_element_type=F32)


def iota(shape, axis):
    return lax.broadcasted_iota(jnp.int32, shape, axis)


def remote(src, dst, send, recv, target):
    return pltpu.make_async_remote_copy(
        src_ref=src,
        dst_ref=dst,
        send_sem=send,
        recv_sem=recv,
        device_id=target,
        device_id_type=pl.DeviceIdType.MESH,
    )


def swap(v):
    return pltpu.roll(v, A, 1)


def left_half():
    return iota((1, 128), 1) < A


def sign():
    return jnp.where(left_half(), 1.0, -1.0)


def table64(product):
    s, c = sincos_int(product & (A - 1), A)
    return c.astype(BF16).astype(F32), s.astype(BF16).astype(F32)


def stacked(product, scale):
    c, s = table64(product)
    return jnp.concatenate([c * scale, s * scale], axis=0).astype(BF16)


def x_tables():
    row = iota((128, 128), 0)
    col = iota((128, 128), 1)
    k1 = 2 * (row & 31) + ((row >> 5) & 1)
    blocks = []
    for rho in range(2):
        c, s = table64(k1 * (2 * (col & 31) + rho))
        same = (row >> 6) == ((col >> 5) & 1)
        blocks.append(jnp.where(same, c, jnp.where(row < A, s, -s)) * (1.0 / A))
    first = jnp.concatenate(blocks, axis=0)[:, :A].astype(BF16)
    lane = iota((A, 128), 1)
    c, s = table64(iota((A, 128), 0) * (lane & 63))
    left = lane < A
    zero = jnp.zeros((A, 128), F32)
    rows = []
    for block in (jnp.where(left, c, -s), jnp.where(left, s, c)):
        block = block * (1.0 / A)
        rows.append(jnp.concatenate([block, zero], axis=1))
        rows.append(jnp.concatenate([zero, block], axis=1))
    second = jnp.concatenate(rows, axis=0).astype(BF16)
    return first, second


def x_forward(slab, potential, out, buf):
    odd = (slab & 1) == 1
    for h in range(2):
        block = potential[h].astype(F32)
        block = jnp.where(odd, block[8:], block[:8])
        sine, cosine = sincos(block)
        for part, wave in enumerate((cosine, sine)):
            for p in range(32):
                start = h * 8 * A + part * 32 + p
                buf[pl.ds(start, 8, stride=A), :] = wave[:, 128 * p : 128 * p + 128]
    first, second = x_tables()
    row = iota((A, 128), 0)
    k1 = 2 * (row & 31) + (row >> 5)
    ts, tc = sincos_int(k1 * (iota((A, 128), 1) & 63), N)
    left = left_half()
    waves = [buf[A * r : A * r + A, :].astype(BF16) for r in range(16)]
    for t in range(8):
        y = dot(first, jnp.concatenate([waves[2 * t], waves[2 * t + 1]], axis=1))
        lines = []
        for k in range(2):
            both = y[:, 128 * k : 128 * k + 128]
            both = jnp.where(left, both[:128], both[128:])
            lines.append(both + swap(both))
        line = jnp.where(left, lines[0], lines[1])
        yr, yi = line[:A], line[A:]
        z = jnp.concatenate(
            [(yr * tc + yi * ts).astype(BF16), (yi * tc - yr * ts).astype(BF16)], axis=1
        )
        spec = dot(z, second)
        for k in range(2):
            r = 2 * t + k
            for q in range(2):
                buf[pl.ds(1024 + 512 * q + r, 32, stride=16), :] = spec[
                    32 * q : 32 * q + 32, 128 * k : 128 * k + 128
                ]
    for q in range(2):
        for f in range(NB):
            start = 1024 + 512 * q + 16 * f
            out[q, f] = buf[start : start + 16, :].astype(BF16)


def tables(jx, band, fresnel, twist):
    lane = iota((KY, 128), 1)
    ky0 = A * (iota((KY, 128), 0) - LOW)
    b_row = iota((A, 128), 0)

    def step(k1, carry):
        fy = ky0 + k1
        for q in range(2):
            fx = ((2 * band + q + A * ((lane & 63) + jx) + N // 2) & (N - 1)) - N // 2
            total = fx * fx + fy * fy
            hs, hc = sincos_int(total, 2 * N)
            inside = total <= (N // 3) ** 2
            fresnel[q, k1, :KY, :] = jnp.where(inside, hc, 0.0)
            fresnel[q, k1, KY:, :] = jnp.where(inside, hs, 0.0)
        ts, tc = sincos_int(b_row * k1, N)
        twist[k1, :A, :] = tc
        twist[k1, A:, :] = ts
        return carry

    lax.fori_loop(0, A, step, 0, unroll=2)


def y_first(slab, out, buf, buf2):
    turn = sign()
    table = stacked(iota((A, A), 0) * iota((A, A), 1), 1.0 / A)
    for i in range(0, 8, 2):
        x = [buf[pl.ds(i + k, A, stride=8), :].astype(BF16) for k in range(2)]
        y = dot(table, jnp.concatenate(x, axis=1))
        for k in range(2):
            line = y[:, 128 * k : 128 * k + 128]
            line = line[:A] + swap(line[A:]) * turn
            ts, tc = sincos_int(iota((A, 128), 0) * (8 * slab + i + k), N)
            buf2[pl.ds(i + k, A, stride=8), :] = line * tc + swap(line) * (ts * turn)
    out[...] = buf2[0:512, :].astype(BF16)


def forward_table(jy):
    row = iota((KY, 128), 0)
    col = iota((KY, 128), 1)
    n2 = NS * (col >> 4) + (col & 7)
    c, s = table64(n2 * (row - LOW - jy))
    blocks = []
    for parity in range(2):
        keep = ((col >> 3) & 1) == parity
        pc = jnp.where(keep, c, 0.0)
        ps = jnp.where(keep, s, 0.0)
        blocks.append(jnp.concatenate([pc, -ps], axis=1))
        blocks.append(jnp.concatenate([ps, pc], axis=1))
    return (jnp.concatenate(blocks, axis=0) * (1.0 / A)).astype(BF16)


def y_second(q, forward, cols, fresnel, twist, buf):
    turn = sign().astype(BF16)
    c, s = table64(iota((A, KY), 0) * (iota((A, KY), 1) - LOW))
    back = jnp.concatenate(
        [jnp.concatenate([c, s], axis=1), jnp.concatenate([-s, c], axis=1)], axis=0
    ).astype(BF16)

    def step(pair, carry):
        at = pl.multiple_of(pair * 16, 16)
        x = jnp.concatenate([cols[q, p, pl.ds(at, 16), :] for p in range(NS)], axis=0)
        g = dot(forward, jnp.concatenate([x, swap(x) * -turn], axis=0))
        v = []
        for k in range(2):
            line, turned = g[96 * k : 96 * k + KY], g[96 * k + KY : 96 * k + 96]
            hc, hs = fresnel[q, 2 * pair + k, :KY, :], fresnel[q, 2 * pair + k, KY:, :]
            both = [line * hc - turned * hs, turned * hc + line * hs]
            v.append(jnp.concatenate(both, axis=0).astype(BF16))
        u = dot(back, jnp.concatenate(v, axis=1))
        for k in range(2):
            line, turned = u[:A, 128 * k : 128 * k + 128], u[A:, 128 * k : 128 * k + 128]
            tc, ts = twist[2 * pair + k, :A, :], twist[2 * pair + k, A:, :]
            buf[pl.ds(2 * pair + k, A, stride=128), :] = line * tc + turned * ts
            buf[pl.ds(A + 2 * pair + k, A, stride=128), :] = turned * tc - line * ts
        return carry

    lax.fori_loop(0, A // 2, step, 0, unroll=4)


def spare_lanes(jx):
    return ((iota((1, 128), 1) - (22 - jx)) & 63) < SPARE


def y_third(q, half, jx, out, buf, buf2):
    row = iota((A, A), 0)
    c, s = table64((2 * (row & 31) + (row >> 5)) * iota((A, A), 1))
    table = jnp.concatenate([c, s], axis=1).astype(BF16)
    gap = spare_lanes(jx)

    def step(g, carry):
        lines = []
        for k in range(2):
            at = pl.multiple_of((32 * half + 4 * g + 2 * k) * 128, 256)
            z = buf[pl.ds(at, 256), :].astype(BF16)
            w = dot(table, jnp.concatenate([z[:128], z[128:]], axis=1))
            lines += [w[:, :128], w[:, 128:]]
        for m in range(3):
            line = jnp.where(gap, pltpu.roll(lines[3], 128 - SPARE * (m + 1), 1), lines[m])
            for h in range(2):
                buf2[pl.ds(16 * m + 8 * h + g, NB, stride=48), :] = line[32 * h : 32 * h + 32]
        return carry

    lax.fori_loop(0, 8, step, 0, unroll=2)

    def pack(f, carry):
        out[q, half, f] = buf2[pl.ds(pl.multiple_of(f * 48, 16), 48), :].astype(BF16)
        return carry

    lax.fori_loop(0, NB, pack, 0, unroll=4)


def inverse_table(jx):
    lane = iota((A, 128), 1)
    c, s = table64((iota((A, 128), 0) + jx) * (lane & 63))
    left = lane < A
    whole = jnp.concatenate([jnp.where(left, c, s), jnp.where(left, -s, c)], axis=0)
    gap = ((iota((128, 128), 0) - (22 - jx)) & 63) < SPARE
    whole = jnp.where(gap, 0.0, whole)
    zero = jnp.zeros((128, 128), F32)
    rows = []
    for m in range(3):
        fourth = jnp.where(gap, pltpu.roll(whole, 128 - SPARE * (m + 1), 0), 0.0)
        rows.append(
            jnp.concatenate([whole if k == m else zero for k in range(3)] + [fourth], axis=1)
        )
    return jnp.concatenate(rows, axis=0).astype(BF16)


def x_second(q, half, table, rows, buf):
    lane = iota((8, 128), 1)
    turn = sign()

    def step(group, carry):
        lhs = []
        for k in range(4):
            block = rows[q, half, 4 * group + k]
            lhs.append(jnp.concatenate([block[16 * m : 16 * m + 16] for m in range(3)], axis=1))
        u = dot(jnp.concatenate(lhs, axis=0), table)
        for k in range(4):
            k1 = 2 * (4 * group + k) + q
            ts, tc = sincos_int(k1 * (lane & 63), N)
            ts, tc = ts[:1] * turn, tc[:1]
            for m in range(4):
                line = u[16 * k : 16 * k + 16, 128 * m : 128 * m + 128]
                line = line * tc - swap(line) * ts
                for h in range(2):
                    start = (32 * half + m) * 128 + h * A + k1
                    buf[pl.ds(start, 8, stride=512), :] = line[8 * h : 8 * h + 8]
        return carry

    lax.fori_loop(0, 8, step, 0, unroll=2)


def tile_table(ids):
    col = iota((NB, 128), 1)
    ids = jnp.broadcast_to(ids, (NB, 128))
    c, s = table64((col & 63) * (ids & 63))
    keep = ((ids >> 6) & 1) == (col >> 6)
    return jnp.concatenate([jnp.where(keep, c, 0.0), jnp.where(keep, s, 0.0)], axis=0).astype(BF16)


def x_third(half, table, out, buf, buf2):
    turn = sign()

    def step(pair, carry):
        at = pl.multiple_of((32 * half + 2 * pair) * 128, 256)
        z = buf[pl.ds(at, 256), :].astype(BF16)
        o = dot(table, jnp.concatenate([z[:128], z[128:]], axis=1))
        for k in range(2):
            line = o[:, 128 * k : 128 * k + 128]
            buf2[pl.ds(2 * pair + k, NB, stride=32), :] = line[:32] - swap(line[32:]) * turn
        return carry

    lax.fori_loop(0, 16, step, 0, unroll=4)
    for p in range(NS):
        out[half, p] = buf2[128 * p : 128 * p + 128, :].astype(BF16)


def own_tiles(band, slab, tiles):
    found = jnp.sum(jnp.where((tiles >> 7) == band, tiles, 0), axis=0, keepdims=True)
    column = jnp.where((iota((NB, 256), 1) >> 3) == iota((NB, 256), 0), found, 0)
    column = jnp.sum(column, axis=1, keepdims=True)
    lane = iota((1, 256), 1)
    ids = [jnp.sum(jnp.where((lane >> 3) == 4 * slab + l, found, 0)) for l in range(4)]
    return column, ids


def probe_factors(ids, beams, shifts, out):
    row = iota((8 * 12, 128), 0)
    by = jnp.zeros_like(row)
    bx = jnp.zeros_like(row)
    ab = jnp.zeros(row.shape, F32)
    for j in range(8):
        here = (row >= 12 * j) & (row < 12 * j + 12)
        by = jnp.where(here, beams[0, j], by)
        bx = jnp.where(here, beams[1, j], bx)
        ab = jnp.where(here, shifts[j], ab)
    at = row - 12 * ((row * 43691) >> 19)
    slot = (at * 43691) >> 17
    g = at - 3 * slot
    ident = jnp.zeros_like(row)
    for l in range(4):
        ident = jnp.where(slot == l, ids[l], ident)
    ry = (ident >> 6) * A + A // 2 + g
    rx = (ident & 63) * A + A // 2 + 2 * g
    m = (F * (by * ry + bx * rx)) & (N - 1)
    s, c = sincos(ab + 2.0 * math.pi / N * m.astype(F32))
    out[0] = c
    out[1] = -s


def split_tiles(pot, out):
    for h in range(2):
        for pair in range(32):
            out[32 * h + pair] = pot[A * h : A * h + A, 128 * pair : 128 * pair + 128]


def ring_weights(out):
    ky = iota((32, 128), 0)
    kx = iota((32, 128), 1) & 63
    kx = jnp.where(kx < 32, kx, kx - A)
    radius = ky * ky + kx * kx
    counts = ring_counts()
    width = A // (2 * NDET)
    for b in range(NDET):
        member = (radius >= (width * b) ** 2) & (radius < (width * (b + 1)) ** 2)
        out[b] = jnp.where(member, A * A / (8.0 * counts[b]), 0.0)


def detect(ids, alpha, parts, pot, weights, out, buf):
    left = iota((A, 128), 1) < A
    turn = sign()
    lane = iota((A, 128), 1)
    c, s = table64(iota((A, 128), 0) * (lane & 63))
    along_x = jnp.concatenate(
        [
            jnp.concatenate([jnp.where(left, c, -s), jnp.where(left, s, c)], axis=1),
            jnp.concatenate([jnp.where(left, s, c), jnp.where(left, -c, s)], axis=1),
        ],
        axis=0,
    )
    along_x = (along_x * (1.0 / A)).astype(BF16)
    row = iota((A, A), 0)
    c, s = table64(jnp.where(row < 32, row, 32 - row) * iota((A, A), 1))
    along_y = jnp.concatenate([c, -s], axis=1) * (1.0 / A)
    along_y = jnp.where(iota((A, 128), 0) == 32, 0.0, along_y).astype(BF16)
    probes = []
    for l in range(4):
        ident = ids[l]
        tile = pot[((ident & 127) >> 1)].astype(F32)
        odd = (ident & 1) == 1
        tile = jnp.where(left != odd, tile, swap(tile))
        ps, pc = sincos(tile)
        ps = ps * turn
        sums = [jnp.zeros((A, 128), F32) for _ in range(2 * G)]
        for j in range(8):
            field = jnp.concatenate(
                [parts[h, j, 32 * l : 32 * l + 32, :].astype(F32) for h in range(2)], axis=0
            )
            for g in range(G):
                at = 12 * j + G * l + g
                sums[g] = sums[g] + field * alpha[0, at : at + 1, :]
                sums[G + g] = sums[G + g] + field * alpha[1, at : at + 1, :]
        for g in range(G):
            probe = sums[g] - swap(sums[G + g]) * turn
            probes.append((probe * pc - swap(probe) * ps).astype(BF16))
    d = dot(jnp.concatenate(probes, axis=0), along_x).astype(BF16)
    images = [d[A * n : A * n + A] for n in range(4 * G)]
    images = [jnp.concatenate([image[:, :128], image[:, 128:]], axis=0) for image in images]
    value = dot(along_y, jnp.concatenate(images, axis=1))
    for n in range(4 * G):
        image = value[:, 128 * n : 128 * n + 128]
        power = image * image
        power = power[:32] + power[32:]
        first = (n // G) * A + (n % G) * NDET
        for b in range(NDET):
            buf[first + b : first + b + 1, :] = jnp.sum(power * weights[b], axis=0, keepdims=True)
    total = lax.dot_general(
        jnp.ones((8, 128), F32),
        buf[0:256, :],
        (((1,), (1,)), ((), ())),
        precision=lax.Precision.HIGHEST,
        preferred_element_type=F32,
    )
    for l in range(4):
        block = total[:, 128 * (l // 2) : 128 * (l // 2) + 128]
        out[l] = (swap(block) if l % 2 else block)[:1]


def kernel(
    beams,
    shifts,
    counts,
    tiles,
    pot1_hbm,
    pot2_hbm,
    out,
    pot1,
    pot2,
    buf,
    buf2,
    buf3,
    pairs,
    fresnel,
    twist,
    msg1,
    rows1,
    cols,
    msg2,
    rows2,
    msg3,
    parts,
    alpha,
    weights,
    res,
    sums,
    load,
    send1,
    recv1,
    sendg,
    recvg,
    send2,
    recv2,
    send3,
    recv3,
    send4,
    recv4,
):
    band = lax.axis_index("beam")
    slab = lax.axis_index("slab")
    jy = beams[0, slab]
    jx = beams[1, slab]
    loads = [
        pltpu.make_async_copy(
            pot1_hbm.at[pl.ds(pl.multiple_of(A * h + 16 * (slab >> 1), 16), 16), :],
            pot1.at[h],
            load.at[h],
        )
        for h in range(2)
    ]
    loads.append(pltpu.make_async_copy(pot2_hbm, pot2, load.at[2]))
    for copy in loads:
        copy.start()
    barrier = pltpu.get_barrier_semaphore()

    def greet(target):
        pl.semaphore_signal(
            barrier, inc=1, device_id=target, device_id_type=pl.DeviceIdType.MESH
        )

    def greet_beam(k, carry):
        greet({"beam": (band + k) & (NB - 1), "slab": slab})
        return carry

    lax.fori_loop(1, NB, greet_beam, 0)

    def greet_slab(k, carry):
        greet({"beam": band, "slab": (slab + k) & (NS - 1)})
        return carry

    lax.fori_loop(1, NS, greet_slab, 0)
    home = band >> 2

    def greet_home(k, carry):
        greet({"beam": (band + k) & (NB - 1), "slab": home})
        return carry

    @pl.when(home != slab)
    def _():
        lax.fori_loop(1, NB, greet_home, 0)

    loads[0].wait()
    loads[1].wait()
    x_forward(slab, pot1, msg1, buf)
    extra = 4 * (NS - 1) - jnp.where(home == slab, NS - 1, 0)
    pl.semaphore_wait(barrier, NB - 1 + NS - 1 + extra)

    def exchange1(q, k):
        target = (band + k) & (NB - 1)
        return remote(
            msg1.at[q, target], rows1.at[q, band], send1.at[q], recv1.at[q],
            {"beam": target, "slab": slab},
        )

    def all_of(ref, sem):
        return pltpu.make_async_copy(ref, ref, sem)

    for q in range(2):
        lax.fori_loop(1, NB, lambda k, c: (exchange1(q, k).start(), c)[1], 0)
    for q in range(2):
        rows1[q, band] = msg1[q, band]
    tables(jx, band, fresnel, twist)
    loads[2].wait()
    split_tiles(pot2, pairs)
    wanted, ids = own_tiles(band, slab, tiles[...])
    tile_tab = tile_table(wanted)
    probe_factors(ids, beams, shifts, alpha)
    ring_weights(weights)
    forward = forward_table(jy)
    inverse = inverse_table(jx)

    right = (slab + 2) & (NS - 1)
    left = (slab + 6) & (NS - 1)
    far = (slab + 4) & (NS - 1)
    partner = slab ^ 1

    def gather(source, q, kind, target):
        view = cols.at[q, source]
        return remote(
            view, view, sendg.at[kind, q], recvg.at[source, q], {"beam": band, "slab": target}
        )

    for q in range(2):
        all_of(rows1.at[q, pl.ds(0, NB - 1)], recv1.at[q]).wait()
        for f in range(NB):
            buf[16 * f : 16 * f + 16, :] = rows1[q, f].astype(F32)
        y_first(slab, cols.at[q, slab], buf, buf2)
        for kind, target in enumerate((right, left, far, partner)):
            gather(slab, q, kind, target).start()

    def near(q):
        for kind, source in enumerate((left, right, far)):
            gather(source, q, 0, source).wait_recv()
            gather(source, q, 4 + kind, partner).start()

    def across(q):
        for source in (partner, left ^ 1, right ^ 1, far ^ 1):
            gather(source, q, 0, partner).wait_recv()

    def exchange2(q, half, k):
        target = (band + k) & (NB - 1)
        return remote(
            msg2.at[q, half, target], rows2.at[q, half, band],
            send2.at[2 * q + half], recv2.at[2 * q + half],
            {"beam": target, "slab": slab},
        )

    def send_rows(q, half):
        y_third(q, half, jx, msg2, buf, buf2)
        lax.fori_loop(1, NB, lambda k, z: (exchange2(q, half, k).start(), z)[1], 0)
        rows2[q, half, band] = msg2[q, half, band]

    near(0)
    across(0)
    y_second(0, forward, cols, fresnel, twist, buf)
    near(1)
    send_rows(0, 0)
    send_rows(0, 1)
    across(1)
    y_second(1, forward, cols, fresnel, twist, buf)
    send_rows(1, 0)
    send_rows(1, 1)

    def exchange3(half, k):
        target = (slab + k) & (NS - 1)
        return remote(
            msg3.at[half, target], parts.at[half, slab],
            send3.at[half], recv3.at[half],
            {"beam": band, "slab": target},
        )

    for q in range(2):
        for half in range(2):
            all_of(rows2.at[q, half, pl.ds(0, NB - 1)], recv2.at[2 * q + half]).wait()
            x_second(q, half, inverse, rows2, buf3)
            if q == 1:
                x_third(half, tile_tab, msg3, buf3, buf2)
                lax.fori_loop(1, NS, lambda k, z: (exchange3(half, k).start(), z)[1], 0)
                parts[half, slab] = msg3[half, slab]
    for half in range(2):
        all_of(parts.at[half, pl.ds(0, NS - 1)], recv3.at[half]).wait()
    detect(ids, alpha, parts, pairs, weights, res, buf)

    def exchange4(l, p):
        return remote(
            res.at[l], sums.at[band], send4.at[0], recv4.at[0],
            {"beam": 4 * slab + l, "slab": p},
        )

    for l in range(4):

        def body(p, carry):
            @pl.when((4 * slab + l != band) | (p != slab))
            def _():
                exchange4(l, p).start()

            return carry

        lax.fori_loop(0, NS, body, 0)

    @pl.when(home == slab)
    def _():
        sums[band] = res[band & 3]
        all_of(sums.at[pl.ds(0, NB - 1)], recv4.at[0]).wait()

    @pl.when(home != slab)
    def _():
        all_of(sums, recv4.at[0]).wait()

    block = band * NS + slab
    mine = jnp.where(iota((4, 256), 1) == block, tiles[...], 0)
    slot = iota((4, 256), 0)
    for k in range(4):
        row = sums[jnp.sum(jnp.where(slot == k, mine, 0)) >> 7]
        row = jnp.where(k < counts[block], row, 0.0)
        for g in range(G):
            out[0, g, k : k + 1, :] = row[:, NDET * g : NDET * g + NDET]

    for q in range(2):
        all_of(msg1.at[q, pl.ds(0, NB - 1)], send1.at[q]).wait()
        for kind in range(7):
            all_of(cols.at[q, 0], sendg.at[kind, q]).wait()
        for half in range(2):
            all_of(msg2.at[q, half, pl.ds(0, NB - 1)], send2.at[2 * q + half]).wait()
    for half in range(2):
        all_of(msg3.at[half, pl.ds(0, NS - 1)], send3.at[half]).wait()

    @pl.when(home == slab)
    def _():
        all_of(sums.at[pl.ds(0, NB - 1)], send4.at[0]).wait()

    @pl.when(home != slab)
    def _():
        all_of(sums, send4.at[0]).wait()


def shards(pot_first, pot_second, beam_index, aberration, tile_table, tile_count):
    args = (beam_index.T, aberration, tile_count, tile_table.T, pot_first, pot_second)
    spaces = [pltpu.SMEM] * 3 + [pltpu.VMEM] + [pltpu.HBM] * 2
    dma = pltpu.SemaphoreType.DMA
    sums = pl.pallas_call(
        kernel,
        out_shape=jax.ShapeDtypeStruct((1, G, 4, NDET), F32),
        in_specs=[pl.BlockSpec(memory_space=space) for space in spaces],
        out_specs=pl.BlockSpec(memory_space=pltpu.VMEM),
        scratch_shapes=[
            pltpu.VMEM((2, 16, N), BF16),
            pltpu.VMEM((128, N), BF16),
            pltpu.VMEM((A * 128, 128), F32),
            pltpu.VMEM((1536, 128), F32),
            pltpu.VMEM((A * 128, 128), F32),
            pltpu.VMEM((64, A, 128), BF16),
            pltpu.VMEM((2, A, 2 * KY, 128), F32),
            pltpu.VMEM((A, 128, 128), F32),
            pltpu.VMEM((2, NB, 16, 128), BF16),
            pltpu.VMEM((2, NB, 16, 128), BF16),
            pltpu.VMEM((2, NS, 512, 128), BF16),
            pltpu.VMEM((2, 2, NB, 48, 128), BF16),
            pltpu.VMEM((2, 2, NB, 48, 128), BF16),
            pltpu.VMEM((2, NS, 128, 128), BF16),
            pltpu.VMEM((2, NS, 128, 128), BF16),
            pltpu.VMEM((2, 96, 128), F32),
            pltpu.VMEM((NDET, 32, 128), F32),
            pltpu.VMEM((4, 1, 128), F32),
            pltpu.VMEM((NB, 1, 128), F32),
            dma((3,)),
            dma((2,)),
            dma((2,)),
            dma((7, 2)),
            dma((NS, 2)),
            dma((4,)),
            dma((4,)),
            dma((2,)),
            dma((2,)),
            dma((1,)),
            dma((1,)),
        ],
        compiler_params=pltpu.CompilerParams(
            vmem_limit_bytes=50 * 1024 * 1024, collective_id=0, has_side_effects=True
        ),
    )(*args)
    return sums.transpose(0, 2, 1, 3)


def solution(mesh):
    return jax.shard_map(
        shards,
        mesh=mesh,
        in_specs=(P("beam", None), P("beam", None), P(), P(), P(), P()),
        out_specs=P(("beam", "slab"), None, None, None),
        check_vma=False,
    )
```

```python
import math

import jax
import jax.numpy as jnp
import numpy as np
from jax import lax
from jax.experimental import pallas as pl
from jax.experimental.pallas import tpu as pltpu
from jax.sharding import PartitionSpec as P

A = 64
N = 4096
F = 64
G = 3
NDET = 16
QMAX = 3
NB = 32
NS = 8
KY = 48
LOW = 24
SPARE = 20
F32 = jnp.float32
BF16 = jnp.bfloat16


def ring_counts():
    d = np.arange(A)
    signed = np.where(d < A // 2, d, d - A)
    radius = signed[:, None] ** 2 + signed[None, :] ** 2
    width = A // (2 * NDET)
    return [
        int(((radius >= (width * b) ** 2) & (radius < (width * (b + 1)) ** 2)).sum())
        for b in range(NDET)
    ]


def poly_sincos(r):
    t = r * r
    sine = r + r * t * (-1.6666667e-1 + t * (8.3333333e-3 + t * (-1.9841270e-4 + t * 2.7557319e-6)))
    cosine = 1.0 + t * (-0.5 + t * (4.1666667e-2 + t * (-1.3888889e-3 + t * 2.4801587e-5)))
    return sine, cosine


def place(sine, cosine, quadrant):
    swap = (quadrant & 1) == 1
    a = jnp.where(swap, cosine, sine)
    b = jnp.where(swap, sine, cosine)
    a = jnp.where((quadrant & 2) == 2, -a, a)
    b = jnp.where(((quadrant + 1) & 2) == 2, -b, b)
    return a, b


def sincos(x):
    k = jnp.floor(x * (2.0 / math.pi) + 0.5)
    r = (x - k * 1.5707963) - k * 2.6794897e-8
    sine, cosine = poly_sincos(r)
    return place(sine, cosine, k.astype(jnp.int32))


def sincos_int(m, period):
    shift = int(math.log2(period)) - 2
    quadrant = (m + (period >> 3)) >> shift
    r = (m - (quadrant << shift)).astype(F32) * (2.0 * math.pi / period)
    sine, cosine = poly_sincos(r)
    return place(sine, cosine, quadrant)


def dot(a, b):
    return jnp.dot(a, b, preferred_element_type=F32)


def iota(shape, axis):
    return lax.broadcasted_iota(jnp.int32, shape, axis)


def remote(src, dst, send, recv, target):
    return pltpu.make_async_remote_copy(
        src_ref=src,
        dst_ref=dst,
        send_sem=send,
        recv_sem=recv,
        device_id=target,
        device_id_type=pl.DeviceIdType.MESH,
    )


def swap(v):
    return pltpu.roll(v, A, 1)


def left_half():
    return iota((1, 128), 1) < A


def sign():
    return jnp.where(left_half(), 1.0, -1.0)


def table64(product):
    s, c = sincos_int(product & (A - 1), A)
    return c.astype(BF16).astype(F32), s.astype(BF16).astype(F32)


def stacked(product, scale):
    c, s = table64(product)
    return jnp.concatenate([c * scale, s * scale], axis=0).astype(BF16)


def x_tables():
    row = iota((128, 128), 0)
    col = iota((128, 128), 1)
    k1 = 2 * (row & 31) + ((row >> 5) & 1)
    blocks = []
    for rho in range(2):
        c, s = table64(k1 * (2 * (col & 31) + rho))
        same = (row >> 6) == ((col >> 5) & 1)
        blocks.append(jnp.where(same, c, jnp.where(row < A, s, -s)) * (1.0 / A))
    first = jnp.concatenate(blocks, axis=0)[:, :A].astype(BF16)
    lane = iota((A, 128), 1)
    c, s = table64(iota((A, 128), 0) * (lane & 63))
    left = lane < A
    zero = jnp.zeros((A, 128), F32)
    rows = []
    for block in (jnp.where(left, c, -s), jnp.where(left, s, c)):
        block = block * (1.0 / A)
        rows.append(jnp.concatenate([block, zero], axis=1))
        rows.append(jnp.concatenate([zero, block], axis=1))
    second = jnp.concatenate(rows, axis=0).astype(BF16)
    return first, second


def x_forward(slab, potential, out, buf):
    odd = (slab & 1) == 1
    for h in range(2):
        block = potential[h].astype(F32)
        block = jnp.where(odd, block[8:], block[:8])
        sine, cosine = sincos(block)
        for part, wave in enumerate((cosine, sine)):
            for p in range(32):
                start = h * 8 * A + part * 32 + p
                buf[pl.ds(start, 8, stride=A), :] = wave[:, 128 * p : 128 * p + 128]
    first, second = x_tables()
    row = iota((A, 128), 0)
    k1 = 2 * (row & 31) + (row >> 5)
    ts, tc = sincos_int(k1 * (iota((A, 128), 1) & 63), N)
    left = left_half()
    waves = [buf[A * r : A * r + A, :].astype(BF16) for r in range(16)]
    for t in range(8):
        y = dot(first, jnp.concatenate([waves[2 * t], waves[2 * t + 1]], axis=1))
        lines = []
        for k in range(2):
            both = y[:, 128 * k : 128 * k + 128]
            both = jnp.where(left, both[:128], both[128:])
            lines.append(both + swap(both))
        line = jnp.where(left, lines[0], lines[1])
        yr, yi = line[:A], line[A:]
        z = jnp.concatenate(
            [(yr * tc + yi * ts).astype(BF16), (yi * tc - yr * ts).astype(BF16)], axis=1
        )
        spec = dot(z, second)
        for k in range(2):
            r = 2 * t + k
            for q in range(2):
                buf[pl.ds(1024 + 512 * q + r, 32, stride=16), :] = spec[
                    32 * q : 32 * q + 32, 128 * k : 128 * k + 128
                ]
    for q in range(2):
        for f in range(NB):
            start = 1024 + 512 * q + 16 * f
            out[q, f] = buf[start : start + 16, :].astype(BF16)


def tables(jx, band, fresnel, twist):
    lane = iota((KY, 128), 1)
    ky0 = A * (iota((KY, 128), 0) - LOW)
    b_row = iota((A, 128), 0)

    def step(k1, carry):
        fy = ky0 + k1
        for q in range(2):
            fx = ((2 * band + q + A * ((lane & 63) + jx) + N // 2) & (N - 1)) - N // 2
            total = fx * fx + fy * fy
            hs, hc = sincos_int(total, 2 * N)
            inside = total <= (N // 3) ** 2
            fresnel[q, k1, :KY, :] = jnp.where(inside, hc, 0.0)
            fresnel[q, k1, KY:, :] = jnp.where(inside, hs, 0.0)
        ts, tc = sincos_int(b_row * k1, N)
        twist[k1, :A, :] = tc
        twist[k1, A:, :] = ts
        return carry

    lax.fori_loop(0, A, step, 0, unroll=2)


def y_first(slab, out, buf, buf2):
    turn = sign()
    table = stacked(iota((A, A), 0) * iota((A, A), 1), 1.0 / A)
    for i in range(0, 8, 2):
        x = [buf[pl.ds(i + k, A, stride=8), :].astype(BF16) for k in range(2)]
        y = dot(table, jnp.concatenate(x, axis=1))
        for k in range(2):
            line = y[:, 128 * k : 128 * k + 128]
            line = line[:A] + swap(line[A:]) * turn
            ts, tc = sincos_int(iota((A, 128), 0) * (8 * slab + i + k), N)
            buf2[pl.ds(i + k, A, stride=8), :] = line * tc + swap(line) * (ts * turn)
    out[...] = buf2[0:512, :].astype(BF16)


def forward_table(jy):
    row = iota((KY, 128), 0)
    col = iota((KY, 128), 1)
    n2 = NS * (col >> 4) + (col & 7)
    c, s = table64(n2 * (row - LOW - jy))
    blocks = []
    for parity in range(2):
        keep = ((col >> 3) & 1) == parity
        pc = jnp.where(keep, c, 0.0)
        ps = jnp.where(keep, s, 0.0)
        blocks.append(jnp.concatenate([pc, -ps], axis=1))
        blocks.append(jnp.concatenate([ps, pc], axis=1))
    return (jnp.concatenate(blocks, axis=0) * (1.0 / A)).astype(BF16)


def y_second(q, forward, cols, fresnel, twist, buf):
    turn = sign().astype(BF16)
    c, s = table64(iota((A, KY), 0) * (iota((A, KY), 1) - LOW))
    back = jnp.concatenate(
        [jnp.concatenate([c, s], axis=1), jnp.concatenate([-s, c], axis=1)], axis=0
    ).astype(BF16)

    def step(group, carry):
        wide = []
        for m in range(8):
            at = pl.multiple_of(group * 128 + 16 * m, 16)
            x = jnp.concatenate([cols[q, p, pl.ds(at, 16), :] for p in range(NS)], axis=0)
            wide.append(jnp.concatenate([x, swap(x) * -turn], axis=0))
        wide = dot(forward, jnp.concatenate(wide, axis=1))
        v = []
        for k in range(16):
            g = wide[96 * (k % 2) : 96 * (k % 2) + 96, 128 * (k // 2) : 128 * (k // 2) + 128]
            line, turned = g[:KY], g[KY:]
            k1 = 16 * group + k
            hc, hs = fresnel[q, k1, :KY, :], fresnel[q, k1, KY:, :]
            both = [line * hc - turned * hs, turned * hc + line * hs]
            v.append(jnp.concatenate(both, axis=0).astype(BF16))
        u = dot(back, jnp.concatenate(v, axis=1))
        for k in range(16):
            line, turned = u[:A, 128 * k : 128 * k + 128], u[A:, 128 * k : 128 * k + 128]
            k1 = 16 * group + k
            tc, ts = twist[k1, :A, :], twist[k1, A:, :]
            buf[pl.ds(k1, A, stride=128), :] = line * tc + turned * ts
            buf[pl.ds(A + k1, A, stride=128), :] = turned * tc - line * ts
        return carry

    lax.fori_loop(0, 4, step, 0, unroll=2)


def spare_lanes(jx):
    return ((iota((1, 128), 1) - (22 - jx)) & 63) < SPARE


def y_third(q, half, jx, out, buf, buf2):
    row = iota((A, A), 0)
    c, s = table64((2 * (row & 31) + (row >> 5)) * iota((A, A), 1))
    table = jnp.concatenate([c, s], axis=1).astype(BF16)
    gap = spare_lanes(jx)

    z = []
    for b in range(32):
        at = (32 * half + b) * 128
        z.append(buf[at : at + 128, :].astype(BF16))
    w = dot(table, jnp.concatenate(z, axis=1))
    for g in range(8):
        lines = [w[:, 128 * (4 * g + m) : 128 * (4 * g + m) + 128] for m in range(4)]
        for m in range(3):
            line = jnp.where(gap, pltpu.roll(lines[3], 128 - SPARE * (m + 1), 1), lines[m])
            for h in range(2):
                buf2[pl.ds(16 * m + 8 * h + g, NB, stride=48), :] = line[32 * h : 32 * h + 32]

    def pack(f, carry):
        out[q, half, f] = buf2[pl.ds(pl.multiple_of(f * 48, 16), 48), :].astype(BF16)
        return carry

    lax.fori_loop(0, NB, pack, 0, unroll=4)


def inverse_table(jx):
    lane = iota((A, 128), 1)
    c, s = table64((iota((A, 128), 0) + jx) * (lane & 63))
    left = lane < A
    whole = jnp.concatenate([jnp.where(left, c, s), jnp.where(left, -s, c)], axis=0)
    gap = ((iota((128, 128), 0) - (22 - jx)) & 63) < SPARE
    whole = jnp.where(gap, 0.0, whole)
    zero = jnp.zeros((128, 128), F32)
    rows = []
    for m in range(3):
        fourth = jnp.where(gap, pltpu.roll(whole, 128 - SPARE * (m + 1), 0), 0.0)
        rows.append(
            jnp.concatenate([whole if k == m else zero for k in range(3)] + [fourth], axis=1)
        )
    return jnp.concatenate(rows, axis=0).astype(BF16)


def x_second(q, half, table, rows, buf):
    lane = iota((8, 128), 1)
    turn = sign()

    lhs = []
    for f in range(NB):
        block = rows[q, half, f]
        lhs.append(jnp.concatenate([block[16 * m : 16 * m + 16] for m in range(3)], axis=1))
    u = dot(jnp.concatenate(lhs, axis=0), table)
    for f in range(NB):
        k1 = 2 * f + q
        ts, tc = sincos_int(k1 * (lane & 63), N)
        ts, tc = ts[:1] * turn, tc[:1]
        for m in range(4):
            line = u[16 * f : 16 * f + 16, 128 * m : 128 * m + 128]
            line = line * tc - swap(line) * ts
            for h in range(2):
                start = (32 * half + m) * 128 + h * A + k1
                buf[pl.ds(start, 8, stride=512), :] = line[8 * h : 8 * h + 8]


def tile_table(ids):
    col = iota((NB, 128), 1)
    ids = jnp.broadcast_to(ids, (NB, 128))
    c, s = table64((col & 63) * (ids & 63))
    keep = ((ids >> 6) & 1) == (col >> 6)
    return jnp.concatenate([jnp.where(keep, c, 0.0), jnp.where(keep, s, 0.0)], axis=0).astype(BF16)


def x_third(half, table, out, buf, buf2):
    turn = sign()

    z = []
    for y in range(32):
        at = (32 * half + y) * 128
        z.append(buf[at : at + 128, :].astype(BF16))
    o = dot(table, jnp.concatenate(z, axis=1))
    for y in range(32):
        line = o[:, 128 * y : 128 * y + 128]
        buf2[pl.ds(y, NB, stride=32), :] = line[:32] - swap(line[32:]) * turn
    for p in range(NS):
        out[half, p] = buf2[128 * p : 128 * p + 128, :].astype(BF16)


def own_tiles(band, slab, tiles):
    found = jnp.sum(jnp.where((tiles >> 7) == band, tiles, 0), axis=0, keepdims=True)
    column = jnp.where((iota((NB, 256), 1) >> 3) == iota((NB, 256), 0), found, 0)
    column = jnp.sum(column, axis=1, keepdims=True)
    lane = iota((1, 256), 1)
    ids = [jnp.sum(jnp.where((lane >> 3) == 4 * slab + l, found, 0)) for l in range(4)]
    return column, ids


def probe_factors(ids, beams, shifts, out):
    row = iota((8 * 12, 128), 0)
    by = jnp.zeros_like(row)
    bx = jnp.zeros_like(row)
    ab = jnp.zeros(row.shape, F32)
    for j in range(8):
        here = (row >= 12 * j) & (row < 12 * j + 12)
        by = jnp.where(here, beams[0, j], by)
        bx = jnp.where(here, beams[1, j], bx)
        ab = jnp.where(here, shifts[j], ab)
    at = row - 12 * ((row * 43691) >> 19)
    slot = (at * 43691) >> 17
    g = at - 3 * slot
    ident = jnp.zeros_like(row)
    for l in range(4):
        ident = jnp.where(slot == l, ids[l], ident)
    ry = (ident >> 6) * A + A // 2 + g
    rx = (ident & 63) * A + A // 2 + 2 * g
    m = (F * (by * ry + bx * rx)) & (N - 1)
    s, c = sincos(ab + 2.0 * math.pi / N * m.astype(F32))
    out[0] = c
    out[1] = -s


def split_tiles(pot, out):
    for h in range(2):
        for pair in range(32):
            out[32 * h + pair] = pot[A * h : A * h + A, 128 * pair : 128 * pair + 128]


def ring_weights(out):
    ky = iota((32, 128), 0)
    kx = iota((32, 128), 1) & 63
    kx = jnp.where(kx < 32, kx, kx - A)
    radius = ky * ky + kx * kx
    counts = ring_counts()
    width = A // (2 * NDET)
    for b in range(NDET):
        member = (radius >= (width * b) ** 2) & (radius < (width * (b + 1)) ** 2)
        out[b] = jnp.where(member, A * A / (8.0 * counts[b]), 0.0)


def detect(ids, alpha, parts, pot, weights, out, buf):
    left = iota((A, 128), 1) < A
    turn = sign()
    lane = iota((A, 128), 1)
    c, s = table64(iota((A, 128), 0) * (lane & 63))
    along_x = jnp.concatenate(
        [
            jnp.concatenate([jnp.where(left, c, -s), jnp.where(left, s, c)], axis=1),
            jnp.concatenate([jnp.where(left, s, c), jnp.where(left, -c, s)], axis=1),
        ],
        axis=0,
    )
    along_x = (along_x * (1.0 / A)).astype(BF16)
    row = iota((A, A), 0)
    c, s = table64(jnp.where(row < 32, row, 32 - row) * iota((A, A), 1))
    along_y = jnp.concatenate([c, -s], axis=1) * (1.0 / A)
    along_y = jnp.where(iota((A, 128), 0) == 32, 0.0, along_y).astype(BF16)
    probes = []
    for l in range(4):
        ident = ids[l]
        tile = pot[((ident & 127) >> 1)].astype(F32)
        odd = (ident & 1) == 1
        tile = jnp.where(left != odd, tile, swap(tile))
        ps, pc = sincos(tile)
        ps = ps * turn
        sums = [jnp.zeros((A, 128), F32) for _ in range(2 * G)]
        for j in range(8):
            field = jnp.concatenate(
                [parts[h, j, 32 * l : 32 * l + 32, :].astype(F32) for h in range(2)], axis=0
            )
            for g in range(G):
                at = 12 * j + G * l + g
                sums[g] = sums[g] + field * alpha[0, at : at + 1, :]
                sums[G + g] = sums[G + g] + field * alpha[1, at : at + 1, :]
        for g in range(G):
            probe = sums[g] - swap(sums[G + g]) * turn
            probes.append((probe * pc - swap(probe) * ps).astype(BF16))
    d = dot(jnp.concatenate(probes, axis=0), along_x).astype(BF16)
    images = [d[A * n : A * n + A] for n in range(4 * G)]
    images = [jnp.concatenate([image[:, :128], image[:, 128:]], axis=0) for image in images]
    value = dot(along_y, jnp.concatenate(images, axis=1))
    for n in range(4 * G):
        image = value[:, 128 * n : 128 * n + 128]
        power = image * image
        power = power[:32] + power[32:]
        first = (n // G) * A + (n % G) * NDET
        for b in range(NDET):
            buf[first + b : first + b + 1, :] = jnp.sum(power * weights[b], axis=0, keepdims=True)
    total = lax.dot_general(
        jnp.ones((8, 128), F32),
        buf[0:256, :],
        (((1,), (1,)), ((), ())),
        precision=lax.Precision.HIGHEST,
        preferred_element_type=F32,
    )
    for l in range(4):
        block = total[:, 128 * (l // 2) : 128 * (l // 2) + 128]
        out[l] = (swap(block) if l % 2 else block)[:1]


def kernel(
    beams,
    shifts,
    counts,
    tiles,
    pot1_hbm,
    pot2_hbm,
    out,
    pot1,
    pot2,
    buf,
    buf2,
    buf3,
    pairs,
    fresnel,
    twist,
    msg1,
    rows1,
    cols,
    msg2,
    rows2,
    msg3,
    parts,
    alpha,
    weights,
    res,
    sums,
    load,
    send1,
    recv1,
    sendg,
    recvg,
    send2,
    recv2,
    send3,
    recv3,
    send4,
    recv4,
):
    band = lax.axis_index("beam")
    slab = lax.axis_index("slab")
    jy = beams[0, slab]
    jx = beams[1, slab]
    loads = [
        pltpu.make_async_copy(
            pot1_hbm.at[pl.ds(pl.multiple_of(A * h + 16 * (slab >> 1), 16), 16), :],
            pot1.at[h],
            load.at[h],
        )
        for h in range(2)
    ]
    loads.append(pltpu.make_async_copy(pot2_hbm, pot2, load.at[2]))
    for copy in loads:
        copy.start()
    barrier = pltpu.get_barrier_semaphore()

    def greet(target):
        pl.semaphore_signal(
            barrier, inc=1, device_id=target, device_id_type=pl.DeviceIdType.MESH
        )

    def greet_beam(k, carry):
        greet({"beam": (band + k) & (NB - 1), "slab": slab})
        return carry

    lax.fori_loop(1, NB, greet_beam, 0)

    def greet_slab(k, carry):
        greet({"beam": band, "slab": (slab + k) & (NS - 1)})
        return carry

    lax.fori_loop(1, NS, greet_slab, 0)
    home = band >> 2

    def greet_home(k, carry):
        greet({"beam": (band + k) & (NB - 1), "slab": home})
        return carry

    @pl.when(home != slab)
    def _():
        lax.fori_loop(1, NB, greet_home, 0)

    loads[0].wait()
    loads[1].wait()
    x_forward(slab, pot1, msg1, buf)
    extra = 4 * (NS - 1) - jnp.where(home == slab, NS - 1, 0)
    pl.semaphore_wait(barrier, NB - 1 + NS - 1 + extra)

    def exchange1(q, k):
        target = (band + k) & (NB - 1)
        return remote(
            msg1.at[q, target], rows1.at[q, band], send1.at[q], recv1.at[q],
            {"beam": target, "slab": slab},
        )

    def all_of(ref, sem):
        return pltpu.make_async_copy(ref, ref, sem)

    for q in range(2):
        lax.fori_loop(1, NB, lambda k, c: (exchange1(q, k).start(), c)[1], 0)
    for q in range(2):
        rows1[q, band] = msg1[q, band]
    tables(jx, band, fresnel, twist)
    loads[2].wait()
    split_tiles(pot2, pairs)
    wanted, ids = own_tiles(band, slab, tiles[...])
    tile_tab = tile_table(wanted)
    probe_factors(ids, beams, shifts, alpha)
    ring_weights(weights)
    forward = forward_table(jy)
    inverse = inverse_table(jx)

    right = (slab + 2) & (NS - 1)
    left = (slab + 6) & (NS - 1)
    far = (slab + 4) & (NS - 1)
    partner = slab ^ 1

    def gather(source, q, kind, target):
        view = cols.at[q, source]
        return remote(
            view, view, sendg.at[kind, q], recvg.at[source, q], {"beam": band, "slab": target}
        )

    def first(q):
        all_of(rows1.at[q, pl.ds(0, NB - 1)], recv1.at[q]).wait()
        for f in range(NB):
            buf[16 * f : 16 * f + 16, :] = rows1[q, f].astype(F32)
        y_first(slab, cols.at[q, slab], buf, buf2)

    def spread(q):
        for kind, target in enumerate((far, left, right, partner)):
            gather(slab, q, kind, target).start()

    def near(q):
        for kind, source in enumerate((left, right, far)):
            gather(source, q, 0, source).wait_recv()
            gather(source, q, 4 + kind, partner).start()

    def across(q):
        for source in (partner, left ^ 1, right ^ 1, far ^ 1):
            gather(source, q, 0, partner).wait_recv()

    def exchange2(q, half, k):
        target = (band + k) & (NB - 1)
        return remote(
            msg2.at[q, half, target], rows2.at[q, half, band],
            send2.at[2 * q + half], recv2.at[2 * q + half],
            {"beam": target, "slab": slab},
        )

    def send_rows(q, half):
        y_third(q, half, jx, msg2, buf, buf2)
        lax.fori_loop(1, NB, lambda k, z: (exchange2(q, half, k).start(), z)[1], 0)
        rows2[q, half, band] = msg2[q, half, band]

    first(0)
    spread(0)
    first(1)
    near(0)
    spread(1)
    across(0)
    y_second(0, forward, cols, fresnel, twist, buf)
    near(1)
    send_rows(0, 0)
    send_rows(0, 1)
    across(1)
    y_second(1, forward, cols, fresnel, twist, buf)
    send_rows(1, 0)
    send_rows(1, 1)

    def exchange3(half, k):
        target = (slab + k) & (NS - 1)
        return remote(
            msg3.at[half, target], parts.at[half, slab],
            send3.at[half], recv3.at[half],
            {"beam": band, "slab": target},
        )

    for q in range(2):
        for half in range(2):
            all_of(rows2.at[q, half, pl.ds(0, NB - 1)], recv2.at[2 * q + half]).wait()
            x_second(q, half, inverse, rows2, buf3)
            if q == 1:
                x_third(half, tile_tab, msg3, buf3, buf2)
                lax.fori_loop(1, NS, lambda k, z: (exchange3(half, k).start(), z)[1], 0)
                parts[half, slab] = msg3[half, slab]
    for half in range(2):
        all_of(parts.at[half, pl.ds(0, NS - 1)], recv3.at[half]).wait()
    detect(ids, alpha, parts, pairs, weights, res, buf)

    def exchange4(l, p):
        return remote(
            res.at[l], sums.at[band], send4.at[0], recv4.at[0],
            {"beam": 4 * slab + l, "slab": p},
        )

    for l in range(4):

        def body(p, carry):
            @pl.when((4 * slab + l != band) | (p != slab))
            def _():
                exchange4(l, p).start()

            return carry

        lax.fori_loop(0, NS, body, 0)

    @pl.when(home == slab)
    def _():
        sums[band] = res[band & 3]
        all_of(sums.at[pl.ds(0, NB - 1)], recv4.at[0]).wait()

    @pl.when(home != slab)
    def _():
        all_of(sums, recv4.at[0]).wait()

    block = band * NS + slab
    mine = jnp.where(iota((4, 256), 1) == block, tiles[...], 0)
    slot = iota((4, 256), 0)
    for k in range(4):
        row = sums[jnp.sum(jnp.where(slot == k, mine, 0)) >> 7]
        row = jnp.where(k < counts[block], row, 0.0)
        for g in range(G):
            out[0, g, k : k + 1, :] = row[:, NDET * g : NDET * g + NDET]

    for q in range(2):
        all_of(msg1.at[q, pl.ds(0, NB - 1)], send1.at[q]).wait()
        for kind in range(7):
            all_of(cols.at[q, 0], sendg.at[kind, q]).wait()
        for half in range(2):
            all_of(msg2.at[q, half, pl.ds(0, NB - 1)], send2.at[2 * q + half]).wait()
    for half in range(2):
        all_of(msg3.at[half, pl.ds(0, NS - 1)], send3.at[half]).wait()

    @pl.when(home == slab)
    def _():
        all_of(sums.at[pl.ds(0, NB - 1)], send4.at[0]).wait()

    @pl.when(home != slab)
    def _():
        all_of(sums, send4.at[0]).wait()


def shards(pot_first, pot_second, beam_index, aberration, tile_table, tile_count):
    args = (beam_index.T, aberration, tile_count, tile_table.T, pot_first, pot_second)
    spaces = [pltpu.SMEM] * 3 + [pltpu.VMEM] + [pltpu.HBM] * 2
    dma = pltpu.SemaphoreType.DMA
    sums = pl.pallas_call(
        kernel,
        out_shape=jax.ShapeDtypeStruct((1, G, 4, NDET), F32),
        in_specs=[pl.BlockSpec(memory_space=space) for space in spaces],
        out_specs=pl.BlockSpec(memory_space=pltpu.VMEM),
        scratch_shapes=[
            pltpu.VMEM((2, 16, N), BF16),
            pltpu.VMEM((128, N), BF16),
            pltpu.VMEM((A * 128, 128), F32),
            pltpu.VMEM((1536, 128), F32),
            pltpu.VMEM((A * 128, 128), F32),
            pltpu.VMEM((64, A, 128), BF16),
            pltpu.VMEM((2, A, 2 * KY, 128), F32),
            pltpu.VMEM((A, 128, 128), F32),
            pltpu.VMEM((2, NB, 16, 128), BF16),
            pltpu.VMEM((2, NB, 16, 128), BF16),
            pltpu.VMEM((2, NS, 512, 128), BF16),
            pltpu.VMEM((2, 2, NB, 48, 128), BF16),
            pltpu.VMEM((2, 2, NB, 48, 128), BF16),
            pltpu.VMEM((2, NS, 128, 128), BF16),
            pltpu.VMEM((2, NS, 128, 128), BF16),
            pltpu.VMEM((2, 96, 128), F32),
            pltpu.VMEM((NDET, 32, 128), F32),
            pltpu.VMEM((4, 1, 128), F32),
            pltpu.VMEM((NB, 1, 128), F32),
            dma((3,)),
            dma((2,)),
            dma((2,)),
            dma((7, 2)),
            dma((NS, 2)),
            dma((4,)),
            dma((4,)),
            dma((2,)),
            dma((2,)),
            dma((1,)),
            dma((1,)),
        ],
        compiler_params=pltpu.CompilerParams(
            vmem_limit_bytes=50 * 1024 * 1024, collective_id=0, has_side_effects=True
        ),
    )(*args)
    return sums.transpose(0, 2, 1, 3)


def solution(mesh):
    return jax.shard_map(
        shards,
        mesh=mesh,
        in_specs=(P("beam", None), P("beam", None), P(), P(), P(), P()),
        out_specs=P(("beam", "slab"), None, None, None),
        check_vma=False,
    )
```

```python
import math

import jax
import jax.numpy as jnp
import numpy as np
from jax import lax
from jax.experimental import pallas as pl
from jax.experimental.pallas import tpu as pltpu
from jax.sharding import PartitionSpec as P

A = 64
N = 4096
F = 64
G = 3
NDET = 16
QMAX = 3
NB = 32
NS = 8
KY = 48
LOW = 24
SPARE = 20
F32 = jnp.float32
BF16 = jnp.bfloat16


def ring_counts():
    d = np.arange(A)
    signed = np.where(d < A // 2, d, d - A)
    radius = signed[:, None] ** 2 + signed[None, :] ** 2
    width = A // (2 * NDET)
    return [
        int(((radius >= (width * b) ** 2) & (radius < (width * (b + 1)) ** 2)).sum())
        for b in range(NDET)
    ]


def poly_sincos(r):
    t = r * r
    sine = r + r * t * (-1.6666667e-1 + t * (8.3333333e-3 + t * (-1.9841270e-4 + t * 2.7557319e-6)))
    cosine = 1.0 + t * (-0.5 + t * (4.1666667e-2 + t * (-1.3888889e-3 + t * 2.4801587e-5)))
    return sine, cosine


def place(sine, cosine, quadrant):
    swap = (quadrant & 1) == 1
    a = jnp.where(swap, cosine, sine)
    b = jnp.where(swap, sine, cosine)
    a = jnp.where((quadrant & 2) == 2, -a, a)
    b = jnp.where(((quadrant + 1) & 2) == 2, -b, b)
    return a, b


def sincos(x):
    k = jnp.floor(x * (2.0 / math.pi) + 0.5)
    r = (x - k * 1.5707963) - k * 2.6794897e-8
    sine, cosine = poly_sincos(r)
    return place(sine, cosine, k.astype(jnp.int32))


def sincos_int(m, period):
    shift = int(math.log2(period)) - 2
    quadrant = (m + (period >> 3)) >> shift
    r = (m - (quadrant << shift)).astype(F32) * (2.0 * math.pi / period)
    sine, cosine = poly_sincos(r)
    return place(sine, cosine, quadrant)


def dot(a, b):
    return jnp.dot(a, b, preferred_element_type=F32)


def iota(shape, axis):
    return lax.broadcasted_iota(jnp.int32, shape, axis)


def remote(src, dst, send, recv, target):
    return pltpu.make_async_remote_copy(
        src_ref=src,
        dst_ref=dst,
        send_sem=send,
        recv_sem=recv,
        device_id=target,
        device_id_type=pl.DeviceIdType.MESH,
    )


def swap(v):
    return pltpu.roll(v, A, 1)


def left_half():
    return iota((1, 128), 1) < A


def sign():
    return jnp.where(left_half(), 1.0, -1.0)


def table64(product):
    s, c = sincos_int(product & (A - 1), A)
    return c.astype(BF16).astype(F32), s.astype(BF16).astype(F32)


def stacked(product, scale):
    c, s = table64(product)
    return jnp.concatenate([c * scale, s * scale], axis=0).astype(BF16)


def x_tables():
    row = iota((128, 128), 0)
    col = iota((128, 128), 1)
    k1 = 2 * (row & 31) + ((row >> 5) & 1)
    blocks = []
    for rho in range(2):
        c, s = table64(k1 * (2 * (col & 31) + rho))
        same = (row >> 6) == ((col >> 5) & 1)
        blocks.append(jnp.where(same, c, jnp.where(row < A, s, -s)) * (1.0 / A))
    first = jnp.concatenate(blocks, axis=0)[:, :A].astype(BF16)
    lane = iota((A, 128), 1)
    c, s = table64(iota((A, 128), 0) * (lane & 63))
    left = lane < A
    zero = jnp.zeros((A, 128), F32)
    rows = []
    for block in (jnp.where(left, c, -s), jnp.where(left, s, c)):
        block = block * (1.0 / A)
        rows.append(jnp.concatenate([block, zero], axis=1))
        rows.append(jnp.concatenate([zero, block], axis=1))
    second = jnp.concatenate(rows, axis=0).astype(BF16)
    return first, second


def x_forward(slab, loads, potential, out, buf):
    first, second = x_tables()
    row = iota((A, 128), 0)
    k1 = 2 * (row & 31) + (row >> 5)
    ts, tc = sincos_int(k1 * (iota((A, 128), 1) & 63), N)
    left = left_half()
    odd = (slab & 1) == 1
    for h in range(2):
        loads[h].wait()
        block = potential[h].astype(F32)
        block = jnp.where(odd, block[8:], block[:8])
        sine, cosine = sincos(block)
        for part, wave in enumerate((cosine, sine)):
            for p in range(32):
                start = h * 8 * A + part * 32 + p
                buf[pl.ds(start, 8, stride=A), :] = wave[:, 128 * p : 128 * p + 128]
    waves = [buf[A * r : A * r + A, :].astype(BF16) for r in range(16)]
    y = dot(first, jnp.concatenate(waves, axis=1))
    lines = []
    for r in range(16):
        both = y[:, 128 * r : 128 * r + 128]
        both = jnp.where(left, both[:128], both[128:])
        lines.append(both + swap(both))
    pairs = []
    for t in range(8):
        line = jnp.where(left, lines[2 * t], lines[2 * t + 1])
        yr, yi = line[:A], line[A:]
        both = [(yr * tc + yi * ts).astype(BF16), (yi * tc - yr * ts).astype(BF16)]
        pairs.append(jnp.concatenate(both, axis=1))
    spec = dot(jnp.concatenate(pairs, axis=0), second)
    for r in range(16):
        for q in range(2):
            start = A * (r >> 1) + 32 * q
            buf[pl.ds(1024 + 512 * q + r, 32, stride=16), :] = spec[
                start : start + 32, 128 * (r & 1) : 128 * (r & 1) + 128
            ]
    for q in range(2):
        for f in range(NB):
            start = 1024 + 512 * q + 16 * f
            out[q, f] = buf[start : start + 16, :].astype(BF16)


def tables(jx, band, fresnel, twist):
    lane = iota((KY, 128), 1)
    ky0 = A * (iota((KY, 128), 0) - LOW)
    b_row = iota((A, 128), 0)

    def step(k1, carry):
        fy = ky0 + k1
        for q in range(2):
            fx = ((2 * band + q + A * ((lane & 63) + jx) + N // 2) & (N - 1)) - N // 2
            total = fx * fx + fy * fy
            hs, hc = sincos_int(total, 2 * N)
            inside = total <= (N // 3) ** 2
            fresnel[q, k1, :KY, :] = jnp.where(inside, hc, 0.0)
            fresnel[q, k1, KY:, :] = jnp.where(inside, hs, 0.0)
        ts, tc = sincos_int(b_row * k1, N)
        twist[k1, :A, :] = tc
        twist[k1, A:, :] = ts
        return carry

    lax.fori_loop(0, A, step, 0, unroll=2)


def y_first(slab, out, buf, buf2):
    turn = sign()
    table = stacked(iota((A, A), 0) * iota((A, A), 1), 1.0 / A)
    for i in range(0, 8, 2):
        x = [buf[pl.ds(i + k, A, stride=8), :].astype(BF16) for k in range(2)]
        y = dot(table, jnp.concatenate(x, axis=1))
        for k in range(2):
            line = y[:, 128 * k : 128 * k + 128]
            line = line[:A] + swap(line[A:]) * turn
            ts, tc = sincos_int(iota((A, 128), 0) * (8 * slab + i + k), N)
            buf2[pl.ds(i + k, A, stride=8), :] = line * tc + swap(line) * (ts * turn)
    out[...] = buf2[0:512, :].astype(BF16)


def forward_table(jy):
    row = iota((KY, 128), 0)
    col = iota((KY, 128), 1)
    n2 = NS * (col >> 4) + (col & 7)
    c, s = table64(n2 * (row - LOW - jy))
    blocks = []
    for parity in range(2):
        keep = ((col >> 3) & 1) == parity
        pc = jnp.where(keep, c, 0.0)
        ps = jnp.where(keep, s, 0.0)
        blocks.append(jnp.concatenate([pc, -ps], axis=1))
        blocks.append(jnp.concatenate([ps, pc], axis=1))
    return (jnp.concatenate(blocks, axis=0) * (1.0 / A)).astype(BF16)


def y_second(q, forward, cols, fresnel, twist, buf):
    turn = sign().astype(BF16)
    c, s = table64(iota((A, KY), 0) * (iota((A, KY), 1) - LOW))
    back = jnp.concatenate(
        [jnp.concatenate([c, s], axis=1), jnp.concatenate([-s, c], axis=1)], axis=0
    ).astype(BF16)

    def step(group, carry):
        wide = []
        for m in range(8):
            at = pl.multiple_of(group * 128 + 16 * m, 16)
            x = jnp.concatenate([cols[q, p, pl.ds(at, 16), :] for p in range(NS)], axis=0)
            wide.append(jnp.concatenate([x, swap(x) * -turn], axis=0))
        wide = dot(forward, jnp.concatenate(wide, axis=1))
        v = []
        for k in range(16):
            g = wide[96 * (k % 2) : 96 * (k % 2) + 96, 128 * (k // 2) : 128 * (k // 2) + 128]
            line, turned = g[:KY], g[KY:]
            k1 = 16 * group + k
            hc, hs = fresnel[q, k1, :KY, :], fresnel[q, k1, KY:, :]
            both = [line * hc - turned * hs, turned * hc + line * hs]
            v.append(jnp.concatenate(both, axis=0).astype(BF16))
        u = dot(back, jnp.concatenate(v, axis=1))
        for k in range(16):
            line, turned = u[:A, 128 * k : 128 * k + 128], u[A:, 128 * k : 128 * k + 128]
            k1 = 16 * group + k
            tc, ts = twist[k1, :A, :], twist[k1, A:, :]
            buf[pl.ds(k1, A, stride=128), :] = line * tc + turned * ts
            buf[pl.ds(A + k1, A, stride=128), :] = turned * tc - line * ts
        return carry

    lax.fori_loop(0, 4, step, 0, unroll=2)


def spare_lanes(jx):
    return ((iota((1, 128), 1) - (22 - jx)) & 63) < SPARE


def y_third(q, half, jx, out, buf, buf2):
    row = iota((A, A), 0)
    c, s = table64((2 * (row & 31) + (row >> 5)) * iota((A, A), 1))
    table = jnp.concatenate([c, s], axis=1).astype(BF16)
    gap = spare_lanes(jx)

    z = []
    for b in range(32):
        at = (32 * half + b) * 128
        z.append(buf[at : at + 128, :].astype(BF16))
    w = dot(table, jnp.concatenate(z, axis=1))
    for g in range(8):
        lines = [w[:, 128 * (4 * g + m) : 128 * (4 * g + m) + 128] for m in range(4)]
        for m in range(3):
            line = jnp.where(gap, pltpu.roll(lines[3], 128 - SPARE * (m + 1), 1), lines[m])
            for h in range(2):
                buf2[pl.ds(16 * m + 8 * h + g, NB, stride=48), :] = line[32 * h : 32 * h + 32]

    def pack(f, carry):
        out[q, half, f] = buf2[pl.ds(pl.multiple_of(f * 48, 16), 48), :].astype(BF16)
        return carry

    lax.fori_loop(0, NB, pack, 0, unroll=4)


def inverse_table(jx):
    lane = iota((A, 128), 1)
    c, s = table64((iota((A, 128), 0) + jx) * (lane & 63))
    left = lane < A
    whole = jnp.concatenate([jnp.where(left, c, s), jnp.where(left, -s, c)], axis=0)
    gap = ((iota((128, 128), 0) - (22 - jx)) & 63) < SPARE
    whole = jnp.where(gap, 0.0, whole)
    zero = jnp.zeros((128, 128), F32)
    rows = []
    for m in range(3):
        fourth = jnp.where(gap, pltpu.roll(whole, 128 - SPARE * (m + 1), 0), 0.0)
        rows.append(
            jnp.concatenate([whole if k == m else zero for k in range(3)] + [fourth], axis=1)
        )
    return jnp.concatenate(rows, axis=0).astype(BF16)


def x_second(q, half, table, rows, buf):
    lane = iota((8, 128), 1)
    turn = sign()

    lhs = []
    for f in range(NB):
        block = rows[q, half, f]
        lhs.append(jnp.concatenate([block[16 * m : 16 * m + 16] for m in range(3)], axis=1))
    u = dot(jnp.concatenate(lhs, axis=0), table)
    for f in range(NB):
        k1 = 2 * f + q
        ts, tc = sincos_int(k1 * (lane & 63), N)
        ts, tc = ts[:1] * turn, tc[:1]
        for m in range(4):
            line = u[16 * f : 16 * f + 16, 128 * m : 128 * m + 128]
            line = line * tc - swap(line) * ts
            for h in range(2):
                start = (32 * half + m) * 128 + h * A + k1
                buf[pl.ds(start, 8, stride=512), :] = line[8 * h : 8 * h + 8]


def tile_table(ids):
    col = iota((NB, 128), 1)
    ids = jnp.broadcast_to(ids, (NB, 128))
    c, s = table64((col & 63) * (ids & 63))
    keep = ((ids >> 6) & 1) == (col >> 6)
    return jnp.concatenate([jnp.where(keep, c, 0.0), jnp.where(keep, s, 0.0)], axis=0).astype(BF16)


def x_third(half, table, out, buf, buf2):
    turn = sign()

    z = []
    for y in range(32):
        at = (32 * half + y) * 128
        z.append(buf[at : at + 128, :].astype(BF16))
    o = dot(table, jnp.concatenate(z, axis=1))
    for y in range(32):
        line = o[:, 128 * y : 128 * y + 128]
        buf2[pl.ds(y, NB, stride=32), :] = line[:32] - swap(line[32:]) * turn
    for p in range(NS):
        out[half, p] = buf2[128 * p : 128 * p + 128, :].astype(BF16)


def own_tiles(band, slab, tiles):
    found = jnp.sum(jnp.where((tiles >> 7) == band, tiles, 0), axis=0, keepdims=True)
    column = jnp.where((iota((NB, 256), 1) >> 3) == iota((NB, 256), 0), found, 0)
    column = jnp.sum(column, axis=1, keepdims=True)
    lane = iota((1, 256), 1)
    ids = [jnp.sum(jnp.where((lane >> 3) == 4 * slab + l, found, 0)) for l in range(4)]
    return column, ids


def probe_factors(ids, beams, shifts, out):
    row = iota((8 * 12, 128), 0)
    by = jnp.zeros_like(row)
    bx = jnp.zeros_like(row)
    ab = jnp.zeros(row.shape, F32)
    for j in range(8):
        here = (row >= 12 * j) & (row < 12 * j + 12)
        by = jnp.where(here, beams[0, j], by)
        bx = jnp.where(here, beams[1, j], bx)
        ab = jnp.where(here, shifts[j], ab)
    at = row - 12 * ((row * 43691) >> 19)
    slot = (at * 43691) >> 17
    g = at - 3 * slot
    ident = jnp.zeros_like(row)
    for l in range(4):
        ident = jnp.where(slot == l, ids[l], ident)
    ry = (ident >> 6) * A + A // 2 + g
    rx = (ident & 63) * A + A // 2 + 2 * g
    m = (F * (by * ry + bx * rx)) & (N - 1)
    s, c = sincos(ab + 2.0 * math.pi / N * m.astype(F32))
    out[0] = c
    out[1] = -s


def split_tiles(pot, out):
    for h in range(2):
        for pair in range(32):
            out[32 * h + pair] = pot[A * h : A * h + A, 128 * pair : 128 * pair + 128]


def ring_weights(out):
    ky = iota((32, 128), 0)
    kx = iota((32, 128), 1) & 63
    kx = jnp.where(kx < 32, kx, kx - A)
    radius = ky * ky + kx * kx
    counts = ring_counts()
    width = A // (2 * NDET)
    for b in range(NDET):
        member = (radius >= (width * b) ** 2) & (radius < (width * (b + 1)) ** 2)
        out[b] = jnp.where(member, A * A / (8.0 * counts[b]), 0.0)


def phases(ids, pot, out):
    left = left_half()
    for l in range(4):
        tile = pot[((ids[l] & 127) >> 1)].astype(F32)
        odd = (ids[l] & 1) == 1
        tile = jnp.where(left != odd, tile, swap(tile))
        s, c = sincos(tile)
        out[l, 0] = c
        out[l, 1] = s * sign()


def probe_rows(half, alpha, parts, phase, out):
    turn = sign()
    for l in range(4):
        sums = [jnp.zeros((32, 128), F32) for _ in range(2 * G)]
        for j in range(8):
            field = parts[half, j, 32 * l : 32 * l + 32, :].astype(F32)
            for g in range(G):
                at = 12 * j + G * l + g
                sums[g] = sums[g] + field * alpha[0, at : at + 1, :]
                sums[G + g] = sums[G + g] + field * alpha[1, at : at + 1, :]
        pc = phase[l, 0, 32 * half : 32 * half + 32, :]
        ps = phase[l, 1, 32 * half : 32 * half + 32, :]
        for g in range(G):
            probe = sums[g] - swap(sums[G + g]) * turn
            at = (G * l + g) * A + 32 * half
            out[at : at + 32, :] = (probe * pc - swap(probe) * ps).astype(BF16)


def detector_tables():
    lane = iota((A, 128), 1)
    left = lane < A
    c, s = table64(iota((A, 128), 0) * (lane & 63))
    along_x = jnp.concatenate(
        [
            jnp.concatenate([jnp.where(left, c, -s), jnp.where(left, s, c)], axis=1),
            jnp.concatenate([jnp.where(left, s, c), jnp.where(left, -c, s)], axis=1),
        ],
        axis=0,
    )
    along_x = (along_x * (1.0 / A)).astype(BF16)
    row = iota((A, A), 0)
    c, s = table64(jnp.where(row < 32, row, 32 - row) * iota((A, A), 1))
    along_y = jnp.concatenate([c, -s], axis=1) * (1.0 / A)
    along_y = jnp.where(iota((A, 128), 0) == 32, 0.0, along_y).astype(BF16)
    return along_x, along_y


def detect(along_x, along_y, probes, weights, out, buf):
    d = dot(probes[...], along_x).astype(BF16)
    images = [d[A * n : A * n + A] for n in range(4 * G)]
    images = [jnp.concatenate([image[:, :128], image[:, 128:]], axis=0) for image in images]
    value = dot(along_y, jnp.concatenate(images, axis=1))
    for n in range(4 * G):
        image = value[:, 128 * n : 128 * n + 128]
        power = image * image
        power = power[:32] + power[32:]
        first = (n // G) * A + (n % G) * NDET
        for b in range(NDET):
            buf[first + b : first + b + 1, :] = jnp.sum(power * weights[b], axis=0, keepdims=True)
    total = lax.dot_general(
        jnp.ones((8, 128), F32),
        buf[0:256, :],
        (((1,), (1,)), ((), ())),
        precision=lax.Precision.HIGHEST,
        preferred_element_type=F32,
    )
    for l in range(4):
        block = total[:, 128 * (l // 2) : 128 * (l // 2) + 128]
        out[l] = (swap(block) if l % 2 else block)[:1]


def kernel(
    beams,
    shifts,
    counts,
    tiles,
    pot1_hbm,
    pot2_hbm,
    out,
    pot1,
    pot2,
    buf,
    buf2,
    buf3,
    pairs,
    fresnel,
    twist,
    msg1,
    rows1,
    cols,
    msg2,
    rows2,
    msg3,
    parts,
    alpha,
    weights,
    phase,
    probes,
    res,
    sums,
    load,
    send1,
    recv1,
    sendg,
    recvg,
    send2,
    recv2,
    send3,
    recv3,
    send4,
    recv4,
):
    band = lax.axis_index("beam")
    slab = lax.axis_index("slab")
    jy = beams[0, slab]
    jx = beams[1, slab]
    loads = [
        pltpu.make_async_copy(
            pot1_hbm.at[pl.ds(pl.multiple_of(A * h + 16 * (slab >> 1), 16), 16), :],
            pot1.at[h],
            load.at[h],
        )
        for h in range(2)
    ]
    loads.append(pltpu.make_async_copy(pot2_hbm, pot2, load.at[2]))
    for copy in loads:
        copy.start()
    barrier = pltpu.get_barrier_semaphore()

    def greet(target):
        pl.semaphore_signal(
            barrier, inc=1, device_id=target, device_id_type=pl.DeviceIdType.MESH
        )

    def greet_beam(k, carry):
        greet({"beam": (band + k) & (NB - 1), "slab": slab})
        return carry

    lax.fori_loop(1, NB, greet_beam, 0)

    def greet_slab(k, carry):
        greet({"beam": band, "slab": (slab + k) & (NS - 1)})
        return carry

    lax.fori_loop(1, NS, greet_slab, 0)
    home = band >> 2

    def greet_home(k, carry):
        greet({"beam": (band + k) & (NB - 1), "slab": home})
        return carry

    @pl.when(home != slab)
    def _():
        lax.fori_loop(1, NB, greet_home, 0)

    x_forward(slab, loads, pot1, msg1, buf)
    extra = 4 * (NS - 1) - jnp.where(home == slab, NS - 1, 0)
    pl.semaphore_wait(barrier, NB - 1 + NS - 1 + extra)

    def exchange1(q, k):
        target = (band + k) & (NB - 1)
        return remote(
            msg1.at[q, target], rows1.at[q, band], send1.at[q], recv1.at[q],
            {"beam": target, "slab": slab},
        )

    def all_of(ref, sem):
        return pltpu.make_async_copy(ref, ref, sem)

    for q in range(2):
        lax.fori_loop(1, NB, lambda k, c: (exchange1(q, k).start(), c)[1], 0)
    for q in range(2):
        rows1[q, band] = msg1[q, band]
    forward = forward_table(jy)

    right = (slab + 2) & (NS - 1)
    left = (slab + 6) & (NS - 1)
    far = (slab + 4) & (NS - 1)
    partner = slab ^ 1

    def gather(source, q, kind, target):
        view = cols.at[q, source]
        return remote(
            view, view, sendg.at[kind, q], recvg.at[source, q], {"beam": band, "slab": target}
        )

    def first(q):
        all_of(rows1.at[q, pl.ds(0, NB - 1)], recv1.at[q]).wait()
        for f in range(NB):
            buf[16 * f : 16 * f + 16, :] = rows1[q, f].astype(F32)
        y_first(slab, cols.at[q, slab], buf, buf2)

    def spread(q):
        for kind, target in enumerate((far, left, right, partner)):
            gather(slab, q, kind, target).start()

    def near(q):
        for kind, source in enumerate((left, right, far)):
            gather(source, q, 0, source).wait_recv()
            gather(source, q, 4 + kind, partner).start()

    def across(q):
        for source in (partner, left ^ 1, right ^ 1, far ^ 1):
            gather(source, q, 0, partner).wait_recv()

    def exchange2(q, half, k):
        target = (band + k) & (NB - 1)
        return remote(
            msg2.at[q, half, target], rows2.at[q, half, band],
            send2.at[2 * q + half], recv2.at[2 * q + half],
            {"beam": target, "slab": slab},
        )

    def send_rows(q, half):
        y_third(q, half, jx, msg2, buf, buf2)
        lax.fori_loop(1, NB, lambda k, z: (exchange2(q, half, k).start(), z)[1], 0)
        rows2[q, half, band] = msg2[q, half, band]

    first(0)
    spread(0)
    first(1)
    tables(jx, band, fresnel, twist)
    near(0)
    spread(1)
    across(0)
    y_second(0, forward, cols, fresnel, twist, buf)
    send_rows(0, 0)
    near(1)
    send_rows(0, 1)
    across(1)
    y_second(1, forward, cols, fresnel, twist, buf)
    send_rows(1, 0)
    send_rows(1, 1)
    loads[2].wait()
    split_tiles(pot2, pairs)
    wanted, ids = own_tiles(band, slab, tiles[...])
    tile_tab = tile_table(wanted)
    probe_factors(ids, beams, shifts, alpha)
    ring_weights(weights)
    phases(ids, pairs, phase)
    along_x, along_y = detector_tables()
    inverse = inverse_table(jx)
    block = band * NS + slab
    mine = jnp.where(iota((4, 256), 1) == block, tiles[...], 0)
    slot = iota((4, 256), 0)
    bands = [jnp.sum(jnp.where(slot == k, mine, 0)) >> 7 for k in range(4)]

    def exchange3(half, k):
        target = (slab + k) & (NS - 1)
        return remote(
            msg3.at[half, target], parts.at[half, slab],
            send3.at[half], recv3.at[half],
            {"beam": band, "slab": target},
        )

    for q in range(2):
        for half in range(2):
            all_of(rows2.at[q, half, pl.ds(0, NB - 1)], recv2.at[2 * q + half]).wait()
            x_second(q, half, inverse, rows2, buf3)
            if q == 1:
                x_third(half, tile_tab, msg3, buf3, buf2)
                for k in range(1, NS):
                    exchange3(half, k).start()
                parts[half, slab] = msg3[half, slab]
    for half in range(2):
        all_of(parts.at[half, pl.ds(0, NS - 1)], recv3.at[half]).wait()
        probe_rows(half, alpha, parts, phase, probes)
    detect(along_x, along_y, probes, weights, res, buf)

    def exchange4(l, p):
        return remote(
            res.at[l], sums.at[band], send4.at[0], recv4.at[0],
            {"beam": 4 * slab + l, "slab": p},
        )

    for l in range(4):
        for k in range(1, NS):
            exchange4(l, (slab + k) & (NS - 1)).start()

        @pl.when(4 * slab + l != band)
        def _():
            exchange4(l, slab).start()

    @pl.when(home == slab)
    def _():
        sums[band] = res[band & 3]
        all_of(sums.at[pl.ds(0, NB - 1)], recv4.at[0]).wait()

    @pl.when(home != slab)
    def _():
        all_of(sums, recv4.at[0]).wait()

    for k in range(4):
        row = sums[bands[k]]
        row = jnp.where(k < counts[block], row, 0.0)
        for g in range(G):
            out[0, g, k : k + 1, :] = row[:, NDET * g : NDET * g + NDET]

    for q in range(2):
        all_of(msg1.at[q, pl.ds(0, NB - 1)], send1.at[q]).wait()
        for kind in range(7):
            all_of(cols.at[q, 0], sendg.at[kind, q]).wait()
        for half in range(2):
            all_of(msg2.at[q, half, pl.ds(0, NB - 1)], send2.at[2 * q + half]).wait()
    for half in range(2):
        all_of(msg3.at[half, pl.ds(0, NS - 1)], send3.at[half]).wait()

    @pl.when(home == slab)
    def _():
        all_of(sums.at[pl.ds(0, NB - 1)], send4.at[0]).wait()

    @pl.when(home != slab)
    def _():
        all_of(sums, send4.at[0]).wait()


def shards(pot_first, pot_second, beam_index, aberration, tile_table, tile_count):
    args = (beam_index.T, aberration, tile_count, tile_table.T, pot_first, pot_second)
    spaces = [pltpu.SMEM] * 3 + [pltpu.VMEM] + [pltpu.HBM] * 2
    dma = pltpu.SemaphoreType.DMA
    sums = pl.pallas_call(
        kernel,
        out_shape=jax.ShapeDtypeStruct((1, G, 4, NDET), F32),
        in_specs=[pl.BlockSpec(memory_space=space) for space in spaces],
        out_specs=pl.BlockSpec(memory_space=pltpu.VMEM),
        scratch_shapes=[
            pltpu.VMEM((2, 16, N), BF16),
            pltpu.VMEM((128, N), BF16),
            pltpu.VMEM((A * 128, 128), F32),
            pltpu.VMEM((1536, 128), F32),
            pltpu.VMEM((A * 128, 128), F32),
            pltpu.VMEM((64, A, 128), BF16),
            pltpu.VMEM((2, A, 2 * KY, 128), F32),
            pltpu.VMEM((A, 128, 128), F32),
            pltpu.VMEM((2, NB, 16, 128), BF16),
            pltpu.VMEM((2, NB, 16, 128), BF16),
            pltpu.VMEM((2, NS, 512, 128), BF16),
            pltpu.VMEM((2, 2, NB, 48, 128), BF16),
            pltpu.VMEM((2, 2, NB, 48, 128), BF16),
            pltpu.VMEM((2, NS, 128, 128), BF16),
            pltpu.VMEM((2, NS, 128, 128), BF16),
            pltpu.VMEM((2, 96, 128), F32),
            pltpu.VMEM((NDET, 32, 128), F32),
            pltpu.VMEM((4, 2, A, 128), F32),
            pltpu.VMEM((4 * G * A, 128), BF16),
            pltpu.VMEM((4, 1, 128), F32),
            pltpu.VMEM((NB, 1, 128), F32),
            dma((3,)),
            dma((2,)),
            dma((2,)),
            dma((7, 2)),
            dma((NS, 2)),
            dma((4,)),
            dma((4,)),
            dma((2,)),
            dma((2,)),
            dma((1,)),
            dma((1,)),
        ],
        compiler_params=pltpu.CompilerParams(
            vmem_limit_bytes=64 * 1024 * 1024, collective_id=0, has_side_effects=True
        ),
    )(*args)
    return sums.transpose(0, 2, 1, 3)


def solution(mesh):
    return jax.shard_map(
        shards,
        mesh=mesh,
        in_specs=(P("beam", None), P("beam", None), P(), P(), P(), P()),
        out_specs=P(("beam", "slab"), None, None, None),
        check_vma=False,
    )
```

```python
import math

import jax
import jax.numpy as jnp
import numpy as np
from jax import lax
from jax.experimental import pallas as pl
from jax.experimental.pallas import tpu as pltpu
from jax.sharding import PartitionSpec as P

A = 64
N = 4096
F = 64
G = 3
NDET = 16
QMAX = 3
NB = 32
NS = 8
KY = 48
LOW = 24
SPARE = 20
F32 = jnp.float32
BF16 = jnp.bfloat16


def ring_counts():
    d = np.arange(A)
    signed = np.where(d < A // 2, d, d - A)
    radius = signed[:, None] ** 2 + signed[None, :] ** 2
    width = A // (2 * NDET)
    return [
        int(((radius >= (width * b) ** 2) & (radius < (width * (b + 1)) ** 2)).sum())
        for b in range(NDET)
    ]


def poly_sincos(r):
    t = r * r
    sine = r + r * t * (-1.6666667e-1 + t * (8.3333333e-3 + t * (-1.9841270e-4 + t * 2.7557319e-6)))
    cosine = 1.0 + t * (-0.5 + t * (4.1666667e-2 + t * (-1.3888889e-3 + t * 2.4801587e-5)))
    return sine, cosine


def place(sine, cosine, quadrant):
    swap = (quadrant & 1) == 1
    a = jnp.where(swap, cosine, sine)
    b = jnp.where(swap, sine, cosine)
    a = jnp.where((quadrant & 2) == 2, -a, a)
    b = jnp.where(((quadrant + 1) & 2) == 2, -b, b)
    return a, b


def sincos(x):
    k = jnp.floor(x * (2.0 / math.pi) + 0.5)
    r = (x - k * 1.5707963) - k * 2.6794897e-8
    sine, cosine = poly_sincos(r)
    return place(sine, cosine, k.astype(jnp.int32))


def sincos_int(m, period):
    shift = int(math.log2(period)) - 2
    quadrant = (m + (period >> 3)) >> shift
    r = (m - (quadrant << shift)).astype(F32) * (2.0 * math.pi / period)
    sine, cosine = poly_sincos(r)
    return place(sine, cosine, quadrant)


def dot(a, b):
    return jnp.dot(a, b, preferred_element_type=F32)


def iota(shape, axis):
    return lax.broadcasted_iota(jnp.int32, shape, axis)


def remote(src, dst, send, recv, target):
    return pltpu.make_async_remote_copy(
        src_ref=src,
        dst_ref=dst,
        send_sem=send,
        recv_sem=recv,
        device_id=target,
        device_id_type=pl.DeviceIdType.MESH,
    )


def swap(v):
    return pltpu.roll(v, A, 1)


def left_half():
    return iota((1, 128), 1) < A


def sign():
    return jnp.where(left_half(), 1.0, -1.0)


def table64(product):
    s, c = sincos_int(product & (A - 1), A)
    return c.astype(BF16).astype(F32), s.astype(BF16).astype(F32)


def stacked(product, scale):
    c, s = table64(product)
    return jnp.concatenate([c * scale, s * scale], axis=0).astype(BF16)


def x_tables():
    row = iota((128, 128), 0)
    col = iota((128, 128), 1)
    k1 = 2 * (row & 31) + ((row >> 5) & 1)
    blocks = []
    for rho in range(2):
        c, s = table64(k1 * (2 * (col & 31) + rho))
        same = (row >> 6) == ((col >> 5) & 1)
        blocks.append(jnp.where(same, c, jnp.where(row < A, s, -s)) * (1.0 / A))
    first = jnp.concatenate(blocks, axis=0)[:, :A].astype(BF16)
    lane = iota((A, 128), 1)
    c, s = table64(iota((A, 128), 0) * (lane & 63))
    left = lane < A
    zero = jnp.zeros((A, 128), F32)
    rows = []
    for block in (jnp.where(left, c, -s), jnp.where(left, s, c)):
        block = block * (1.0 / A)
        rows.append(jnp.concatenate([block, zero], axis=1))
        rows.append(jnp.concatenate([zero, block], axis=1))
    second = jnp.concatenate(rows, axis=0).astype(BF16)
    return first, second


def x_forward(slab, loads, potential, out, buf):
    first, second = x_tables()
    row = iota((A, 128), 0)
    k1 = 2 * (row & 31) + (row >> 5)
    ts, tc = sincos_int(k1 * (iota((A, 128), 1) & 63), N)
    left = left_half()
    odd = (slab & 1) == 1
    for h in range(2):
        loads[h].wait()
        block = potential[h].astype(F32)
        block = jnp.where(odd, block[8:], block[:8])
        sine, cosine = sincos(block)
        for part, wave in enumerate((cosine, sine)):
            for p in range(32):
                start = h * 8 * A + part * 32 + p
                buf[pl.ds(start, 8, stride=A), :] = wave[:, 128 * p : 128 * p + 128]
    waves = [buf[A * r : A * r + A, :].astype(BF16) for r in range(16)]
    y = dot(first, jnp.concatenate(waves, axis=1))
    lines = []
    for r in range(16):
        both = y[:, 128 * r : 128 * r + 128]
        both = jnp.where(left, both[:128], both[128:])
        lines.append(both + swap(both))
    pairs = []
    for t in range(8):
        line = jnp.where(left, lines[2 * t], lines[2 * t + 1])
        yr, yi = line[:A], line[A:]
        both = [(yr * tc + yi * ts).astype(BF16), (yi * tc - yr * ts).astype(BF16)]
        pairs.append(jnp.concatenate(both, axis=1))
    spec = dot(jnp.concatenate(pairs, axis=0), second)
    for r in range(16):
        for q in range(2):
            start = A * (r >> 1) + 32 * q
            buf[pl.ds(1024 + 512 * q + r, 32, stride=16), :] = spec[
                start : start + 32, 128 * (r & 1) : 128 * (r & 1) + 128
            ]
    for q in range(2):
        for f in range(NB):
            start = 1024 + 512 * q + 16 * f
            out[q, f] = buf[start : start + 16, :].astype(BF16)


def fresnel_table(jx, band, out):
    lane = iota((KY, 128), 1)
    ky0 = A * (iota((KY, 128), 0) - LOW)
    square_x = []
    for q in range(2):
        fx = ((2 * band + q + A * ((lane & 63) + jx) + N // 2) & (N - 1)) - N // 2
        square_x.append(fx * fx)
    ec, es = math.cos(2.0 * math.pi / N), math.sin(2.0 * math.pi / N)

    def step(block, carry):
        fy = ky0 + 8 * block
        total = [square + fy * fy for square in square_x]
        factor = [sincos_int(value, 2 * N) for value in total]
        ds, dc = sincos_int(2 * fy + 1, 2 * N)
        for k in range(8):
            for q in range(2):
                hs, hc = factor[q]
                inside = total[q] <= (N // 3) ** 2
                out[q, 8 * block + k, :KY, :] = jnp.where(inside, hc, 0.0)
                out[q, 8 * block + k, KY:, :] = jnp.where(inside, hs, 0.0)
                total[q] = total[q] + 2 * fy + 1
                factor[q] = (hs * dc + hc * ds, hc * dc - hs * ds)
            ds, dc = ds * ec + dc * es, dc * ec - ds * es
            fy = fy + 1
        return carry

    lax.fori_loop(0, 8, step, 0)


def twist_table(out):
    b_row = iota((A, 128), 0)
    rs, rc = sincos_int(b_row, N)

    def step(block, carry):
        ts, tc = sincos_int(b_row * (8 * block), N)
        for k in range(8):
            out[8 * block + k, :A, :] = tc
            out[8 * block + k, A:, :] = ts
            ts, tc = ts * rc + tc * rs, tc * rc - ts * rs
        return carry

    lax.fori_loop(0, 8, step, 0)


def y_first(slab, out, buf, buf2):
    turn = sign()
    table = stacked(iota((A, A), 0) * iota((A, A), 1), 1.0 / A)
    for i in range(0, 8, 2):
        x = [buf[pl.ds(i + k, A, stride=8), :].astype(BF16) for k in range(2)]
        y = dot(table, jnp.concatenate(x, axis=1))
        for k in range(2):
            line = y[:, 128 * k : 128 * k + 128]
            line = line[:A] + swap(line[A:]) * turn
            ts, tc = sincos_int(iota((A, 128), 0) * (8 * slab + i + k), N)
            buf2[pl.ds(i + k, A, stride=8), :] = line * tc + swap(line) * (ts * turn)
    out[...] = buf2[0:512, :].astype(BF16)


def forward_table(jy):
    row = iota((KY, 128), 0)
    col = iota((KY, 128), 1)
    n2 = NS * (col >> 4) + (col & 7)
    c, s = table64(n2 * (row - LOW - jy))
    blocks = []
    for parity in range(2):
        keep = ((col >> 3) & 1) == parity
        pc = jnp.where(keep, c, 0.0)
        ps = jnp.where(keep, s, 0.0)
        blocks.append(jnp.concatenate([pc, -ps], axis=1))
        blocks.append(jnp.concatenate([ps, pc], axis=1))
    return (jnp.concatenate(blocks, axis=0) * (1.0 / A)).astype(BF16)


def y_second(q, forward, cols, fresnel, twist, buf):
    turn = sign().astype(BF16)
    c, s = table64(iota((A, KY), 0) * (iota((A, KY), 1) - LOW))
    back = jnp.concatenate(
        [jnp.concatenate([c, s], axis=1), jnp.concatenate([-s, c], axis=1)], axis=0
    ).astype(BF16)

    def step(group, carry):
        wide = []
        for m in range(8):
            at = pl.multiple_of(group * 128 + 16 * m, 16)
            x = jnp.concatenate([cols[q, p, pl.ds(at, 16), :] for p in range(NS)], axis=0)
            wide.append(jnp.concatenate([x, swap(x) * -turn], axis=0))
        wide = dot(forward, jnp.concatenate(wide, axis=1))
        v = []
        for k in range(16):
            g = wide[96 * (k % 2) : 96 * (k % 2) + 96, 128 * (k // 2) : 128 * (k // 2) + 128]
            line, turned = g[:KY], g[KY:]
            k1 = 16 * group + k
            hc, hs = fresnel[q, k1, :KY, :], fresnel[q, k1, KY:, :]
            both = [line * hc - turned * hs, turned * hc + line * hs]
            v.append(jnp.concatenate(both, axis=0).astype(BF16))
        u = dot(back, jnp.concatenate(v, axis=1))
        for k in range(16):
            line, turned = u[:A, 128 * k : 128 * k + 128], u[A:, 128 * k : 128 * k + 128]
            k1 = 16 * group + k
            tc, ts = twist[k1, :A, :], twist[k1, A:, :]
            buf[pl.ds(k1, A, stride=128), :] = line * tc + turned * ts
            buf[pl.ds(A + k1, A, stride=128), :] = turned * tc - line * ts
        return carry

    lax.fori_loop(0, 4, step, 0, unroll=4)


def spare_lanes(jx):
    return ((iota((1, 128), 1) - (22 - jx)) & 63) < SPARE


def y_third(q, half, jx, out, buf, buf2):
    row = iota((A, A), 0)
    c, s = table64((2 * (row & 31) + (row >> 5)) * iota((A, A), 1))
    table = jnp.concatenate([c, s], axis=1).astype(BF16)
    gap = spare_lanes(jx)

    z = []
    for b in range(32):
        at = (32 * half + b) * 128
        z.append(buf[at : at + 128, :].astype(BF16))
    w = dot(table, jnp.concatenate(z, axis=1))
    for g in range(8):
        lines = [w[:, 128 * (4 * g + m) : 128 * (4 * g + m) + 128] for m in range(4)]
        for m in range(3):
            line = jnp.where(gap, pltpu.roll(lines[3], 128 - SPARE * (m + 1), 1), lines[m])
            for h in range(2):
                buf2[pl.ds(16 * m + 8 * h + g, NB, stride=48), :] = line[32 * h : 32 * h + 32]

    for f in range(NB):
        out[q, half, f] = buf2[48 * f : 48 * f + 48, :].astype(BF16)


def inverse_table(jx):
    lane = iota((A, 128), 1)
    c, s = table64((iota((A, 128), 0) + jx) * (lane & 63))
    left = lane < A
    whole = jnp.concatenate([jnp.where(left, c, s), jnp.where(left, -s, c)], axis=0)
    gap = ((iota((128, 128), 0) - (22 - jx)) & 63) < SPARE
    whole = jnp.where(gap, 0.0, whole)
    zero = jnp.zeros((128, 128), F32)
    rows = []
    for m in range(3):
        fourth = jnp.where(gap, pltpu.roll(whole, 128 - SPARE * (m + 1), 0), 0.0)
        rows.append(
            jnp.concatenate([whole if k == m else zero for k in range(3)] + [fourth], axis=1)
        )
    return jnp.concatenate(rows, axis=0).astype(BF16)


def x_second(q, half, table, rows, buf):
    lane = iota((8, 128), 1)
    turn = sign()

    lhs = []
    for f in range(NB):
        block = rows[q, half, f]
        lhs.append(jnp.concatenate([block[16 * m : 16 * m + 16] for m in range(3)], axis=1))
    u = dot(jnp.concatenate(lhs, axis=0), table)
    for f in range(NB):
        k1 = 2 * f + q
        ts, tc = sincos_int(k1 * (lane & 63), N)
        ts, tc = ts[:1] * turn, tc[:1]
        for m in range(4):
            line = u[16 * f : 16 * f + 16, 128 * m : 128 * m + 128]
            line = line * tc - swap(line) * ts
            for h in range(2):
                start = (32 * half + m) * 128 + h * A + k1
                buf[pl.ds(start, 8, stride=512), :] = line[8 * h : 8 * h + 8]


def tile_table(ids):
    col = iota((NB, 128), 1)
    ids = jnp.broadcast_to(ids, (NB, 128))
    c, s = table64((col & 63) * (ids & 63))
    keep = ((ids >> 6) & 1) == (col >> 6)
    return jnp.concatenate([jnp.where(keep, c, 0.0), jnp.where(keep, s, 0.0)], axis=0).astype(BF16)


def x_third(half, table, out, buf, buf2):
    turn = sign()

    z = []
    for y in range(32):
        at = (32 * half + y) * 128
        z.append(buf[at : at + 128, :].astype(BF16))
    o = dot(table, jnp.concatenate(z, axis=1))
    for y in range(32):
        line = o[:, 128 * y : 128 * y + 128]
        buf2[pl.ds(y, NB, stride=32), :] = line[:32] - swap(line[32:]) * turn
    for p in range(NS):
        out[half, p] = buf2[128 * p : 128 * p + 128, :].astype(BF16)


def own_tiles(band, slab, tiles):
    found = jnp.sum(jnp.where((tiles >> 7) == band, tiles, 0), axis=0, keepdims=True)
    column = jnp.where((iota((NB, 256), 1) >> 3) == iota((NB, 256), 0), found, 0)
    column = jnp.sum(column, axis=1, keepdims=True)
    lane = iota((1, 256), 1)
    ids = [jnp.sum(jnp.where((lane >> 3) == 4 * slab + l, found, 0)) for l in range(4)]
    return column, ids


def probe_factors(ids, beams, shifts, out):
    row = iota((8 * 12, 128), 0)
    by = jnp.zeros_like(row)
    bx = jnp.zeros_like(row)
    ab = jnp.zeros(row.shape, F32)
    for j in range(8):
        here = (row >= 12 * j) & (row < 12 * j + 12)
        by = jnp.where(here, beams[0, j], by)
        bx = jnp.where(here, beams[1, j], bx)
        ab = jnp.where(here, shifts[j], ab)
    at = row - 12 * ((row * 43691) >> 19)
    slot = (at * 43691) >> 17
    g = at - 3 * slot
    ident = jnp.zeros_like(row)
    for l in range(4):
        ident = jnp.where(slot == l, ids[l], ident)
    ry = (ident >> 6) * A + A // 2 + g
    rx = (ident & 63) * A + A // 2 + 2 * g
    m = (F * (by * ry + bx * rx)) & (N - 1)
    s, c = sincos(ab + 2.0 * math.pi / N * m.astype(F32))
    out[0] = c
    out[1] = -s


def split_tiles(pot, out):
    for h in range(2):
        for pair in range(32):
            out[32 * h + pair] = pot[A * h : A * h + A, 128 * pair : 128 * pair + 128]


def ring_weights(out):
    ky = iota((32, 128), 0)
    kx = iota((32, 128), 1) & 63
    kx = jnp.where(kx < 32, kx, kx - A)
    radius = ky * ky + kx * kx
    counts = ring_counts()
    width = A // (2 * NDET)
    for b in range(NDET):
        member = (radius >= (width * b) ** 2) & (radius < (width * (b + 1)) ** 2)
        out[b] = jnp.where(member, A * A / (8.0 * counts[b]), 0.0)


def phases(ids, pot, out):
    left = left_half()
    for l in range(4):
        tile = pot[((ids[l] & 127) >> 1)].astype(F32)
        odd = (ids[l] & 1) == 1
        tile = jnp.where(left != odd, tile, swap(tile))
        s, c = sincos(tile)
        out[l, 0] = c
        out[l, 1] = s * sign()


def probe_rows(half, alpha, parts, phase, out):
    turn = sign()
    for l in range(4):
        sums = [jnp.zeros((32, 128), F32) for _ in range(2 * G)]
        for j in range(8):
            field = parts[half, j, 32 * l : 32 * l + 32, :].astype(F32)
            for g in range(G):
                at = 12 * j + G * l + g
                sums[g] = sums[g] + field * alpha[0, at : at + 1, :]
                sums[G + g] = sums[G + g] + field * alpha[1, at : at + 1, :]
        pc = phase[l, 0, 32 * half : 32 * half + 32, :]
        ps = phase[l, 1, 32 * half : 32 * half + 32, :]
        for g in range(G):
            probe = sums[g] - swap(sums[G + g]) * turn
            at = (G * l + g) * A + 32 * half
            out[at : at + 32, :] = (probe * pc - swap(probe) * ps).astype(BF16)


def detector_tables():
    lane = iota((A, 128), 1)
    left = lane < A
    c, s = table64(iota((A, 128), 0) * (lane & 63))
    along_x = jnp.concatenate(
        [
            jnp.concatenate([jnp.where(left, c, -s), jnp.where(left, s, c)], axis=1),
            jnp.concatenate([jnp.where(left, s, c), jnp.where(left, -c, s)], axis=1),
        ],
        axis=0,
    )
    along_x = (along_x * (1.0 / A)).astype(BF16)
    row = iota((A, A), 0)
    c, s = table64(jnp.where(row < 32, row, 32 - row) * iota((A, A), 1))
    along_y = jnp.concatenate([c, -s], axis=1) * (1.0 / A)
    along_y = jnp.where(iota((A, 128), 0) == 32, 0.0, along_y).astype(BF16)
    return along_x, along_y


def detect(along_x, along_y, probes, weights, out, buf):
    d = dot(probes[...], along_x).astype(BF16)
    images = [d[A * n : A * n + A] for n in range(4 * G)]
    images = [jnp.concatenate([image[:, :128], image[:, 128:]], axis=0) for image in images]
    value = dot(along_y, jnp.concatenate(images, axis=1))
    for n in range(4 * G):
        image = value[:, 128 * n : 128 * n + 128]
        power = image * image
        power = power[:32] + power[32:]
        first = (n // G) * A + (n % G) * NDET
        for b in range(NDET):
            buf[first + b : first + b + 1, :] = jnp.sum(power * weights[b], axis=0, keepdims=True)
    total = lax.dot_general(
        jnp.ones((8, 128), F32),
        buf[0:256, :],
        (((1,), (1,)), ((), ())),
        precision=lax.Precision.HIGHEST,
        preferred_element_type=F32,
    )
    for l in range(4):
        block = total[:, 128 * (l // 2) : 128 * (l // 2) + 128]
        out[l] = (swap(block) if l % 2 else block)[:1]


def kernel(
    beams,
    shifts,
    counts,
    tiles,
    pot1_hbm,
    pot2_hbm,
    out,
    pot1,
    pot2,
    buf,
    buf2,
    buf3,
    pairs,
    fresnel,
    twist,
    msg1,
    rows1,
    cols,
    msg2,
    rows2,
    msg3,
    parts,
    alpha,
    weights,
    phase,
    probes,
    res,
    sums,
    load,
    send1,
    recv1,
    sendg,
    recvg,
    send2,
    recv2,
    send3,
    recv3,
    send4,
    recv4,
):
    band = lax.axis_index("beam")
    slab = lax.axis_index("slab")
    jy = beams[0, slab]
    jx = beams[1, slab]
    loads = [
        pltpu.make_async_copy(
            pot1_hbm.at[pl.ds(pl.multiple_of(A * h + 16 * (slab >> 1), 16), 16), :],
            pot1.at[h],
            load.at[h],
        )
        for h in range(2)
    ]
    loads.append(pltpu.make_async_copy(pot2_hbm, pot2, load.at[2]))
    for copy in loads:
        copy.start()
    barrier = pltpu.get_barrier_semaphore()

    def greet(target):
        pl.semaphore_signal(
            barrier, inc=1, device_id=target, device_id_type=pl.DeviceIdType.MESH
        )

    def greet_beam(k, carry):
        greet({"beam": (band + k) & (NB - 1), "slab": slab})
        return carry

    lax.fori_loop(1, NB, greet_beam, 0)

    def greet_slab(k, carry):
        greet({"beam": band, "slab": (slab + k) & (NS - 1)})
        return carry

    lax.fori_loop(1, NS, greet_slab, 0)
    home = band >> 2

    def greet_home(k, carry):
        greet({"beam": (band + k) & (NB - 1), "slab": home})
        return carry

    @pl.when(home != slab)
    def _():
        lax.fori_loop(1, NB, greet_home, 0)

    x_forward(slab, loads, pot1, msg1, buf)
    extra = 4 * (NS - 1) - jnp.where(home == slab, NS - 1, 0)
    pl.semaphore_wait(barrier, NB - 1 + NS - 1 + extra)

    def exchange1(q, k):
        target = (band + k) & (NB - 1)
        return remote(
            msg1.at[q, target], rows1.at[q, band], send1.at[q], recv1.at[q],
            {"beam": target, "slab": slab},
        )

    def all_of(ref, sem):
        return pltpu.make_async_copy(ref, ref, sem)

    for q in range(2):
        lax.fori_loop(1, NB, lambda k, c: (exchange1(q, k).start(), c)[1], 0)
    for q in range(2):
        rows1[q, band] = msg1[q, band]
    fresnel_table(jx, band, fresnel)
    forward = forward_table(jy)

    right = (slab + 2) & (NS - 1)
    left = (slab + 6) & (NS - 1)
    far = (slab + 4) & (NS - 1)
    partner = slab ^ 1

    def gather(source, q, kind, target):
        view = cols.at[q, source]
        return remote(
            view, view, sendg.at[kind, q], recvg.at[source, q], {"beam": band, "slab": target}
        )

    def first(q):
        all_of(rows1.at[q, pl.ds(0, NB - 1)], recv1.at[q]).wait()
        for f in range(NB):
            buf[16 * f : 16 * f + 16, :] = rows1[q, f].astype(F32)
        y_first(slab, cols.at[q, slab], buf, buf2)

    def spread(q):
        for kind, target in enumerate((far, left, right, partner)):
            gather(slab, q, kind, target).start()

    def near(q):
        for kind, source in enumerate((left, right, far)):
            gather(source, q, 0, source).wait_recv()
            gather(source, q, 4 + kind, partner).start()

    def across(q):
        for source in (partner, left ^ 1, right ^ 1, far ^ 1):
            gather(source, q, 0, partner).wait_recv()

    def exchange2(q, half, k):
        target = (band + k) & (NB - 1)
        return remote(
            msg2.at[q, half, target], rows2.at[q, half, band],
            send2.at[2 * q + half], recv2.at[2 * q + half],
            {"beam": target, "slab": slab},
        )

    def send_rows(q, half):
        y_third(q, half, jx, msg2, buf, buf2)
        lax.fori_loop(1, NB, lambda k, z: (exchange2(q, half, k).start(), z)[1], 0)
        rows2[q, half, band] = msg2[q, half, band]

    first(0)
    spread(0)
    first(1)
    twist_table(twist)
    near(0)
    spread(1)
    across(0)
    y_second(0, forward, cols, fresnel, twist, buf)
    send_rows(0, 0)
    near(1)
    send_rows(0, 1)
    across(1)
    y_second(1, forward, cols, fresnel, twist, buf)
    send_rows(1, 0)
    send_rows(1, 1)
    loads[2].wait()
    split_tiles(pot2, pairs)
    wanted, ids = own_tiles(band, slab, tiles[...])
    tile_tab = tile_table(wanted)
    probe_factors(ids, beams, shifts, alpha)
    ring_weights(weights)
    phases(ids, pairs, phase)
    along_x, along_y = detector_tables()
    inverse = inverse_table(jx)
    block = band * NS + slab
    mine = jnp.where(iota((4, 256), 1) == block, tiles[...], 0)
    slot = iota((4, 256), 0)
    bands = [jnp.sum(jnp.where(slot == k, mine, 0)) >> 7 for k in range(4)]

    def exchange3(half, k):
        target = (slab + k) & (NS - 1)
        return remote(
            msg3.at[half, target], parts.at[half, slab],
            send3.at[half], recv3.at[half],
            {"beam": band, "slab": target},
        )

    for q in range(2):
        for half in range(2):
            all_of(rows2.at[q, half, pl.ds(0, NB - 1)], recv2.at[2 * q + half]).wait()
            x_second(q, half, inverse, rows2, buf3)
            if q == 1:
                x_third(half, tile_tab, msg3, buf3, buf2)
                for k in range(1, NS):
                    exchange3(half, k).start()
                parts[half, slab] = msg3[half, slab]
    for half in range(2):
        all_of(parts.at[half, pl.ds(0, NS - 1)], recv3.at[half]).wait()
        probe_rows(half, alpha, parts, phase, probes)
    detect(along_x, along_y, probes, weights, res, buf)

    def exchange4(l, p):
        return remote(
            res.at[l], sums.at[band], send4.at[0], recv4.at[0],
            {"beam": 4 * slab + l, "slab": p},
        )

    for l in range(4):
        for k in range(1, NS):
            exchange4(l, (slab + k) & (NS - 1)).start()

        @pl.when(4 * slab + l != band)
        def _():
            exchange4(l, slab).start()

    @pl.when(home == slab)
    def _():
        sums[band] = res[band & 3]
        all_of(sums.at[pl.ds(0, NB - 1)], recv4.at[0]).wait()

    @pl.when(home != slab)
    def _():
        all_of(sums, recv4.at[0]).wait()

    for k in range(4):
        row = sums[bands[k]]
        row = jnp.where(k < counts[block], row, 0.0)
        for g in range(G):
            out[0, g, k : k + 1, :] = row[:, NDET * g : NDET * g + NDET]

    for q in range(2):
        all_of(msg1.at[q, pl.ds(0, NB - 1)], send1.at[q]).wait()
        for kind in range(7):
            all_of(cols.at[q, 0], sendg.at[kind, q]).wait()
        for half in range(2):
            all_of(msg2.at[q, half, pl.ds(0, NB - 1)], send2.at[2 * q + half]).wait()
    for half in range(2):
        all_of(msg3.at[half, pl.ds(0, NS - 1)], send3.at[half]).wait()

    @pl.when(home == slab)
    def _():
        all_of(sums.at[pl.ds(0, NB - 1)], send4.at[0]).wait()

    @pl.when(home != slab)
    def _():
        all_of(sums, send4.at[0]).wait()


def shards(pot_first, pot_second, beam_index, aberration, tile_table, tile_count):
    args = (beam_index.T, aberration, tile_count, tile_table.T, pot_first, pot_second)
    spaces = [pltpu.SMEM] * 3 + [pltpu.VMEM] + [pltpu.HBM] * 2
    dma = pltpu.SemaphoreType.DMA
    sums = pl.pallas_call(
        kernel,
        out_shape=jax.ShapeDtypeStruct((1, G, 4, NDET), F32),
        in_specs=[pl.BlockSpec(memory_space=space) for space in spaces],
        out_specs=pl.BlockSpec(memory_space=pltpu.VMEM),
        scratch_shapes=[
            pltpu.VMEM((2, 16, N), BF16),
            pltpu.VMEM((128, N), BF16),
            pltpu.VMEM((A * 128, 128), F32),
            pltpu.VMEM((1536, 128), F32),
            pltpu.VMEM((A * 128, 128), F32),
            pltpu.VMEM((64, A, 128), BF16),
            pltpu.VMEM((2, A, 2 * KY, 128), F32),
            pltpu.VMEM((A, 128, 128), F32),
            pltpu.VMEM((2, NB, 16, 128), BF16),
            pltpu.VMEM((2, NB, 16, 128), BF16),
            pltpu.VMEM((2, NS, 512, 128), BF16),
            pltpu.VMEM((2, 2, NB, 48, 128), BF16),
            pltpu.VMEM((2, 2, NB, 48, 128), BF16),
            pltpu.VMEM((2, NS, 128, 128), BF16),
            pltpu.VMEM((2, NS, 128, 128), BF16),
            pltpu.VMEM((2, 96, 128), F32),
            pltpu.VMEM((NDET, 32, 128), F32),
            pltpu.VMEM((4, 2, A, 128), F32),
            pltpu.VMEM((4 * G * A, 128), BF16),
            pltpu.VMEM((4, 1, 128), F32),
            pltpu.VMEM((NB, 1, 128), F32),
            dma((3,)),
            dma((2,)),
            dma((2,)),
            dma((7, 2)),
            dma((NS, 2)),
            dma((4,)),
            dma((4,)),
            dma((2,)),
            dma((2,)),
            dma((1,)),
            dma((1,)),
        ],
        compiler_params=pltpu.CompilerParams(
            vmem_limit_bytes=64 * 1024 * 1024, collective_id=0, has_side_effects=True
        ),
    )(*args)
    return sums.transpose(0, 2, 1, 3)


def solution(mesh):
    return jax.shard_map(
        shards,
        mesh=mesh,
        in_specs=(P("beam", None), P("beam", None), P(), P(), P(), P()),
        out_specs=P(("beam", "slab"), None, None, None),
        check_vma=False,
    )
```

```python
import math

import jax
import jax.numpy as jnp
import numpy as np
from jax import lax
from jax.experimental import pallas as pl
from jax.experimental.pallas import tpu as pltpu
from jax.sharding import PartitionSpec as P

A = 64
N = 4096
F = 64
G = 3
NDET = 16
QMAX = 3
NB = 32
NS = 8
KY = 48
LOW = 24
SPARE = 20
F32 = jnp.float32
BF16 = jnp.bfloat16


def ring_counts():
    d = np.arange(A)
    signed = np.where(d < A // 2, d, d - A)
    radius = signed[:, None] ** 2 + signed[None, :] ** 2
    width = A // (2 * NDET)
    return [
        int(((radius >= (width * b) ** 2) & (radius < (width * (b + 1)) ** 2)).sum())
        for b in range(NDET)
    ]


def poly_sincos(r):
    t = r * r
    sine = r + r * t * (-1.6666667e-1 + t * (8.3333333e-3 + t * (-1.9841270e-4 + t * 2.7557319e-6)))
    cosine = 1.0 + t * (-0.5 + t * (4.1666667e-2 + t * (-1.3888889e-3 + t * 2.4801587e-5)))
    return sine, cosine


def place(sine, cosine, quadrant):
    swap = (quadrant & 1) == 1
    a = jnp.where(swap, cosine, sine)
    b = jnp.where(swap, sine, cosine)
    a = jnp.where((quadrant & 2) == 2, -a, a)
    b = jnp.where(((quadrant + 1) & 2) == 2, -b, b)
    return a, b


def sincos(x):
    k = jnp.floor(x * (2.0 / math.pi) + 0.5)
    r = (x - k * 1.5707963) - k * 2.6794897e-8
    sine, cosine = poly_sincos(r)
    return place(sine, cosine, k.astype(jnp.int32))


def sincos_int(m, period):
    shift = int(math.log2(period)) - 2
    quadrant = (m + (period >> 3)) >> shift
    r = (m - (quadrant << shift)).astype(F32) * (2.0 * math.pi / period)
    sine, cosine = poly_sincos(r)
    return place(sine, cosine, quadrant)


def dot(a, b):
    return jnp.dot(a, b, preferred_element_type=F32)


def iota(shape, axis):
    return lax.broadcasted_iota(jnp.int32, shape, axis)


def remote(src, dst, send, recv, target):
    return pltpu.make_async_remote_copy(
        src_ref=src,
        dst_ref=dst,
        send_sem=send,
        recv_sem=recv,
        device_id=target,
        device_id_type=pl.DeviceIdType.MESH,
    )


def swap(v):
    return pltpu.roll(v, A, 1)


def left_half():
    return iota((1, 128), 1) < A


def sign():
    return jnp.where(left_half(), 1.0, -1.0)


def table64(product):
    s, c = sincos_int(product & (A - 1), A)
    return c.astype(BF16).astype(F32), s.astype(BF16).astype(F32)


def stacked(product, scale):
    c, s = table64(product)
    return jnp.concatenate([c * scale, s * scale], axis=0).astype(BF16)


def x_tables():
    row = iota((128, 128), 0)
    col = iota((128, 128), 1)
    k1 = 2 * (row & 31) + ((row >> 5) & 1)
    blocks = []
    for rho in range(2):
        c, s = table64(k1 * (2 * (col & 31) + rho))
        same = (row >> 6) == ((col >> 5) & 1)
        blocks.append(jnp.where(same, c, jnp.where(row < A, s, -s)) * (1.0 / A))
    first = jnp.concatenate(blocks, axis=0)[:, :A].astype(BF16)
    lane = iota((A, 128), 1)
    c, s = table64(iota((A, 128), 0) * (lane & 63))
    left = lane < A
    zero = jnp.zeros((A, 128), F32)
    rows = []
    for block in (jnp.where(left, c, -s), jnp.where(left, s, c)):
        block = block * (1.0 / A)
        rows.append(jnp.concatenate([block, zero], axis=1))
        rows.append(jnp.concatenate([zero, block], axis=1))
    second = jnp.concatenate(rows, axis=0).astype(BF16)
    return first, second


def x_forward(slab, loads, potential, out, buf):
    first, second = x_tables()
    row = iota((A, 128), 0)
    k1 = 2 * (row & 31) + (row >> 5)
    ts, tc = sincos_int(k1 * (iota((A, 128), 1) & 63), N)
    left = left_half()
    odd = (slab & 1) == 1
    for h in range(2):
        loads[h].wait()
        block = potential[h].astype(F32)
        block = jnp.where(odd, block[8:], block[:8])
        sine, cosine = sincos(block)
        for part, wave in enumerate((cosine, sine)):
            for p in range(32):
                start = h * 8 * A + part * 32 + p
                buf[pl.ds(start, 8, stride=A), :] = wave[:, 128 * p : 128 * p + 128]
    waves = [buf[A * r : A * r + A, :].astype(BF16) for r in range(16)]
    y = dot(first, jnp.concatenate(waves, axis=1))
    lines = []
    for r in range(16):
        both = y[:, 128 * r : 128 * r + 128]
        both = jnp.where(left, both[:128], both[128:])
        lines.append(both + swap(both))
    pairs = []
    for t in range(8):
        line = jnp.where(left, lines[2 * t], lines[2 * t + 1])
        yr, yi = line[:A], line[A:]
        both = [(yr * tc + yi * ts).astype(BF16), (yi * tc - yr * ts).astype(BF16)]
        pairs.append(jnp.concatenate(both, axis=1))
    spec = dot(jnp.concatenate(pairs, axis=0), second)
    for r in range(16):
        for q in range(2):
            start = A * (r >> 1) + 32 * q
            buf[pl.ds(1024 + 512 * q + r, 32, stride=16), :] = spec[
                start : start + 32, 128 * (r & 1) : 128 * (r & 1) + 128
            ]
    for q in range(2):
        for f in range(NB):
            start = 1024 + 512 * q + 16 * f
            out[q, f] = buf[start : start + 16, :].astype(BF16)


def fresnel_table(jx, band, out):
    lane = iota((KY, 128), 1)
    ky0 = A * (iota((KY, 128), 0) - LOW)
    square_x = []
    for q in range(2):
        fx = ((2 * band + q + A * ((lane & 63) + jx) + N // 2) & (N - 1)) - N // 2
        square_x.append(fx * fx)
    ec, es = math.cos(2.0 * math.pi / N), math.sin(2.0 * math.pi / N)

    def step(block, carry):
        fy = ky0 + 8 * block
        total = [square + fy * fy for square in square_x]
        factor = [sincos_int(value, 2 * N) for value in total]
        ds, dc = sincos_int(2 * fy + 1, 2 * N)
        for k in range(8):
            for q in range(2):
                hs, hc = factor[q]
                inside = total[q] <= (N // 3) ** 2
                out[q, 8 * block + k, :KY, :] = jnp.where(inside, hc, 0.0)
                out[q, 8 * block + k, KY:, :] = jnp.where(inside, hs, 0.0)
                total[q] = total[q] + 2 * fy + 1
                factor[q] = (hs * dc + hc * ds, hc * dc - hs * ds)
            ds, dc = ds * ec + dc * es, dc * ec - ds * es
            fy = fy + 1
        return carry

    lax.fori_loop(0, 8, step, 0)


def twist_table(out):
    b_row = iota((A, 128), 0)
    rs, rc = sincos_int(b_row, N)

    def step(block, carry):
        ts, tc = sincos_int(b_row * (8 * block), N)
        for k in range(8):
            out[8 * block + k, :A, :] = tc
            out[8 * block + k, A:, :] = ts
            ts, tc = ts * rc + tc * rs, tc * rc - ts * rs
        return carry

    lax.fori_loop(0, 8, step, 0)


def first_twist(slab, out):
    turn = sign()
    for i in range(8):
        ts, tc = sincos_int(iota((A, 128), 0) * (8 * slab + i), N)
        out[i, :A, :] = tc
        out[i, A:, :] = ts * turn


def y_first(table, twist, out, buf, buf2):
    turn = sign()
    x = [buf[pl.ds(i, A, stride=8), :].astype(BF16) for i in range(8)]
    y = dot(table, jnp.concatenate(x, axis=1))
    for i in range(8):
        line = y[:, 128 * i : 128 * i + 128]
        line = line[:A] + swap(line[A:]) * turn
        buf2[pl.ds(i, A, stride=8), :] = line * twist[i, :A, :] + swap(line) * twist[i, A:, :]
    out[...] = buf2[0:512, :].astype(BF16)


def forward_table(jy):
    row = iota((KY, 128), 0)
    col = iota((KY, 128), 1)
    n2 = NS * (col >> 4) + (col & 7)
    c, s = table64(n2 * (row - LOW - jy))
    blocks = []
    for parity in range(2):
        keep = ((col >> 3) & 1) == parity
        pc = jnp.where(keep, c, 0.0)
        ps = jnp.where(keep, s, 0.0)
        blocks.append(jnp.concatenate([pc, -ps], axis=1))
        blocks.append(jnp.concatenate([ps, pc], axis=1))
    return (jnp.concatenate(blocks, axis=0) * (1.0 / A)).astype(BF16)


def y_second(q, forward, cols, fresnel, twist, buf):
    turn = sign().astype(BF16)
    c, s = table64(iota((A, KY), 0) * (iota((A, KY), 1) - LOW))
    back = jnp.concatenate(
        [jnp.concatenate([c, s], axis=1), jnp.concatenate([-s, c], axis=1)], axis=0
    ).astype(BF16)

    def step(group, carry):
        wide = []
        for m in range(8):
            at = pl.multiple_of(group * 128 + 16 * m, 16)
            x = jnp.concatenate([cols[q, p, pl.ds(at, 16), :] for p in range(NS)], axis=0)
            wide.append(jnp.concatenate([x, swap(x) * -turn], axis=0))
        wide = dot(forward, jnp.concatenate(wide, axis=1))
        v = []
        for k in range(16):
            g = wide[96 * (k % 2) : 96 * (k % 2) + 96, 128 * (k // 2) : 128 * (k // 2) + 128]
            line, turned = g[:KY], g[KY:]
            k1 = 16 * group + k
            hc, hs = fresnel[q, k1, :KY, :], fresnel[q, k1, KY:, :]
            both = [line * hc - turned * hs, turned * hc + line * hs]
            v.append(jnp.concatenate(both, axis=0).astype(BF16))
        u = dot(back, jnp.concatenate(v, axis=1))
        for k in range(16):
            line, turned = u[:A, 128 * k : 128 * k + 128], u[A:, 128 * k : 128 * k + 128]
            k1 = 16 * group + k
            tc, ts = twist[k1, :A, :], twist[k1, A:, :]
            buf[pl.ds(k1, A, stride=128), :] = line * tc + turned * ts
            buf[pl.ds(A + k1, A, stride=128), :] = turned * tc - line * ts
        return carry

    lax.fori_loop(0, 4, step, 0, unroll=4)


def spare_lanes(jx):
    return ((iota((1, 128), 1) - (22 - jx)) & 63) < SPARE


def y_third(q, half, jx, out, buf, buf2):
    row = iota((A, A), 0)
    c, s = table64((2 * (row & 31) + (row >> 5)) * iota((A, A), 1))
    table = jnp.concatenate([c, s], axis=1).astype(BF16)
    gap = spare_lanes(jx)

    z = []
    for b in range(32):
        at = (32 * half + b) * 128
        z.append(buf[at : at + 128, :].astype(BF16))
    w = dot(table, jnp.concatenate(z, axis=1))
    for g in range(8):
        lines = [w[:, 128 * (4 * g + m) : 128 * (4 * g + m) + 128] for m in range(4)]
        for m in range(3):
            line = jnp.where(gap, pltpu.roll(lines[3], 128 - SPARE * (m + 1), 1), lines[m])
            for h in range(2):
                buf2[pl.ds(16 * m + 8 * h + g, NB, stride=48), :] = line[32 * h : 32 * h + 32]

    for f in range(NB):
        out[q, half, f] = buf2[48 * f : 48 * f + 48, :].astype(BF16)


def inverse_table(jx):
    lane = iota((A, 128), 1)
    c, s = table64((iota((A, 128), 0) + jx) * (lane & 63))
    left = lane < A
    whole = jnp.concatenate([jnp.where(left, c, s), jnp.where(left, -s, c)], axis=0)
    gap = ((iota((128, 128), 0) - (22 - jx)) & 63) < SPARE
    whole = jnp.where(gap, 0.0, whole)
    zero = jnp.zeros((128, 128), F32)
    rows = []
    for m in range(3):
        fourth = jnp.where(gap, pltpu.roll(whole, 128 - SPARE * (m + 1), 0), 0.0)
        rows.append(
            jnp.concatenate([whole if k == m else zero for k in range(3)] + [fourth], axis=1)
        )
    return jnp.concatenate(rows, axis=0).astype(BF16)


def x_second(q, half, table, rows, buf):
    lane = iota((8, 128), 1)
    turn = sign()

    lhs = []
    for f in range(NB):
        block = rows[q, half, f]
        lhs.append(jnp.concatenate([block[16 * m : 16 * m + 16] for m in range(3)], axis=1))
    u = dot(jnp.concatenate(lhs, axis=0), table)
    for f in range(NB):
        k1 = 2 * f + q
        ts, tc = sincos_int(k1 * (lane & 63), N)
        ts, tc = ts[:1] * turn, tc[:1]
        for m in range(4):
            line = u[16 * f : 16 * f + 16, 128 * m : 128 * m + 128]
            line = line * tc - swap(line) * ts
            for h in range(2):
                start = (32 * half + m) * 128 + h * A + k1
                buf[pl.ds(start, 8, stride=512), :] = line[8 * h : 8 * h + 8]


def tile_table(ids):
    col = iota((NB, 128), 1)
    ids = jnp.broadcast_to(ids, (NB, 128))
    c, s = table64((col & 63) * (ids & 63))
    keep = ((ids >> 6) & 1) == (col >> 6)
    return jnp.concatenate([jnp.where(keep, c, 0.0), jnp.where(keep, s, 0.0)], axis=0).astype(BF16)


def x_third(half, table, out, buf, buf2):
    turn = sign()

    z = []
    for y in range(32):
        at = (32 * half + y) * 128
        z.append(buf[at : at + 128, :].astype(BF16))
    o = dot(table, jnp.concatenate(z, axis=1))
    for y in range(32):
        line = o[:, 128 * y : 128 * y + 128]
        buf2[pl.ds(y, NB, stride=32), :] = line[:32] - swap(line[32:]) * turn
    for p in range(NS):
        out[half, p] = buf2[128 * p : 128 * p + 128, :].astype(BF16)


def own_tiles(band, slab, tiles):
    found = jnp.sum(jnp.where((tiles >> 7) == band, tiles, 0), axis=0, keepdims=True)
    column = jnp.where((iota((NB, 256), 1) >> 3) == iota((NB, 256), 0), found, 0)
    column = jnp.sum(column, axis=1, keepdims=True)
    lane = iota((1, 256), 1)
    ids = [jnp.sum(jnp.where((lane >> 3) == 4 * slab + l, found, 0)) for l in range(4)]
    return column, ids


def probe_factors(ids, beams, shifts, out):
    row = iota((8 * 12, 128), 0)
    by = jnp.zeros_like(row)
    bx = jnp.zeros_like(row)
    ab = jnp.zeros(row.shape, F32)
    for j in range(8):
        here = (row >= 12 * j) & (row < 12 * j + 12)
        by = jnp.where(here, beams[0, j], by)
        bx = jnp.where(here, beams[1, j], bx)
        ab = jnp.where(here, shifts[j], ab)
    at = row - 12 * ((row * 43691) >> 19)
    slot = (at * 43691) >> 17
    g = at - 3 * slot
    ident = jnp.zeros_like(row)
    for l in range(4):
        ident = jnp.where(slot == l, ids[l], ident)
    ry = (ident >> 6) * A + A // 2 + g
    rx = (ident & 63) * A + A // 2 + 2 * g
    m = (F * (by * ry + bx * rx)) & (N - 1)
    s, c = sincos(ab + 2.0 * math.pi / N * m.astype(F32))
    out[0] = c
    out[1] = -s


def split_tiles(pot, out):
    for h in range(2):
        for pair in range(32):
            out[32 * h + pair] = pot[A * h : A * h + A, 128 * pair : 128 * pair + 128]


def ring_weights(out):
    ky = iota((32, 128), 0)
    kx = iota((32, 128), 1) & 63
    kx = jnp.where(kx < 32, kx, kx - A)
    radius = ky * ky + kx * kx
    counts = ring_counts()
    width = A // (2 * NDET)
    for b in range(NDET):
        member = (radius >= (width * b) ** 2) & (radius < (width * (b + 1)) ** 2)
        out[b] = jnp.where(member, A * A / (8.0 * counts[b]), 0.0)


def phases(ids, pot, out):
    left = left_half()
    for l in range(4):
        tile = pot[((ids[l] & 127) >> 1)].astype(F32)
        odd = (ids[l] & 1) == 1
        tile = jnp.where(left != odd, tile, swap(tile))
        s, c = sincos(tile)
        out[l, 0] = c
        out[l, 1] = s * sign()


def probe_rows(half, alpha, parts, phase, out):
    turn = sign()
    for l in range(4):
        sums = [jnp.zeros((32, 128), F32) for _ in range(2 * G)]
        for j in range(8):
            field = parts[half, j, 32 * l : 32 * l + 32, :].astype(F32)
            for g in range(G):
                at = 12 * j + G * l + g
                sums[g] = sums[g] + field * alpha[0, at : at + 1, :]
                sums[G + g] = sums[G + g] + field * alpha[1, at : at + 1, :]
        pc = phase[l, 0, 32 * half : 32 * half + 32, :]
        ps = phase[l, 1, 32 * half : 32 * half + 32, :]
        for g in range(G):
            probe = sums[g] - swap(sums[G + g]) * turn
            at = (G * l + g) * A + 32 * half
            out[at : at + 32, :] = (probe * pc - swap(probe) * ps).astype(BF16)


def detector_tables():
    lane = iota((A, 128), 1)
    left = lane < A
    c, s = table64(iota((A, 128), 0) * (lane & 63))
    along_x = jnp.concatenate(
        [
            jnp.concatenate([jnp.where(left, c, -s), jnp.where(left, s, c)], axis=1),
            jnp.concatenate([jnp.where(left, s, c), jnp.where(left, -c, s)], axis=1),
        ],
        axis=0,
    )
    along_x = (along_x * (1.0 / A)).astype(BF16)
    row = iota((A, A), 0)
    c, s = table64(jnp.where(row < 32, row, 32 - row) * iota((A, A), 1))
    along_y = jnp.concatenate([c, -s], axis=1) * (1.0 / A)
    along_y = jnp.where(iota((A, 128), 0) == 32, 0.0, along_y).astype(BF16)
    return along_x, along_y


def detect(along_x, along_y, probes, weights, out, buf):
    d = dot(probes[...], along_x).astype(BF16)
    images = [d[A * n : A * n + A] for n in range(4 * G)]
    images = [jnp.concatenate([image[:, :128], image[:, 128:]], axis=0) for image in images]
    value = dot(along_y, jnp.concatenate(images, axis=1))
    for n in range(4 * G):
        image = value[:, 128 * n : 128 * n + 128]
        power = image * image
        power = power[:32] + power[32:]
        first = (n // G) * A + (n % G) * NDET
        for b in range(NDET):
            buf[first + b : first + b + 1, :] = jnp.sum(power * weights[b], axis=0, keepdims=True)
    total = lax.dot_general(
        jnp.ones((8, 128), F32),
        buf[0:256, :],
        (((1,), (1,)), ((), ())),
        precision=lax.Precision.HIGHEST,
        preferred_element_type=F32,
    )
    for l in range(4):
        block = total[:, 128 * (l // 2) : 128 * (l // 2) + 128]
        out[l] = (swap(block) if l % 2 else block)[:1]


def kernel(
    beams,
    shifts,
    counts,
    tiles,
    pot1_hbm,
    pot2_hbm,
    out,
    pot1,
    pot2,
    buf,
    buf2,
    buf3,
    pairs,
    twist1,
    fresnel,
    twist,
    msg1,
    rows1,
    cols,
    msg2,
    rows2,
    msg3,
    parts,
    alpha,
    weights,
    phase,
    probes,
    res,
    sums,
    load,
    send1,
    recv1,
    sendg,
    recvg,
    send2,
    recv2,
    send3,
    recv3,
    send4,
    recv4,
):
    band = lax.axis_index("beam")
    slab = lax.axis_index("slab")
    jy = beams[0, slab]
    jx = beams[1, slab]
    loads = [
        pltpu.make_async_copy(
            pot1_hbm.at[pl.ds(pl.multiple_of(A * h + 16 * (slab >> 1), 16), 16), :],
            pot1.at[h],
            load.at[h],
        )
        for h in range(2)
    ]
    loads.append(pltpu.make_async_copy(pot2_hbm, pot2, load.at[2]))
    for copy in loads:
        copy.start()
    barrier = pltpu.get_barrier_semaphore()

    def greet(target):
        pl.semaphore_signal(
            barrier, inc=1, device_id=target, device_id_type=pl.DeviceIdType.MESH
        )

    def greet_beam(k, carry):
        greet({"beam": (band + k) & (NB - 1), "slab": slab})
        return carry

    lax.fori_loop(1, NB, greet_beam, 0)

    def greet_slab(k, carry):
        greet({"beam": band, "slab": (slab + k) & (NS - 1)})
        return carry

    lax.fori_loop(1, NS, greet_slab, 0)
    home = band >> 2

    def greet_home(k, carry):
        greet({"beam": (band + k) & (NB - 1), "slab": home})
        return carry

    @pl.when(home != slab)
    def _():
        lax.fori_loop(1, NB, greet_home, 0)

    x_forward(slab, loads, pot1, msg1, buf)
    extra = 4 * (NS - 1) - jnp.where(home == slab, NS - 1, 0)
    pl.semaphore_wait(barrier, NB - 1 + NS - 1 + extra)

    def exchange1(q, k):
        target = (band + k) & (NB - 1)
        return remote(
            msg1.at[q, target], rows1.at[q, band], send1.at[q], recv1.at[q],
            {"beam": target, "slab": slab},
        )

    def all_of(ref, sem):
        return pltpu.make_async_copy(ref, ref, sem)

    for q in range(2):
        lax.fori_loop(1, NB, lambda k, c: (exchange1(q, k).start(), c)[1], 0)
    for q in range(2):
        rows1[q, band] = msg1[q, band]
    first_table = stacked(iota((A, A), 0) * iota((A, A), 1), 1.0 / A)
    first_twist(slab, twist1)
    fresnel_table(jx, band, fresnel)
    forward = forward_table(jy)

    right = (slab + 2) & (NS - 1)
    left = (slab + 6) & (NS - 1)
    far = (slab + 4) & (NS - 1)
    partner = slab ^ 1

    def gather(source, q, kind, target):
        view = cols.at[q, source]
        return remote(
            view, view, sendg.at[kind, q], recvg.at[source, q], {"beam": band, "slab": target}
        )

    def first(q):
        all_of(rows1.at[q, pl.ds(0, NB - 1)], recv1.at[q]).wait()
        for f in range(NB):
            buf[16 * f : 16 * f + 16, :] = rows1[q, f].astype(F32)
        y_first(first_table, twist1, cols.at[q, slab], buf, buf2)

    def spread(q):
        for kind, target in enumerate((far, left, right, partner)):
            gather(slab, q, kind, target).start()

    def near(q):
        for kind, source in enumerate((left, right, far)):
            gather(source, q, 0, source).wait_recv()
            gather(source, q, 4 + kind, partner).start()

    def across(q):
        for source in (partner, left ^ 1, right ^ 1, far ^ 1):
            gather(source, q, 0, partner).wait_recv()

    def exchange2(q, half, k):
        target = (band + k) & (NB - 1)
        return remote(
            msg2.at[q, half, target], rows2.at[q, half, band],
            send2.at[2 * q + half], recv2.at[2 * q + half],
            {"beam": target, "slab": slab},
        )

    def send_rows(q, half):
        y_third(q, half, jx, msg2, buf, buf2)
        lax.fori_loop(1, NB, lambda k, z: (exchange2(q, half, k).start(), z)[1], 0)
        rows2[q, half, band] = msg2[q, half, band]

    first(0)
    spread(0)
    first(1)
    twist_table(twist)
    near(0)
    spread(1)
    across(0)
    y_second(0, forward, cols, fresnel, twist, buf)
    send_rows(0, 0)
    near(1)
    send_rows(0, 1)
    across(1)
    y_second(1, forward, cols, fresnel, twist, buf)
    send_rows(1, 0)
    send_rows(1, 1)
    loads[2].wait()
    split_tiles(pot2, pairs)
    wanted, ids = own_tiles(band, slab, tiles[...])
    tile_tab = tile_table(wanted)
    probe_factors(ids, beams, shifts, alpha)
    ring_weights(weights)
    phases(ids, pairs, phase)
    along_x, along_y = detector_tables()
    inverse = inverse_table(jx)
    block = band * NS + slab
    mine = jnp.where(iota((4, 256), 1) == block, tiles[...], 0)
    slot = iota((4, 256), 0)
    bands = [jnp.sum(jnp.where(slot == k, mine, 0)) >> 7 for k in range(4)]

    def exchange3(half, k):
        target = (slab + k) & (NS - 1)
        return remote(
            msg3.at[half, target], parts.at[half, slab],
            send3.at[half], recv3.at[half],
            {"beam": band, "slab": target},
        )

    for q in range(2):
        for half in range(2):
            all_of(rows2.at[q, half, pl.ds(0, NB - 1)], recv2.at[2 * q + half]).wait()
            x_second(q, half, inverse, rows2, buf3)
            if q == 1:
                x_third(half, tile_tab, msg3, buf3, buf2)
                for k in range(1, NS):
                    exchange3(half, k).start()
                parts[half, slab] = msg3[half, slab]
    for half in range(2):
        all_of(parts.at[half, pl.ds(0, NS - 1)], recv3.at[half]).wait()
        probe_rows(half, alpha, parts, phase, probes)
    detect(along_x, along_y, probes, weights, res, buf)

    def exchange4(l, p):
        return remote(
            res.at[l], sums.at[band], send4.at[0], recv4.at[0],
            {"beam": 4 * slab + l, "slab": p},
        )

    for l in range(4):
        for k in range(1, NS):
            exchange4(l, (slab + k) & (NS - 1)).start()

        @pl.when(4 * slab + l != band)
        def _():
            exchange4(l, slab).start()

    for q in range(2):
        all_of(msg1.at[q, pl.ds(0, NB - 1)], send1.at[q]).wait()
        for kind in range(7):
            all_of(cols.at[q, 0], sendg.at[kind, q]).wait()
        for half in range(2):
            all_of(msg2.at[q, half, pl.ds(0, NB - 1)], send2.at[2 * q + half]).wait()
    for half in range(2):
        all_of(msg3.at[half, pl.ds(0, NS - 1)], send3.at[half]).wait()

    @pl.when(home == slab)
    def _():
        sums[band] = res[band & 3]
        all_of(sums.at[pl.ds(0, NB - 1)], recv4.at[0]).wait()

    @pl.when(home != slab)
    def _():
        all_of(sums, recv4.at[0]).wait()

    for k in range(4):
        row = sums[bands[k]]
        row = jnp.where(k < counts[block], row, 0.0)
        for g in range(G):
            out[0, g, k : k + 1, :] = row[:, NDET * g : NDET * g + NDET]

    @pl.when(home == slab)
    def _():
        all_of(sums.at[pl.ds(0, NB - 1)], send4.at[0]).wait()

    @pl.when(home != slab)
    def _():
        all_of(sums, send4.at[0]).wait()


def shards(pot_first, pot_second, beam_index, aberration, tile_table, tile_count):
    args = (beam_index.T, aberration, tile_count, tile_table.T, pot_first, pot_second)
    spaces = [pltpu.SMEM] * 3 + [pltpu.VMEM] + [pltpu.HBM] * 2
    dma = pltpu.SemaphoreType.DMA
    sums = pl.pallas_call(
        kernel,
        out_shape=jax.ShapeDtypeStruct((1, G, 4, NDET), F32),
        in_specs=[pl.BlockSpec(memory_space=space) for space in spaces],
        out_specs=pl.BlockSpec(memory_space=pltpu.VMEM),
        scratch_shapes=[
            pltpu.VMEM((2, 16, N), BF16),
            pltpu.VMEM((128, N), BF16),
            pltpu.VMEM((A * 128, 128), F32),
            pltpu.VMEM((1536, 128), F32),
            pltpu.VMEM((A * 128, 128), F32),
            pltpu.VMEM((64, A, 128), BF16),
            pltpu.VMEM((8, 128, 128), F32),
            pltpu.VMEM((2, A, 2 * KY, 128), F32),
            pltpu.VMEM((A, 128, 128), F32),
            pltpu.VMEM((2, NB, 16, 128), BF16),
            pltpu.VMEM((2, NB, 16, 128), BF16),
            pltpu.VMEM((2, NS, 512, 128), BF16),
            pltpu.VMEM((2, 2, NB, 48, 128), BF16),
            pltpu.VMEM((2, 2, NB, 48, 128), BF16),
            pltpu.VMEM((2, NS, 128, 128), BF16),
            pltpu.VMEM((2, NS, 128, 128), BF16),
            pltpu.VMEM((2, 96, 128), F32),
            pltpu.VMEM((NDET, 32, 128), F32),
            pltpu.VMEM((4, 2, A, 128), F32),
            pltpu.VMEM((4 * G * A, 128), BF16),
            pltpu.VMEM((4, 1, 128), F32),
            pltpu.VMEM((NB, 1, 128), F32),
            dma((3,)),
            dma((2,)),
            dma((2,)),
            dma((7, 2)),
            dma((NS, 2)),
            dma((4,)),
            dma((4,)),
            dma((2,)),
            dma((2,)),
            dma((1,)),
            dma((1,)),
        ],
        compiler_params=pltpu.CompilerParams(
            vmem_limit_bytes=64 * 1024 * 1024, collective_id=0, has_side_effects=True
        ),
    )(*args)
    return sums.transpose(0, 2, 1, 3)


def solution(mesh):
    return jax.shard_map(
        shards,
        mesh=mesh,
        in_specs=(P("beam", None), P("beam", None), P(), P(), P(), P()),
        out_specs=P(("beam", "slab"), None, None, None),
        check_vma=False,
    )
```
